512 devices in a mesh: sx: 64 (over z, y), sy: 8 (over x, core).
Axes of the slice: x: 4, y: 4, z: 16, core: 2. Of those that a mesh axis runs over, the one named last changes fastest.
Arguments:
- frames: bfloat16 [2, 128, 2048, 8], P(None, 'sy', 'sx'), may hold values from -6 to 6
- hidden_init: bfloat16 [128, 2048, 256], P('sy', 'sx'), may hold values from -1 to 1
- cell_init: float32 [128, 2048, 256], P('sy', 'sx'), may hold values from -6 to 6
- conv_weight: bfloat16 [9, 264, 1024], P(None, None, 'sx'), may hold values from -0.125 to 0.125
- gate_offsets_bias: float32 [1024], replicated, may hold values from -3 to 3
- land_mask: int32 [128, 2048], P('sy', 'sx'), may hold values 0 or 1
- projection_coefficients: bfloat16 [256], replicated, may hold values from -0.375 to 0.375
Outputs:
- hidden_out: bfloat16 [128, 2048, 256], P('sy', 'sx')
- cell_out: float32 [128, 2048, 256], P('sy', 'sx')
- predicted_flux: float32 [128, 2048], P('sy', 'sx')
The draws below stay inside these ranges and needn't reach their ends.
All inputs are finite; a program needn't handle non-finite values. No bound on the sum of `land_mask` on one device may be relied on, other than what follows from the above.
Results may differ from the reference program's by a relative error of at most 0.0046.
Values may be sent and summed in bfloat16 or wider, within the bound.
No kernel may reach another device: no remote copies, remote signals or barrier semaphores. Data moves between devices by JAX's collectives and lax.ppermute only.
A program may use at most 64 MiB of HBM per device.

```python
import math
import jax
import jax.numpy as jnp
from jax import lax

HID = 256
CX = 8
STEPS = 2
CIN = 264
NLAT = 128
NLON = 2048


def with_ends(values, stream_key, smallest, high):
    longest = values.shape.index(max(values.shape))
    spots = []
    for shift in (0, 1):
        where = [jax.random.randint(jax.random.fold_in(stream_key, axis), (), 0, length) for axis, length in enumerate(values.shape)]
        where[longest] = (where[longest] + shift) % values.shape[longest]
        spots.append(tuple(where))
    return values.at[spots[0]].set(smallest).at[spots[1]].set(high)


def levels(rng, extent, shards, least, high):
    gain = 1.0
    for position, parts in shards:
        steps = jax.random.uniform(jax.random.fold_in(jax.random.fold_in(rng, 6), position), (parts,), jnp.float32, least / len(shards), high / len(shards))
        gain = gain * jnp.repeat(jnp.exp(steps), extent[position] // parts).reshape((-1,) + (1,) * (len(extent) - 1 - position))
    return gain


def scatter_about(key, extent, deviation, bound, split=(), kind=jnp.bfloat16):
    array = jax.random.normal(key, extent, jnp.float32) * deviation
    if len(split) > 0:
        array = levels(key, extent, split, -0.22, 0.18) * array
    return jnp.clip(array, min=-bound, max=bound).astype(kind)


def setup_inputs(seed: int = 0) -> dict:
    key_list = jax.random.split(jax.random.key(seed), 8)
    return {
        "frames": scatter_about(key_list[0], (STEPS, NLAT, NLON, CX), 1.0, 6.0, ((1, 8), (2, 64))),
        "hidden_init": jnp.clip(jax.random.uniform(key_list[1], (NLAT, NLON, HID), jnp.float32, -1.0, 1.0) * levels(key_list[1], (NLAT, NLON, HID), ((0, 8), (1, 64)), -0.4, 0.0), -1.0, 1.0).astype(jnp.bfloat16),
        "cell_init": scatter_about(key_list[2], (NLAT, NLON, HID), 1.0, 6.0, ((0, 8), (1, 64)), jnp.float32),
        "conv_weight": scatter_about(key_list[3], (9, CIN, 4 * HID), (9 * CIN) ** -0.5, 0.125, ((2, 64),)),
        "gate_offsets_bias": scatter_about(key_list[4], (4 * HID,), 0.5, 3.0, (), jnp.float32),
        "land_mask": with_ends((jax.random.randint(key_list[5], (NLAT, NLON), 0, 5) < 4).astype(jnp.int32), jax.random.fold_in(key_list[5], 1), 0, 1),
        "projection_coefficients": scatter_about(key_list[6], (HID,), HID ** -0.5, 0.375),
    }


def gate_matrix_block(padded, weight_flat, bias, start, block, ncol):
    neighbourhood_window = lax.dynamic_slice_in_dim(padded, start, block + 2, 0)
    pieces = [neighbourhood_window[a:a + block, b:b + ncol, :] for a in range(3) for b in range(3)]
    patches = jnp.concatenate(pieces, -1).reshape(block * ncol, -1)
    gates = jnp.dot(patches, weight_flat, preferred_element_type=jnp.float32)
    return gates.reshape(block, ncol, -1) + bias


def reference(frames, hidden_init, cell_init, conv_weight, gate_offsets_bias, land_mask, projection_coefficients):
    kept_locations = land_mask.astype(jnp.float32)[:, :, None]
    weight_flat = conv_weight.reshape(9 * CIN, 4 * HID)
    block = math.gcd(NLAT, 8)
    latent_carry, memory_carry = hidden_init, cell_init
    for step in range(STEPS):
        inputs = jnp.concatenate([frames[step], latent_carry], -1)
        padded = jnp.pad(inputs, ((1, 1), (1, 1), (0, 0)))

        def one(index, padded=padded, memory_carry=memory_carry):
            start = (index * block).astype(jnp.int32)
            gates = gate_matrix_block(padded, weight_flat, gate_offsets_bias, start, block, NLON)
            cell_part = lax.dynamic_slice_in_dim(memory_carry, start, block, 0)
            keep_part = lax.dynamic_slice_in_dim(kept_locations, start, block, 0)
            in_gate = jax.nn.sigmoid(gates[..., :HID])
            decay_factor = jax.nn.sigmoid(gates[..., HID:2 * HID])
            candidate = jnp.tanh(gates[..., 2 * HID:3 * HID])
            out_gate = jax.nn.sigmoid(gates[..., 3 * HID:])
            new_cell = decay_factor * cell_part + in_gate * candidate
            new_hidden = (keep_part * out_gate * jnp.tanh(new_cell)).astype(jnp.bfloat16)
            return new_cell, new_hidden

        cells, hiddens = lax.map(one, jnp.arange(NLAT // block, dtype=jnp.int32))
        memory_carry = cells.reshape(NLAT, NLON, HID)
        latent_carry = hiddens.reshape(NLAT, NLON, HID)
    predicted_flux = jnp.dot(latent_carry, projection_coefficients, preferred_element_type=jnp.float32) * kept_locations[:, :, 0]
    return latent_carry, memory_carry, predicted_flux
```

```python
import jax
import jax.numpy as jnp
from jax import lax
from jax.sharding import Mesh, PartitionSpec as P

KPAD = 2560
HID = 256


def pack_weights(conv_weight):
    taps, cin, cols = conv_weight.shape
    cx = cin - HID
    flipped = jnp.transpose(conv_weight, (2, 0, 1))
    hidden = flipped[:, :, cx:].reshape(cols, taps * HID)
    frame = flipped[:, :, :cx].reshape(cols, taps * cx)
    packed = jnp.concatenate([hidden, frame], axis=1)
    return jnp.pad(packed, ((0, 0), (0, KPAD - packed.shape[1])))


def spread(block, axes):
    count = lax.axis_size(axes)
    copies = jnp.broadcast_to(block[None], (count,) + block.shape)
    return lax.all_to_all(copies, axes, 0, 0)


def shifted(block, axes, step):
    count = lax.axis_size(axes)
    pairs = [(i, i + step) for i in range(count) if 0 <= i + step < count]
    return lax.ppermute(block, axes, pairs)


def widened(block, width):
    for axes, dim in ((("x", "c"), 0), (("z", "y"), 1)):
        size = block.shape[dim]
        low = shifted(lax.slice_in_dim(block, size - width, size, axis=dim), axes, 1)
        high = shifted(lax.slice_in_dim(block, 0, width, axis=dim), axes, -1)
        block = jnp.concatenate([low, block, high], axis=dim)
    return block


def patches_of(hidden, frame):
    rows, cols = hidden.shape[0] - 2, hidden.shape[1] - 2
    pieces = [hidden[a : a + rows, b : b + cols] for a in range(3) for b in range(3)]
    pieces += [frame[a : a + rows, b : b + cols] for a in range(3) for b in range(3)]
    out = jnp.concatenate(pieces, -1)
    out = jnp.pad(out, ((0, 0), (0, 0), (0, KPAD - out.shape[2])))
    return out.reshape(rows * cols, KPAD)


def cell_update(patches, weight, bias, cell, keep):
    rows, cols, width = cell.shape
    gates = lax.dot_general(
        patches, weight, (((1,), (1,)), ((), ())), preferred_element_type=jnp.float32
    )
    gates = gates.reshape(rows, cols, -1) + bias
    in_gate = jax.nn.sigmoid(gates[..., :width])
    decay_factor = jax.nn.sigmoid(gates[..., width : 2 * width])
    candidate = jnp.tanh(gates[..., 2 * width : 3 * width])
    out_gate = jax.nn.sigmoid(gates[..., 3 * width :])
    cell = decay_factor * cell + in_gate * candidate
    return (keep[..., None] * out_gate * jnp.tanh(cell)).astype(jnp.bfloat16), cell


def body(frames, hidden_init, cell_init, conv_weight, bias, land_mask, projection):
    rows, cols, width = hidden_init.shape
    cx = frames.shape[3]
    x, c = lax.axis_index("x"), lax.axis_index("c")
    packed = pack_weights(conv_weight)
    unit = lax.dynamic_slice(packed, (c * 8, x * (KPAD // 4)), (8, KPAD // 4))
    by_z = spread(unit, "z")
    by_z, frames, hidden_init, cell_init, land_mask = lax.optimization_barrier(
        (by_z, frames, hidden_init, cell_init, land_mask)
    )
    by_yx = spread(by_z, ("y", "x"))
    half = by_yx.reshape(4, 4, 16, 8, KPAD // 4)
    other = lax.ppermute(half, "c", [(0, 1), (1, 0)])
    first = jnp.where(c == 0, half, other)
    second = jnp.where(c == 0, other, half)
    weight = jnp.transpose(jnp.stack([first, second]), (3, 1, 0, 4, 2, 5)).reshape(1024, KPAD)

    keep = land_mask.astype(jnp.float32)
    packed_state = jnp.concatenate(
        [
            hidden_init,
            cell_init.astype(jnp.bfloat16),
            frames[0],
            frames[1],
            land_mask.astype(jnp.bfloat16)[..., None],
        ],
        axis=-1,
    )
    wide = widened(packed_state, 2)
    hidden = wide[..., :width]
    frame0 = wide[..., 2 * width : 2 * width + cx]
    frame1 = wide[..., 2 * width + cx : 2 * width + 2 * cx]
    keep_wide = wide[1:-1, 1:-1, 2 * width + 2 * cx].astype(jnp.float32)
    cell_wide = wide[1:-1, 1:-1, width : 2 * width].astype(jnp.float32)
    cell_wide = lax.dynamic_update_slice(cell_wide, cell_init, (1, 1, 0))

    hidden, cell = cell_update(patches_of(hidden, frame0), weight, bias, cell_wide, keep_wide)
    hidden, cell = cell_update(
        patches_of(hidden, frame1[1:-1, 1:-1]), weight, bias, cell[1:-1, 1:-1], keep
    )
    flux = jnp.dot(hidden, projection, preferred_element_type=jnp.float32) * keep
    return hidden, cell, flux


def solution(mesh):
    split = Mesh(mesh.devices.reshape(16, 4, 4, 2), ("z", "y", "x", "c"))
    sx, sy = ("z", "y"), ("x", "c")
    in_specs = (
        P(None, sy, sx, None),
        P(sy, sx, None),
        P(sy, sx, None),
        P(None, None, sx),
        P(),
        P(sy, sx),
        P(),
    )
    out_specs = (P(sy, sx, None), P(sy, sx, None), P(sy, sx))
    return jax.shard_map(body, mesh=split, in_specs=in_specs, out_specs=out_specs, check_vma=False)
```

```python
import jax
import jax.numpy as jnp
from jax import lax
from jax.experimental import pallas as pl
from jax.experimental.pallas import tpu as pltpu
from jax.sharding import Mesh, PartitionSpec as P

KPAD = 2560
HID = 256
F32 = jnp.float32
BF16 = jnp.bfloat16
NT = (((1,), (1,)), ((), ()))
NN = (((1,), (0,)), ((), ()))
VMEM = pl.BlockSpec(memory_space=pltpu.VMEM)
SMEM = pl.BlockSpec(memory_space=pltpu.SMEM)
PARAMS = pltpu.CompilerParams(vmem_limit_bytes=48 * 1024 * 1024)


def pack_weights(conv_weight):
    taps, cin, cols = conv_weight.shape
    cx = cin - HID
    flipped = jnp.transpose(conv_weight, (2, 0, 1))
    hidden = flipped[:, :, cx:].reshape(cols, taps * HID)
    frame = flipped[:, :, :cx].reshape(cols, taps * cx)
    packed = jnp.concatenate([hidden, frame], axis=1)
    return jnp.pad(packed, ((0, 0), (0, KPAD - packed.shape[1])))


def spread(block, axes):
    count = lax.axis_size(axes)
    copies = jnp.broadcast_to(block[None], (count,) + block.shape)
    return lax.all_to_all(copies, axes, 0, 0)


def shifted(block, axes, step):
    count = lax.axis_size(axes)
    pairs = [(i, i + step) for i in range(count) if 0 <= i + step < count]
    return lax.ppermute(block, axes, pairs)


def widened(block, width):
    for axes, dim in ((("x", "c"), 0), (("z", "y"), 1)):
        size = block.shape[dim]
        low = shifted(lax.slice_in_dim(block, size - width, size, axis=dim), axes, 1)
        high = shifted(lax.slice_in_dim(block, 0, width, axis=dim), axes, -1)
        block = jnp.concatenate([low, block, high], axis=dim)
    return block


def taps_of(source, rows, cols):
    return [source[a : a + rows, b : b + cols] for a in range(3) for b in range(3)]


def patches_of(hidden, frame):
    rows, cols = frame.shape[0] - 2, frame.shape[1] - 2
    pieces = [] if hidden is None else taps_of(hidden, rows, cols)
    pieces += taps_of(frame, rows, cols)
    out = jnp.concatenate(pieces, -1)
    width = -(-out.shape[2] // 256) * 256
    out = jnp.pad(out, ((0, 0), (0, 0), (0, width - out.shape[2])))
    return out.reshape(rows * cols, width)


def ringed(core, left, right):
    pad = ((0, 6), (0, 0))
    return jnp.concatenate([core, jnp.pad(left, pad), jnp.pad(right, pad)], axis=0)


def chooser(half, shape, channel_axis):
    place = lax.broadcasted_iota(jnp.int32, shape, 1 - channel_axis)
    natural = lax.broadcasted_iota(jnp.int32, shape, channel_axis)
    y = lax.shift_right_logical(place, 5)
    zz = lax.shift_right_logical(place, 3) & 3
    wanted = zz * 64 + y * 16 + half * 8 + (place & 7)
    return jnp.where(natural == wanted, 1.0, 0.0).astype(BF16)


def parts_of(value):
    high = value.astype(BF16)
    rest = value - high.astype(F32)
    middle = rest.astype(BF16)
    return high, middle, (rest - middle.astype(F32)).astype(BF16)


def moved(value, choice):
    dots = [lax.dot_general(p, choice, NN, preferred_element_type=F32) for p in parts_of(value)]
    return dots[0] + (dots[1] + dots[2])


def half_step(patches, weight_ref, bias, cell, keep):
    gates = []
    for pair in range(2):
        rhs = jnp.concatenate(
            [
                jnp.concatenate(
                    [
                        weight_ref[y * 4 + x, q * 32 : (q + 1) * 32, :]
                        for q in (2 * pair, 2 * pair + 1)
                        for y in range(4)
                    ],
                    axis=0,
                )
                for x in range(4)
            ],
            axis=1,
        )
        both = lax.dot_general(patches, rhs, NT, preferred_element_type=F32)
        gates.append(both[:, :128] + bias[2 * pair][None])
        gates.append(both[:, 128:] + bias[2 * pair + 1][None])
    sig = lambda v: 0.5 * jnp.tanh(0.5 * v) + 0.5
    cell = sig(gates[1]) * cell + sig(gates[0]) * jnp.tanh(gates[2])
    hidden = (keep * sig(gates[3]) * jnp.tanh(cell)).astype(BF16)
    return hidden, cell


def first_kernel(half_ref, patches_ref, weight_ref, bias_ref, cell_ref, keep_ref, hid_out, cell_out):
    choice = chooser(half_ref[0], (HID, 128), 0)
    cell = moved(cell_ref[...], choice)
    hidden, cell = half_step(patches_ref[...], weight_ref, bias_ref[...], cell, keep_ref[...])
    hid_out[...] = hidden
    cell_out[...] = cell


def first_step(half, patches, weight, bias, cell, keep):
    count = patches.shape[0]
    return pl.pallas_call(
        first_kernel,
        out_shape=(
            jax.ShapeDtypeStruct((count, 128), BF16),
            jax.ShapeDtypeStruct((count, 128), F32),
        ),
        in_specs=[SMEM] + [VMEM] * 5,
        out_specs=(VMEM, VMEM),
        compiler_params=PARAMS,
        cost_estimate=pl.CostEstimate(
            flops=2 * count * KPAD * 512, bytes_accessed=6_000_000, transcendentals=count * 640
        ),
    )(half, patches, weight, bias, cell, keep)


def second_kernel(
    half_ref,
    hid0_ref,
    hid1_ref,
    cell0_ref,
    cell1_ref,
    frame_ref,
    weight0_ref,
    weight1_ref,
    bias_ref,
    keep_ref,
    keep2_ref,
    proj_ref,
    hid_out,
    cell_out,
    flux_out,
    wide,
    patches,
):
    choices = [chooser(half_ref[i], (128, HID), 1) for i in range(2)]
    natural = lax.dot_general(
        hid0_ref[...], choices[0], NN, preferred_element_type=F32
    ) + lax.dot_general(hid1_ref[...], choices[1], NN, preferred_element_type=F32)
    wide[:, 8:40, :] = natural[:576].reshape(18, 32, HID)
    for row in range(18):
        wide[row, 7:8, :] = natural[576 + row : 577 + row]
        wide[row, 40:41, :] = natural[600 + row : 601 + row]
    for b in range(3):
        moved_rows = wide[:, 7 + b : 39 + b, :].astype(BF16)
        for a in range(3):
            t = 3 * a + b
            patches[:, t * HID : (t + 1) * HID] = moved_rows[a : a + 16].reshape(512, HID)
    patches[:, 9 * HID :] = frame_ref[...]
    hid, cell = None, None
    for i, (weight_ref, cell_ref) in enumerate(((weight0_ref, cell0_ref), (weight1_ref, cell1_ref))):
        new_hid, new_cell = half_step(
            patches[...], weight_ref, bias_ref[i], cell_ref[32:544, :], keep_ref[...]
        )
        one = lax.dot_general(new_hid, choices[i], NN, preferred_element_type=F32)
        two = moved(new_cell, choices[i])
        hid = one if hid is None else hid + one
        cell = two if cell is None else cell + two
    hid = hid.astype(BF16)
    hid_out[...] = hid
    cell_out[...] = cell
    flux = lax.dot_general(proj_ref[...], hid, NT, preferred_element_type=F32)
    for row in range(16):
        flux_out[row : row + 1, :] = flux[0:1, row * 32 : (row + 1) * 32] * keep2_ref[row : row + 1, :]


def second_step(halves, hids, cells, frame, weights, bias, keep, keep2, proj):
    return pl.pallas_call(
        second_kernel,
        out_shape=(
            jax.ShapeDtypeStruct((512, HID), BF16),
            jax.ShapeDtypeStruct((512, HID), F32),
            jax.ShapeDtypeStruct((16, 32), F32),
        ),
        in_specs=[SMEM] + [VMEM] * 11,
        out_specs=(VMEM, VMEM, VMEM),
        scratch_shapes=[pltpu.VMEM((18, 48, HID), F32), pltpu.VMEM((512, KPAD), BF16)],
        compiler_params=PARAMS,
        cost_estimate=pl.CostEstimate(
            flops=2 * 512 * KPAD * 1024, bytes_accessed=8_000_000, transcendentals=512 * 1280
        ),
    )(halves, *hids, *cells, frame, *weights, bias, keep, keep2, proj)


def compute(halves, own, other, wide, cell_init, land_mask, bias, projection, cx):
    rows, cols = land_mask.shape
    width = HID
    keep = land_mask.astype(F32)
    hidden = wide[..., :width]
    frame0 = wide[..., 2 * width : 2 * width + cx]
    frame1 = wide[..., 2 * width + cx : 2 * width + 2 * cx]
    keep_wide = wide[1:-1, 1:-1, 2 * width + 2 * cx :].astype(F32)
    cell_wide = wide[1:-1, 1:-1, width : 2 * width].astype(F32)
    middle = jnp.concatenate([cell_wide[:1, 1:-1], cell_init, cell_wide[-1:, 1:-1]], axis=0)
    cell1 = ringed(middle.reshape(-1, width), cell_wide[:, 0], cell_wide[:, -1])
    keep1 = ringed(keep_wide[:, 1:-1].reshape(-1, 1), keep_wide[:, 0], keep_wide[:, -1])
    patches1 = ringed(
        patches_of(hidden[:, 1:-1], frame0[:, 1:-1]),
        patches_of(hidden[:, :3], frame0[:, :3]),
        patches_of(hidden[:, -3:], frame0[:, -3:]),
    )
    frame2 = patches_of(None, frame1[1:-1, 1:-1])

    by_half = jnp.transpose(bias.reshape(4, 4, 4, 2, 8), (3, 0, 2, 1, 4)).reshape(2, 4, 128)
    bias2 = jnp.stack([by_half[halves[0]], by_half[halves[1]]])
    hid0, cell0 = first_step(halves[:1], patches1, own, bias2[0], cell1, keep1)
    hid1, cell1 = first_step(halves[1:], patches1, other, bias2[1], cell1, keep1)
    proj = jnp.broadcast_to(projection[None], (16, width))
    hidden, cell, flux = second_step(
        halves, (hid0, hid1), (cell0, cell1), frame2, (own, other), bias2,
        keep.reshape(-1, 1), keep, proj,
    )
    return hidden.reshape(rows, cols, width), cell.reshape(rows, cols, width), flux


def body(frames, hidden_init, cell_init, conv_weight, bias, land_mask, projection):
    cx = frames.shape[3]
    x, c = lax.axis_index("x"), lax.axis_index("c")
    packed = pack_weights(conv_weight)
    unit = lax.dynamic_slice(packed, (c * 8, x * (KPAD // 4)), (8, KPAD // 4))
    by_z = spread(unit, "z").reshape(128, KPAD // 4)
    own = spread(by_z, ("y", "x"))
    other = lax.ppermute(own, "c", [(0, 1), (1, 0)])
    packed_state = jnp.concatenate(
        [
            hidden_init,
            cell_init.astype(BF16),
            frames[0],
            frames[1],
            land_mask.astype(BF16)[..., None],
        ],
        axis=-1,
    )
    wide = widened(packed_state, 2)
    halves = jnp.stack([c, 1 - c]).astype(jnp.int32)
    return compute(halves, own, other, wide, cell_init, land_mask, bias, projection, cx)


def solution(mesh):
    split = Mesh(mesh.devices.reshape(16, 4, 4, 2), ("z", "y", "x", "c"))
    sx, sy = ("z", "y"), ("x", "c")
    in_specs = (
        P(None, sy, sx, None),
        P(sy, sx, None),
        P(sy, sx, None),
        P(None, None, sx),
        P(),
        P(sy, sx),
        P(),
    )
    out_specs = (P(sy, sx, None), P(sy, sx, None), P(sy, sx))
    return jax.shard_map(body, mesh=split, in_specs=in_specs, out_specs=out_specs, check_vma=False)
```

```python
import functools

import jax
import jax.numpy as jnp
from jax import lax
from jax.experimental import pallas as pl
from jax.experimental.pallas import tpu as pltpu
from jax.sharding import Mesh, PartitionSpec as P

KPAD = 2560
HID = 256
AUX = 128
PACK = 2 * HID + AUX
F32 = jnp.float32
BF16 = jnp.bfloat16
NT = (((1,), (1,)), ((), ()))
NN = (((1,), (0,)), ((), ()))
VMEM = pl.BlockSpec(memory_space=pltpu.VMEM)
SMEM = pl.BlockSpec(memory_space=pltpu.SMEM)
PARAMS = pltpu.CompilerParams(vmem_limit_bytes=16 * 1024 * 1024)


def pack_weights(conv_weight):
    taps, cin, cols = conv_weight.shape
    cx = cin - HID
    flipped = jnp.transpose(conv_weight, (2, 0, 1))
    hidden = flipped[:, :, cx:].reshape(cols, taps * HID)
    frame = flipped[:, :, :cx].reshape(cols, taps * cx)
    packed = jnp.concatenate([hidden, frame], axis=1)
    return jnp.pad(packed, ((0, 0), (0, KPAD - packed.shape[1])))


def spread(block, axes):
    count = lax.axis_size(axes)
    copies = jnp.broadcast_to(block[None], (count,) + block.shape)
    return lax.all_to_all(copies, axes, 0, 0)


def shifted(block, axes, step):
    count = lax.axis_size(axes)
    pairs = [(i, i + step) for i in range(count) if 0 <= i + step < count]
    return lax.ppermute(block, axes, pairs)


def ends_kernel(hidden_ref, cell_ref, aux_ref, last_out, first_out):
    for out, start in ((last_out, 14), (first_out, 0)):
        for j in range(2):
            rows = slice(j * 32, (j + 1) * 32)
            out[rows, :HID] = hidden_ref[start + j]
            out[rows, HID : 2 * HID] = cell_ref[start + j].astype(BF16)
            out[rows, 2 * HID :] = aux_ref[start + j]


def ends_of(hidden, cell, aux):
    return pl.pallas_call(
        ends_kernel,
        out_shape=(jax.ShapeDtypeStruct((64, PACK), BF16),) * 2,
        in_specs=[VMEM] * 3,
        out_specs=(VMEM, VMEM),
        compiler_params=PARAMS,
        cost_estimate=pl.CostEstimate(flops=0, bytes_accessed=1_000_000, transcendentals=0),
    )(hidden, cell, aux)


def sides_kernel(hidden_ref, cell_ref, aux_ref, low_ref, high_ref, last_out, first_out, last, first):
    for out, scratch, start, at in ((last_out, last, 16, 14), (first_out, first, 0, 0)):
        cols = slice(start, start + 16)
        for r in range(20):
            into = slice(2 * r, 2 * r + 2)
            if r < 2 or r >= 18:
                ref, j = (low_ref, r) if r < 2 else (high_ref, r - 18)
                block = ref[j * 32 + start : j * 32 + start + 16, :].astype(F32)
                scratch[into, :] = block[at : at + 2]
            else:
                scratch[into, :HID] = hidden_ref[r - 2, cols, :].astype(F32)[at : at + 2]
                scratch[into, HID : 2 * HID] = cell_ref[r - 2, cols, :][at : at + 2]
                scratch[into, 2 * HID :] = aux_ref[r - 2, cols, :].astype(F32)[at : at + 2]
        scratch[40:, :] = jnp.zeros((8, PACK), F32)
        out[...] = scratch[...].astype(BF16)


def sides_of(hidden, cell, aux, low, high):
    return pl.pallas_call(
        sides_kernel,
        out_shape=(jax.ShapeDtypeStruct((48, PACK), BF16),) * 2,
        in_specs=[VMEM] * 5,
        out_specs=(VMEM, VMEM),
        scratch_shapes=[pltpu.VMEM((48, PACK), F32)] * 2,
        compiler_params=PARAMS,
        cost_estimate=pl.CostEstimate(flops=0, bytes_accessed=1_000_000, transcendentals=0),
    )(hidden, cell, aux, low, high)


def placer(tap, first, cx):
    source = lax.broadcasted_iota(jnp.int32, (AUX, AUX), 0)
    target = lax.broadcasted_iota(jnp.int32, (AUX, AUX), 1)
    hit = (target - source == tap * cx - first) & (source >= first) & (source < first + cx)
    return jnp.where(hit, 1.0, 0.0).astype(BF16)


def prep_kernel(
    cx,
    hidden_ref,
    cell_ref,
    aux_ref,
    low_ref,
    high_ref,
    left_ref,
    right_ref,
    patches_out,
    frame_out,
    cell_out,
    keep_out,
    wide,
):
    wide[2:18, 8:40, :HID] = hidden_ref[...].astype(F32)
    wide[2:18, 8:40, HID:] = aux_ref[...].astype(F32)
    for ref, row in ((low_ref, 0), (high_ref, 18)):
        both = ref[...].astype(F32).reshape(2, 32, PACK)
        wide[row : row + 2, 8:40, :HID] = both[:, :, :HID]
        wide[row : row + 2, 8:40, HID:] = both[:, :, 2 * HID :]
    cell_out[:32, :] = low_ref[32:, HID : 2 * HID].astype(F32)
    cell_out[32:544, :] = cell_ref[...].reshape(512, HID)
    cell_out[544:576, :] = high_ref[:32, HID : 2 * HID].astype(F32)
    cell_out[576:, :] = jnp.zeros((48, HID), F32)
    for ref, col, near, base in ((left_ref, 6, 1, 575), (right_ref, 40, 0, 599)):
        rows = ref[...].astype(F32)
        for r in range(20):
            pair = rows[2 * r : 2 * r + 2]
            wide[r, col : col + 2, :HID] = pair[:, :HID]
            wide[r, col : col + 2, HID:] = pair[:, 2 * HID :]
            if 1 <= r < 19:
                cell_out[base + r : base + r + 1, :] = pair[near : near + 1, HID : 2 * HID]

    def border(b, a):
        pad = jnp.zeros((6, HID + AUX), F32)
        left = wide[a : a + 18, 6 + b, :]
        right = wide[a : a + 18, 39 + b, :]
        return jnp.concatenate([left, pad, right, pad], axis=0).astype(BF16)

    first = jnp.zeros((624, AUX), F32)
    second = jnp.zeros((512, AUX), F32)
    for b in range(3):
        cols = wide[:, 7 + b : 39 + b, :].astype(BF16)
        for a in range(3):
            t = 3 * a + b
            core = cols[a : a + 18].reshape(576, HID + AUX)
            edge = border(b, a)
            patches_out[:576, t * HID : (t + 1) * HID] = core[:, :HID]
            patches_out[576:, t * HID : (t + 1) * HID] = edge[:, :HID]
            aux = jnp.concatenate([core[:, HID:], edge[:, HID:]], axis=0)
            first = first + lax.dot_general(aux, placer(t, 0, cx), NN, preferred_element_type=F32)
            second = second + lax.dot_general(
                aux[32:544], placer(t, cx, cx), NN, preferred_element_type=F32
            )
            if t == 4:
                source = lax.broadcasted_iota(jnp.int32, (AUX, AUX), 0)
                copy = jnp.where(source == 2 * cx, 1.0, 0.0).astype(BF16)
                keep_out[...] = lax.dot_general(aux, copy, NN, preferred_element_type=F32)
    patches_out[:, 9 * HID : 9 * HID + AUX] = first.astype(BF16)
    patches_out[:, 9 * HID + AUX :] = jnp.zeros((624, AUX), BF16)
    frame_out[:, :AUX] = second.astype(BF16)
    frame_out[:, AUX:] = jnp.zeros((512, AUX), BF16)


def prepared(cx, hidden, cell, aux, low, high, left, right):
    return pl.pallas_call(
        functools.partial(prep_kernel, cx),
        out_shape=(
            jax.ShapeDtypeStruct((624, KPAD), BF16),
            jax.ShapeDtypeStruct((512, HID), BF16),
            jax.ShapeDtypeStruct((624, HID), F32),
            jax.ShapeDtypeStruct((624, 128), F32),
        ),
        in_specs=[VMEM] * 7,
        out_specs=(VMEM,) * 4,
        scratch_shapes=[pltpu.VMEM((20, 48, HID + AUX), F32)],
        compiler_params=PARAMS,
        cost_estimate=pl.CostEstimate(flops=0, bytes_accessed=12_000_000, transcendentals=0),
    )(hidden, cell, aux, low, high, left, right)


def chooser(half, shape, channel_axis):
    place = lax.broadcasted_iota(jnp.int32, shape, 1 - channel_axis)
    natural = lax.broadcasted_iota(jnp.int32, shape, channel_axis)
    y = lax.shift_right_logical(place, 5)
    zz = lax.shift_right_logical(place, 3) & 3
    wanted = zz * 64 + y * 16 + half * 8 + (place & 7)
    return jnp.where(natural == wanted, 1.0, 0.0).astype(BF16)


def parts_of(value):
    high = value.astype(BF16)
    rest = value - high.astype(F32)
    middle = rest.astype(BF16)
    return high, middle, (rest - middle.astype(F32)).astype(BF16)


def moved(value, choice):
    dots = [lax.dot_general(p, choice, NN, preferred_element_type=F32) for p in parts_of(value)]
    return dots[0] + (dots[1] + dots[2])


def half_step(patches, weight_ref, bias, cell, keep):
    gates = []
    for pair in range(2):
        rhs = jnp.concatenate(
            [
                jnp.concatenate(
                    [
                        weight_ref[y * 4 + x, q * 32 : (q + 1) * 32, :]
                        for q in (2 * pair, 2 * pair + 1)
                        for y in range(4)
                    ],
                    axis=0,
                )
                for x in range(4)
            ],
            axis=1,
        )
        both = lax.dot_general(patches, rhs, NT, preferred_element_type=F32)
        gates.append(both[:, :128] + bias[2 * pair][None])
        gates.append(both[:, 128:] + bias[2 * pair + 1][None])
    sig = lambda v: 0.5 * jnp.tanh(0.5 * v) + 0.5
    cell = sig(gates[1]) * cell + sig(gates[0]) * jnp.tanh(gates[2])
    hidden = (keep * sig(gates[3]) * jnp.tanh(cell)).astype(BF16)
    return hidden, cell


def first_kernel(half_ref, patches_ref, weight_ref, bias_ref, cell_ref, keep_ref, hid_out, cell_out):
    choice = chooser(half_ref[0], (HID, 128), 0)
    cell = moved(cell_ref[...], choice)
    hidden, cell = half_step(patches_ref[...], weight_ref, bias_ref[...], cell, keep_ref[...])
    hid_out[...] = hidden
    cell_out[...] = cell


def first_step(half, patches, weight, bias, cell, keep):
    count = patches.shape[0]
    return pl.pallas_call(
        first_kernel,
        out_shape=(
            jax.ShapeDtypeStruct((count, 128), BF16),
            jax.ShapeDtypeStruct((count, 128), F32),
        ),
        in_specs=[SMEM] + [VMEM] * 5,
        out_specs=(VMEM, VMEM),
        compiler_params=PARAMS,
        cost_estimate=pl.CostEstimate(
            flops=2 * count * KPAD * 512, bytes_accessed=6_000_000, transcendentals=count * 640
        ),
    )(half, patches, weight, bias, cell, keep)


def second_kernel(
    half_ref,
    hid0_ref,
    hid1_ref,
    cell0_ref,
    cell1_ref,
    frame_ref,
    weight0_ref,
    weight1_ref,
    bias_ref,
    keep_ref,
    keep2_ref,
    proj_ref,
    hid_out,
    cell_out,
    flux_out,
    wide,
    patches,
):
    choices = [chooser(half_ref[i], (128, HID), 1) for i in range(2)]
    natural = lax.dot_general(
        hid0_ref[...], choices[0], NN, preferred_element_type=F32
    ) + lax.dot_general(hid1_ref[...], choices[1], NN, preferred_element_type=F32)
    wide[:, 8:40, :] = natural[:576].reshape(18, 32, HID)
    for row in range(18):
        wide[row, 7:8, :] = natural[576 + row : 577 + row]
        wide[row, 40:41, :] = natural[600 + row : 601 + row]
    for b in range(3):
        moved_rows = wide[:, 7 + b : 39 + b, :].astype(BF16)
        for a in range(3):
            t = 3 * a + b
            patches[:, t * HID : (t + 1) * HID] = moved_rows[a : a + 16].reshape(512, HID)
    patches[:, 9 * HID :] = frame_ref[...]
    hid, cell = None, None
    for i, (weight_ref, cell_ref) in enumerate(((weight0_ref, cell0_ref), (weight1_ref, cell1_ref))):
        new_hid, new_cell = half_step(
            patches[...], weight_ref, bias_ref[i], cell_ref[32:544, :], keep_ref[32:544, :]
        )
        one = lax.dot_general(new_hid, choices[i], NN, preferred_element_type=F32)
        two = moved(new_cell, choices[i])
        hid = one if hid is None else hid + one
        cell = two if cell is None else cell + two
    hid = hid.astype(BF16)
    hid_out[...] = hid
    cell_out[...] = cell
    flux = lax.dot_general(proj_ref[...], hid, NT, preferred_element_type=F32)
    for row in range(16):
        flux_out[row : row + 1, :] = flux[0:1, row * 32 : (row + 1) * 32] * keep2_ref[row : row + 1, :]


def second_step(halves, hids, cells, frame, weights, bias, keep, keep2, proj):
    return pl.pallas_call(
        second_kernel,
        out_shape=(
            jax.ShapeDtypeStruct((512, HID), BF16),
            jax.ShapeDtypeStruct((512, HID), F32),
            jax.ShapeDtypeStruct((16, 32), F32),
        ),
        in_specs=[SMEM] + [VMEM] * 11,
        out_specs=(VMEM, VMEM, VMEM),
        scratch_shapes=[pltpu.VMEM((18, 48, HID), F32), pltpu.VMEM((512, KPAD), BF16)],
        compiler_params=PARAMS,
        cost_estimate=pl.CostEstimate(
            flops=2 * 512 * KPAD * 1024, bytes_accessed=8_000_000, transcendentals=512 * 1280
        ),
    )(halves, *hids, *cells, frame, *weights, bias, keep, keep2, proj)


def compute(halves, own, other, prep, land_mask, bias, projection):
    rows, cols = land_mask.shape
    patches1, frame2, cell1, keep1 = prep
    by_half = jnp.transpose(bias.reshape(4, 4, 4, 2, 8), (3, 0, 2, 1, 4)).reshape(2, 4, 128)
    bias2 = jnp.stack([by_half[halves[0]], by_half[halves[1]]])
    hid0, cell0 = first_step(halves[:1], patches1, own, bias2[0], cell1, keep1)
    hid1, cell1 = first_step(halves[1:], patches1, other, bias2[1], cell1, keep1)
    proj = jnp.broadcast_to(projection[None], (16, HID))
    hidden, cell, flux = second_step(
        halves, (hid0, hid1), (cell0, cell1), frame2, (own, other), bias2,
        keep1, land_mask.astype(F32), proj,
    )
    return hidden.reshape(rows, cols, HID), cell.reshape(rows, cols, HID), flux


def aux_of(frames, land_mask):
    rows, cols = land_mask.shape
    both = jnp.transpose(frames, (1, 2, 0, 3)).reshape(rows, cols, -1)
    aux = jnp.concatenate([both, land_mask.astype(BF16)[..., None]], axis=-1)
    return jnp.pad(aux, ((0, 0), (0, 0), (0, AUX - aux.shape[2])))


def body(frames, hidden_init, cell_init, conv_weight, bias, land_mask, projection):
    cx = frames.shape[3]
    x, c = lax.axis_index("x"), lax.axis_index("c")
    packed = pack_weights(conv_weight)
    unit = lax.dynamic_slice(packed, (c * 8, x * (KPAD // 4)), (8, KPAD // 4))
    by_z = spread(unit, "z").reshape(128, KPAD // 4)

    state = (hidden_init, cell_init, aux_of(frames, land_mask))
    last, first = ends_of(*state)
    low = shifted(last, ("x", "c"), 1)
    high = shifted(first, ("x", "c"), -1)
    by_z, low, high = lax.optimization_barrier((by_z, low, high))

    own = spread(by_z, ("y", "x"))
    last, first = sides_of(*state, low, high)
    left = shifted(last, ("z", "y"), 1)
    right = shifted(first, ("z", "y"), -1)
    prep = prepared(cx, *state, low, high, left, right)
    own, prep = lax.optimization_barrier((own, prep))
    other = lax.ppermute(own, "c", [(0, 1), (1, 0)])
    halves = jnp.stack([c, 1 - c]).astype(jnp.int32)
    return compute(halves, own, other, prep, land_mask, bias, projection)


def solution(mesh):
    split = Mesh(mesh.devices.reshape(16, 4, 4, 2), ("z", "y", "x", "c"))
    sx, sy = ("z", "y"), ("x", "c")
    in_specs = (
        P(None, sy, sx, None),
        P(sy, sx, None),
        P(sy, sx, None),
        P(None, None, sx),
        P(),
        P(sy, sx),
        P(),
    )
    out_specs = (P(sy, sx, None), P(sy, sx, None), P(sy, sx))
    return jax.shard_map(body, mesh=split, in_specs=in_specs, out_specs=out_specs, check_vma=False)
```

```python
import functools

import jax
import jax.numpy as jnp
from jax import lax
from jax.experimental import pallas as pl
from jax.experimental.pallas import tpu as pltpu
from jax.sharding import Mesh, PartitionSpec as P

KPAD = 2560
CHUNK = KPAD // 4
HID = 256
AUX = 128
PACK = 2 * HID + AUX
F32 = jnp.float32
BF16 = jnp.bfloat16
NT = (((1,), (1,)), ((), ()))
NN = (((1,), (0,)), ((), ()))
VMEM = pl.BlockSpec(memory_space=pltpu.VMEM)
SMEM = pl.BlockSpec(memory_space=pltpu.SMEM)
PARAMS = pltpu.CompilerParams(vmem_limit_bytes=16 * 1024 * 1024)


def pack_weights(conv_weight):
    taps, cin, cols = conv_weight.shape
    cx = cin - HID
    flipped = jnp.transpose(conv_weight, (2, 0, 1))
    hidden = flipped[:, :, cx:].reshape(cols, taps * HID)
    frame = flipped[:, :, :cx].reshape(cols, taps * cx)
    packed = jnp.concatenate([hidden, frame], axis=1)
    return jnp.pad(packed, ((0, 0), (0, KPAD - packed.shape[1])))


def spread(block, axes):
    count = lax.axis_size(axes)
    copies = jnp.broadcast_to(block[None], (count,) + block.shape)
    return lax.all_to_all(copies, axes, 0, 0)


def turned(block, axis, step):
    count = lax.axis_size(axis)
    return lax.ppermute(block, axis, [(i, (i + step) % count) for i in range(count)])


def shifted(block, axes, step):
    count = lax.axis_size(axes)
    pairs = [(i, i + step) for i in range(count) if 0 <= i + step < count]
    return lax.ppermute(block, axes, pairs)


def ends_kernel(hidden_ref, cell_ref, aux_ref, last_out, first_out):
    for out, start in ((last_out, 14), (first_out, 0)):
        for j in range(2):
            rows = slice(j * 32, (j + 1) * 32)
            out[rows, :HID] = hidden_ref[start + j]
            out[rows, HID : 2 * HID] = cell_ref[start + j].astype(BF16)
            out[rows, 2 * HID :] = aux_ref[start + j]


def ends_of(hidden, cell, aux):
    return pl.pallas_call(
        ends_kernel,
        out_shape=(jax.ShapeDtypeStruct((64, PACK), BF16),) * 2,
        in_specs=[VMEM] * 3,
        out_specs=(VMEM, VMEM),
        compiler_params=PARAMS,
        cost_estimate=pl.CostEstimate(flops=0, bytes_accessed=1_000_000, transcendentals=0),
    )(hidden, cell, aux)


def sides_kernel(hidden_ref, cell_ref, aux_ref, low_ref, high_ref, last_out, first_out, last, first):
    for out, scratch, start, at in ((last_out, last, 16, 14), (first_out, first, 0, 0)):
        cols = slice(start, start + 16)
        for r in range(20):
            into = slice(2 * r, 2 * r + 2)
            if r < 2 or r >= 18:
                ref, j = (low_ref, r) if r < 2 else (high_ref, r - 18)
                block = ref[j * 32 + start : j * 32 + start + 16, :].astype(F32)
                scratch[into, :] = block[at : at + 2]
            else:
                scratch[into, :HID] = hidden_ref[r - 2, cols, :].astype(F32)[at : at + 2]
                scratch[into, HID : 2 * HID] = cell_ref[r - 2, cols, :][at : at + 2]
                scratch[into, 2 * HID :] = aux_ref[r - 2, cols, :].astype(F32)[at : at + 2]
        scratch[40:, :] = jnp.zeros((8, PACK), F32)
        out[...] = scratch[...].astype(BF16)


def sides_of(hidden, cell, aux, low, high):
    return pl.pallas_call(
        sides_kernel,
        out_shape=(jax.ShapeDtypeStruct((48, PACK), BF16),) * 2,
        in_specs=[VMEM] * 5,
        out_specs=(VMEM, VMEM),
        scratch_shapes=[pltpu.VMEM((48, PACK), F32)] * 2,
        compiler_params=PARAMS,
        cost_estimate=pl.CostEstimate(flops=0, bytes_accessed=1_000_000, transcendentals=0),
    )(hidden, cell, aux, low, high)


def placer(tap, first, cx):
    source = lax.broadcasted_iota(jnp.int32, (AUX, AUX), 0)
    target = lax.broadcasted_iota(jnp.int32, (AUX, AUX), 1)
    hit = (target - source == tap * cx - first) & (source >= first) & (source < first + cx)
    return jnp.where(hit, 1.0, 0.0).astype(BF16)


def put(ref, rows, lane, value):
    for i in range(value.shape[1] // 128):
        group = lane // 128 + i
        at = group % 5 * 128
        ref[group // 5, rows, at : at + 128] = value[:, i * 128 : (i + 1) * 128]


def prep_kernel(
    cx,
    hidden_ref,
    cell_ref,
    aux_ref,
    low_ref,
    high_ref,
    left_ref,
    right_ref,
    patches_out,
    frame_out,
    cell_out,
    keep_out,
    wide,
):
    wide[2:18, 8:40, :HID] = hidden_ref[...].astype(F32)
    wide[2:18, 8:40, HID:] = aux_ref[...].astype(F32)
    for ref, row in ((low_ref, 0), (high_ref, 18)):
        both = ref[...].astype(F32).reshape(2, 32, PACK)
        wide[row : row + 2, 8:40, :HID] = both[:, :, :HID]
        wide[row : row + 2, 8:40, HID:] = both[:, :, 2 * HID :]
    cell_out[:32, :] = low_ref[32:, HID : 2 * HID].astype(F32)
    cell_out[32:544, :] = cell_ref[...].reshape(512, HID)
    cell_out[544:576, :] = high_ref[:32, HID : 2 * HID].astype(F32)
    cell_out[576:, :] = jnp.zeros((48, HID), F32)
    for ref, col, near, base in ((left_ref, 6, 1, 575), (right_ref, 40, 0, 599)):
        rows = ref[...].astype(F32)
        for r in range(20):
            pair = rows[2 * r : 2 * r + 2]
            wide[r, col : col + 2, :HID] = pair[:, :HID]
            wide[r, col : col + 2, HID:] = pair[:, 2 * HID :]
            if 1 <= r < 19:
                cell_out[base + r : base + r + 1, :] = pair[near : near + 1, HID : 2 * HID]

    def border(b, a):
        pad = jnp.zeros((6, HID + AUX), F32)
        left = wide[a : a + 18, 6 + b, :]
        right = wide[a : a + 18, 39 + b, :]
        return jnp.concatenate([left, pad, right, pad], axis=0).astype(BF16)

    first = jnp.zeros((624, AUX), F32)
    second = jnp.zeros((512, AUX), F32)
    for b in range(3):
        cols = wide[:, 7 + b : 39 + b, :].astype(BF16)
        for a in range(3):
            t = 3 * a + b
            core = cols[a : a + 18].reshape(576, HID + AUX)
            edge = border(b, a)
            put(patches_out, slice(0, 576), t * HID, core[:, :HID])
            put(patches_out, slice(576, 624), t * HID, edge[:, :HID])
            aux = jnp.concatenate([core[:, HID:], edge[:, HID:]], axis=0)
            first = first + lax.dot_general(aux, placer(t, 0, cx), NN, preferred_element_type=F32)
            second = second + lax.dot_general(
                aux[32:544], placer(t, cx, cx), NN, preferred_element_type=F32
            )
            if t == 4:
                source = lax.broadcasted_iota(jnp.int32, (AUX, AUX), 0)
                copy = jnp.where(source == 2 * cx, 1.0, 0.0).astype(BF16)
                keep_out[...] = lax.dot_general(aux, copy, NN, preferred_element_type=F32)
    put(patches_out, slice(0, 624), 9 * HID, first.astype(BF16))
    put(patches_out, slice(0, 624), 9 * HID + AUX, jnp.zeros((624, AUX), BF16))
    frame_out[:, :AUX] = second.astype(BF16)
    frame_out[:, AUX:] = jnp.zeros((512, AUX), BF16)


def prepared(cx, hidden, cell, aux, low, high, left, right):
    return pl.pallas_call(
        functools.partial(prep_kernel, cx),
        out_shape=(
            jax.ShapeDtypeStruct((4, 624, CHUNK), BF16),
            jax.ShapeDtypeStruct((512, HID), BF16),
            jax.ShapeDtypeStruct((624, HID), F32),
            jax.ShapeDtypeStruct((624, 128), F32),
        ),
        in_specs=[VMEM] * 7,
        out_specs=(VMEM,) * 4,
        scratch_shapes=[pltpu.VMEM((20, 48, HID + AUX), F32)],
        compiler_params=PARAMS,
        cost_estimate=pl.CostEstimate(flops=0, bytes_accessed=100_000, transcendentals=0),
    )(hidden, cell, aux, low, high, left, right)


def chooser(half, shape, channel_axis):
    place = lax.broadcasted_iota(jnp.int32, shape, 1 - channel_axis)
    natural = lax.broadcasted_iota(jnp.int32, shape, channel_axis)
    y = lax.shift_right_logical(place, 5)
    zz = lax.shift_right_logical(place, 3) & 3
    wanted = zz * 64 + y * 16 + half * 8 + (place & 7)
    return jnp.where(natural == wanted, 1.0, 0.0).astype(BF16)


def parts_of(value):
    high = value.astype(BF16)
    rest = value - high.astype(F32)
    middle = rest.astype(BF16)
    return high, middle, (rest - middle.astype(F32)).astype(BF16)


def moved(value, choice):
    dots = [lax.dot_general(p, choice, NN, preferred_element_type=F32) for p in parts_of(value)]
    return dots[0] + (dots[1] + dots[2])


def product(patches, weight_ref, pair):
    rhs = jnp.concatenate(
        [
            weight_ref[y, q * 32 : (q + 1) * 32, :]
            for q in (2 * pair, 2 * pair + 1)
            for y in range(4)
        ],
        axis=0,
    )
    return lax.dot_general(patches, rhs, NT, preferred_element_type=F32)


def sigmoid(value):
    return 0.5 * jnp.tanh(0.5 * value) + 0.5


def updated(sums, bias, cell, keep):
    in_gate = sigmoid(sums[0][:, :128] + bias[0][None])
    decay_factor = sigmoid(sums[0][:, 128:] + bias[1][None])
    candidate = jnp.tanh(sums[1][:, :128] + bias[2][None])
    out_gate = sigmoid(sums[1][:, 128:] + bias[3][None])
    cell = decay_factor * cell + in_gate * candidate
    return (keep * out_gate * jnp.tanh(cell)).astype(BF16), cell


def partial_kernel(slot, more, ids_ref, patches_ref, own_ref, other_ref, *refs):
    total = refs[-1]
    patches = patches_ref[ids_ref[slot]]
    for i, weight_ref in enumerate((own_ref, other_ref)):
        for pair in range(2):
            value = product(patches, weight_ref, pair)
            if more:
                value = value + refs[0][i, pair]
            total[i, pair] = value


def partial(slot, ids, patches, own, other, *before):
    count = patches.shape[1]
    return pl.pallas_call(
        functools.partial(partial_kernel, slot, len(before) > 0),
        out_shape=jax.ShapeDtypeStruct((2, 2, count, HID), F32),
        in_specs=[SMEM] + [VMEM] * (3 + len(before)),
        out_specs=VMEM,
        input_output_aliases={4: 0} if before else {},
        compiler_params=PARAMS,
        cost_estimate=pl.CostEstimate(flops=0, bytes_accessed=100_000, transcendentals=0),
    )(ids, patches, own, other, *before)


def final_kernel(
    ids_ref,
    half_ref,
    patches_ref,
    total_ref,
    own0,
    own1,
    own2,
    own3,
    other0,
    other1,
    other2,
    other3,
    bias_ref,
    cell_ref,
    keep_ref,
    frame_ref,
    keep2_ref,
    proj_ref,
    hid_out,
    cell_out,
    flux_out,
    wide,
    patches,
):
    weights = ((own0, own1, own2, own3), (other0, other1, other2, other3))
    choices = [chooser(half_ref[i], (128, HID), 1) for i in range(2)]
    natural, cells = None, []
    for i in range(2):
        sums = []
        for pair in range(2):
            value = total_ref[i, pair]
            for slot in (1, 2, 3):
                value = value + product(patches_ref[ids_ref[slot]], weights[i][slot], pair)
            sums.append(value)
        cell = moved(cell_ref[...], chooser(half_ref[i], (HID, 128), 0))
        hid, cell = updated(sums, bias_ref[i], cell, keep_ref[...])
        cells.append(cell[32:544])
        one = lax.dot_general(hid, choices[i], NN, preferred_element_type=F32)
        natural = one if natural is None else natural + one

    wide[:, 8:40, :] = natural[:576].reshape(18, 32, HID)
    for row in range(18):
        wide[row, 7:8, :] = natural[576 + row : 577 + row]
        wide[row, 40:41, :] = natural[600 + row : 601 + row]
    for b in range(3):
        moved_rows = wide[:, 7 + b : 39 + b, :].astype(BF16)
        for a in range(3):
            put(patches, slice(0, 512), (3 * a + b) * HID, moved_rows[a : a + 16].reshape(512, HID))
    put(patches, slice(0, 512), 9 * HID, frame_ref[...])

    hid, cell = None, None
    for i in range(2):
        sums = []
        for pair in range(2):
            value = None
            for slot in range(4):
                part = product(patches[ids_ref[slot]], weights[i][slot], pair)
                value = part if value is None else value + part
            sums.append(value)
        new_hid, new_cell = updated(sums, bias_ref[i], cells[i], keep_ref[32:544, :])
        one = lax.dot_general(new_hid, choices[i], NN, preferred_element_type=F32)
        two = moved(new_cell, choices[i])
        hid = one if hid is None else hid + one
        cell = two if cell is None else cell + two
    hid = hid.astype(BF16)
    hid_out[...] = hid
    cell_out[...] = cell
    flux = lax.dot_general(proj_ref[...], hid, NT, preferred_element_type=F32)
    for row in range(16):
        flux_out[row : row + 1, :] = flux[0:1, row * 32 : (row + 1) * 32] * keep2_ref[row : row + 1, :]


def finished(ids, halves, patches, total, own, other, bias, cell, keep, frame, keep2, proj):
    return pl.pallas_call(
        final_kernel,
        out_shape=(
            jax.ShapeDtypeStruct((512, HID), BF16),
            jax.ShapeDtypeStruct((512, HID), F32),
            jax.ShapeDtypeStruct((16, 32), F32),
        ),
        in_specs=[SMEM] * 2 + [VMEM] * 16,
        out_specs=(VMEM, VMEM, VMEM),
        scratch_shapes=[pltpu.VMEM((18, 48, HID), F32), pltpu.VMEM((4, 512, CHUNK), BF16)],
        compiler_params=PARAMS,
        cost_estimate=pl.CostEstimate(
            flops=2 * 824 * KPAD * 1024, bytes_accessed=14_000_000, transcendentals=1136 * 1280
        ),
    )(ids, halves, patches, total, *own, *other, bias, cell, keep, frame, keep2, proj)


def compute(ids, halves, own, swapped, prep, land_mask, bias2, proj):
    rows, cols = land_mask.shape
    patches1, frame2, cell1, keep1 = prep
    other = [swapped(0, own[0])]
    total = partial(0, ids, patches1, own[0], other[0])
    later, total = lax.optimization_barrier((own[1:], total))
    own = own[:1] + later
    other += [swapped(slot, own[slot]) for slot in (1, 2, 3)]
    hidden, cell, flux = finished(
        ids, halves, patches1, total, own, other, bias2, cell1, keep1, frame2,
        land_mask.astype(F32), proj,
    )
    return hidden.reshape(rows, cols, HID), cell.reshape(rows, cols, HID), flux


def bias_of(bias, c):
    by_half = jnp.transpose(bias.reshape(4, 4, 4, 2, 8), (3, 0, 2, 1, 4)).reshape(2, 4, 128)
    return jnp.where(c == 0, by_half, by_half[::-1])


def aux_of(frames, land_mask):
    rows, cols = land_mask.shape
    both = jnp.transpose(frames, (1, 2, 0, 3)).reshape(rows, cols, -1)
    aux = jnp.concatenate([both, land_mask.astype(BF16)[..., None]], axis=-1)
    return jnp.pad(aux, ((0, 0), (0, 0), (0, AUX - aux.shape[2])))


def body(frames, hidden_init, cell_init, conv_weight, bias, land_mask, projection):
    cx = frames.shape[3]
    x, c = lax.axis_index("x"), lax.axis_index("c")
    packed = pack_weights(conv_weight)
    unit = lax.dynamic_slice(packed, (c * 8, x * (KPAD // 4)), (8, KPAD // 4))
    by_z = spread(unit, "z").reshape(128, KPAD // 4)

    state = (hidden_init, cell_init, aux_of(frames, land_mask))
    last, first = ends_of(*state)
    low = shifted(last, ("x", "c"), 1)
    high = shifted(first, ("x", "c"), -1)
    halves = jnp.stack([c, 1 - c]).astype(jnp.int32)
    ids = jnp.stack([x, (x + 2) % 4, (x + 1) % 4, (x + 3) % 4]).astype(jnp.int32)
    proj = jnp.broadcast_to(projection[None], (16, HID))
    bias2 = bias_of(bias, c)
    by_z, low, high, halves, ids, proj, bias2 = lax.optimization_barrier(
        (by_z, low, high, halves, ids, proj, bias2)
    )

    by_y = spread(by_z, "y")
    last, first = sides_of(*state, low, high)
    left = shifted(last, ("z", "y"), 1)
    right = shifted(first, ("z", "y"), -1)
    by_y, left, right = lax.optimization_barrier((by_y, left, right))

    own = [by_y] + [turned(by_y, "x", step) for step in (2, -1, 1)]
    prep = prepared(cx, *state, low, high, left, right)
    swapped = lambda slot, piece: turned(piece, "c", 1)
    return compute(ids, halves, own, swapped, prep, land_mask, bias2, proj)


def solution(mesh):
    split = Mesh(mesh.devices.reshape(16, 4, 4, 2), ("z", "y", "x", "c"))
    sx, sy = ("z", "y"), ("x", "c")
    in_specs = (
        P(None, sy, sx, None),
        P(sy, sx, None),
        P(sy, sx, None),
        P(None, None, sx),
        P(),
        P(sy, sx),
        P(),
    )
    out_specs = (P(sy, sx, None), P(sy, sx, None), P(sy, sx))
    return jax.shard_map(body, mesh=split, in_specs=in_specs, out_specs=out_specs, check_vma=False)
```

```python
import functools

import jax
import jax.numpy as jnp
from jax import lax
from jax.experimental import pallas as pl
from jax.experimental.pallas import tpu as pltpu
from jax.sharding import Mesh, PartitionSpec as P

KPAD = 2560
CHUNK = KPAD // 4
HID = 256
AUX = 128
PACK = 2 * HID + AUX
F32 = jnp.float32
BF16 = jnp.bfloat16
NT = (((1,), (1,)), ((), ()))
NN = (((1,), (0,)), ((), ()))
VMEM = pl.BlockSpec(memory_space=pltpu.VMEM)
SMEM = pl.BlockSpec(memory_space=pltpu.SMEM)
PARAMS = pltpu.CompilerParams(vmem_limit_bytes=16 * 1024 * 1024)


def pack_weights(conv_weight):
    taps, cin, cols = conv_weight.shape
    cx = cin - HID
    flipped = jnp.transpose(conv_weight, (2, 0, 1))
    hidden = flipped[:, :, cx:].reshape(cols, taps * HID)
    frame = flipped[:, :, :cx].reshape(cols, taps * cx)
    packed = jnp.concatenate([hidden, frame], axis=1)
    return jnp.pad(packed, ((0, 0), (0, KPAD - packed.shape[1])))


def spread(block, axes):
    count = lax.axis_size(axes)
    copies = jnp.broadcast_to(block[None], (count,) + block.shape)
    return lax.all_to_all(copies, axes, 0, 0)


def turned(block, axis, step):
    count = lax.axis_size(axis)
    return lax.ppermute(block, axis, [(i, (i + step) % count) for i in range(count)])


def shifted(block, axes, step):
    count = lax.axis_size(axes)
    pairs = [(i, i + step) for i in range(count) if 0 <= i + step < count]
    return lax.ppermute(block, axes, pairs)


def ends_kernel(hidden_ref, cell_ref, aux_ref, last_out, first_out):
    for out, start in ((last_out, 14), (first_out, 0)):
        for j in range(2):
            rows = slice(j * 32, (j + 1) * 32)
            out[rows, :HID] = hidden_ref[start + j]
            out[rows, HID : 2 * HID] = cell_ref[start + j].astype(BF16)
            out[rows, 2 * HID :] = aux_ref[start + j]


def ends_of(hidden, cell, aux):
    return pl.pallas_call(
        ends_kernel,
        out_shape=(jax.ShapeDtypeStruct((64, PACK), BF16),) * 2,
        in_specs=[VMEM] * 3,
        out_specs=(VMEM, VMEM),
        compiler_params=PARAMS,
        cost_estimate=pl.CostEstimate(flops=0, bytes_accessed=1_000_000, transcendentals=0),
    )(hidden, cell, aux)


def sides_kernel(hidden_ref, cell_ref, aux_ref, low_ref, high_ref, last_out, first_out, last, first):
    for out, scratch, start, at in ((last_out, last, 16, 14), (first_out, first, 0, 0)):
        cols = slice(start, start + 16)
        for r in range(20):
            into = slice(2 * r, 2 * r + 2)
            if r < 2 or r >= 18:
                ref, j = (low_ref, r) if r < 2 else (high_ref, r - 18)
                block = ref[j * 32 + start : j * 32 + start + 16, :].astype(F32)
                scratch[into, :] = block[at : at + 2]
            else:
                scratch[into, :HID] = hidden_ref[r - 2, cols, :].astype(F32)[at : at + 2]
                scratch[into, HID : 2 * HID] = cell_ref[r - 2, cols, :][at : at + 2]
                scratch[into, 2 * HID :] = aux_ref[r - 2, cols, :].astype(F32)[at : at + 2]
        scratch[40:, :] = jnp.zeros((8, PACK), F32)
        out[...] = scratch[...].astype(BF16)


def sides_of(hidden, cell, aux, low, high):
    return pl.pallas_call(
        sides_kernel,
        out_shape=(jax.ShapeDtypeStruct((48, PACK), BF16),) * 2,
        in_specs=[VMEM] * 5,
        out_specs=(VMEM, VMEM),
        scratch_shapes=[pltpu.VMEM((48, PACK), F32)] * 2,
        compiler_params=PARAMS,
        cost_estimate=pl.CostEstimate(flops=0, bytes_accessed=1_000_000, transcendentals=0),
    )(hidden, cell, aux, low, high)


def placer(tap, first, cx):
    source = lax.broadcasted_iota(jnp.int32, (AUX, AUX), 0)
    target = lax.broadcasted_iota(jnp.int32, (AUX, AUX), 1)
    hit = (target - source == tap * cx - first) & (source >= first) & (source < first + cx)
    return jnp.where(hit, 1.0, 0.0).astype(BF16)


def put(ref, rows, lane, value):
    for i in range(value.shape[1] // 128):
        group = lane // 128 + i
        at = group % 5 * 128
        ref[group // 5, rows, at : at + 128] = value[:, i * 128 : (i + 1) * 128]


def prep_kernel(
    cx,
    hidden_ref,
    cell_ref,
    aux_ref,
    low_ref,
    high_ref,
    left_ref,
    right_ref,
    patches_out,
    frame_out,
    cell_out,
    keep_out,
    wide,
):
    wide[2:18, 8:40, :HID] = hidden_ref[...].astype(F32)
    wide[2:18, 8:40, HID:] = aux_ref[...].astype(F32)
    for ref, row in ((low_ref, 0), (high_ref, 18)):
        both = ref[...].astype(F32).reshape(2, 32, PACK)
        wide[row : row + 2, 8:40, :HID] = both[:, :, :HID]
        wide[row : row + 2, 8:40, HID:] = both[:, :, 2 * HID :]
    cell_out[:32, :] = low_ref[32:, HID : 2 * HID].astype(F32)
    cell_out[32:544, :] = cell_ref[...].reshape(512, HID)
    cell_out[544:576, :] = high_ref[:32, HID : 2 * HID].astype(F32)
    cell_out[576:, :] = jnp.zeros((48, HID), F32)
    for ref, col, near, base in ((left_ref, 6, 1, 575), (right_ref, 40, 0, 599)):
        rows = ref[...].astype(F32)
        for r in range(20):
            pair = rows[2 * r : 2 * r + 2]
            wide[r, col : col + 2, :HID] = pair[:, :HID]
            wide[r, col : col + 2, HID:] = pair[:, 2 * HID :]
            if 1 <= r < 19:
                cell_out[base + r : base + r + 1, :] = pair[near : near + 1, HID : 2 * HID]

    def border(b, a):
        pad = jnp.zeros((6, HID + AUX), F32)
        left = wide[a : a + 18, 6 + b, :]
        right = wide[a : a + 18, 39 + b, :]
        return jnp.concatenate([left, pad, right, pad], axis=0).astype(BF16)

    first = jnp.zeros((624, AUX), F32)
    second = jnp.zeros((512, AUX), F32)
    for b in range(3):
        cols = wide[:, 7 + b : 39 + b, :].astype(BF16)
        for a in range(3):
            t = 3 * a + b
            core = cols[a : a + 18].reshape(576, HID + AUX)
            edge = border(b, a)
            put(patches_out, slice(0, 576), t * HID, core[:, :HID])
            put(patches_out, slice(576, 624), t * HID, edge[:, :HID])
            aux = jnp.concatenate([core[:, HID:], edge[:, HID:]], axis=0)
            first = first + lax.dot_general(aux, placer(t, 0, cx), NN, preferred_element_type=F32)
            second = second + lax.dot_general(
                aux[32:544], placer(t, cx, cx), NN, preferred_element_type=F32
            )
            if t == 4:
                source = lax.broadcasted_iota(jnp.int32, (AUX, AUX), 0)
                copy = jnp.where(source == 2 * cx, 1.0, 0.0).astype(BF16)
                keep_out[...] = lax.dot_general(aux, copy, NN, preferred_element_type=F32)
    put(patches_out, slice(0, 624), 9 * HID, first.astype(BF16))
    put(patches_out, slice(0, 624), 9 * HID + AUX, jnp.zeros((624, AUX), BF16))
    frame_out[:, :AUX] = second.astype(BF16)
    frame_out[:, AUX:] = jnp.zeros((512, AUX), BF16)


def prepared(cx, hidden, cell, aux, low, high, left, right):
    return pl.pallas_call(
        functools.partial(prep_kernel, cx),
        out_shape=(
            jax.ShapeDtypeStruct((4, 624, CHUNK), BF16),
            jax.ShapeDtypeStruct((512, HID), BF16),
            jax.ShapeDtypeStruct((624, HID), F32),
            jax.ShapeDtypeStruct((624, 128), F32),
        ),
        in_specs=[VMEM] * 7,
        out_specs=(VMEM,) * 4,
        scratch_shapes=[pltpu.VMEM((20, 48, HID + AUX), F32)],
        compiler_params=PARAMS,
        cost_estimate=pl.CostEstimate(flops=0, bytes_accessed=100_000, transcendentals=0),
    )(hidden, cell, aux, low, high, left, right)


def chooser(half, shape, channel_axis):
    place = lax.broadcasted_iota(jnp.int32, shape, 1 - channel_axis)
    natural = lax.broadcasted_iota(jnp.int32, shape, channel_axis)
    y = lax.shift_right_logical(place, 5)
    zz = lax.shift_right_logical(place, 3) & 3
    wanted = zz * 64 + y * 16 + half * 8 + (place & 7)
    return jnp.where(natural == wanted, 1.0, 0.0).astype(BF16)


def parts_of(value):
    high = value.astype(BF16)
    rest = value - high.astype(F32)
    middle = rest.astype(BF16)
    return high, middle, (rest - middle.astype(F32)).astype(BF16)


def moved(value, choice):
    dots = [lax.dot_general(p, choice, NN, preferred_element_type=F32) for p in parts_of(value)]
    return dots[0] + (dots[1] + dots[2])


def product(patches, weight_ref, pair, chunk=0):
    rhs = jnp.concatenate(
        [
            weight_ref[chunk * 4 + y, q * 32 : (q + 1) * 32, :]
            for q in (2 * pair, 2 * pair + 1)
            for y in range(4)
        ],
        axis=0,
    )
    return lax.dot_general(patches, rhs, NT, preferred_element_type=F32)


def sigmoid(value):
    return 0.5 * jnp.tanh(0.5 * value) + 0.5


def updated(sums, bias, cell, keep):
    in_gate = sigmoid(sums[0][:, :128] + bias[0][None])
    decay_factor = sigmoid(sums[0][:, 128:] + bias[1][None])
    candidate = jnp.tanh(sums[1][:, :128] + bias[2][None])
    out_gate = sigmoid(sums[1][:, 128:] + bias[3][None])
    cell = decay_factor * cell + in_gate * candidate
    return (keep * out_gate * jnp.tanh(cell)).astype(BF16), cell


def partial_kernel(ids_ref, patches_ref, own_ref, other_ref, total):
    patches = patches_ref[ids_ref[0]]
    for i, weight_ref in enumerate((own_ref, other_ref)):
        for pair in range(2):
            total[i, pair] = product(patches, weight_ref, pair)


def partial(ids, patches, own, other):
    count = patches.shape[1]
    return pl.pallas_call(
        partial_kernel,
        out_shape=jax.ShapeDtypeStruct((2, 2, count, HID), F32),
        in_specs=[SMEM] + [VMEM] * 3,
        out_specs=VMEM,
        compiler_params=PARAMS,
        cost_estimate=pl.CostEstimate(flops=0, bytes_accessed=100_000, transcendentals=0),
    )(ids, patches, own, other)


def first_half(i, half, ids_ref, patches_ref, total_ref, rest_ref, bias_ref, cell_ref, keep_ref):
    sums = []
    for pair in range(2):
        value = total_ref[i, pair]
        for slot in (1, 2, 3):
            value = value + product(patches_ref[ids_ref[slot]], rest_ref, pair, slot - 1)
        sums.append(value)
    cell = moved(cell_ref[...], chooser(half, (HID, 128), 0))
    return updated(sums, bias_ref[i], cell, keep_ref[...])


def own_kernel(ids_ref, half_ref, *refs):
    *ins, hid_out, cell_out = refs
    hid_out[...], cell_out[...] = first_half(0, half_ref[0], ids_ref, *ins)


def own_half(ids, halves, patches, total, rest, bias, cell, keep):
    count = patches.shape[1]
    return pl.pallas_call(
        own_kernel,
        out_shape=(
            jax.ShapeDtypeStruct((count, 128), BF16),
            jax.ShapeDtypeStruct((count, 128), F32),
        ),
        in_specs=[SMEM] * 2 + [VMEM] * 6,
        out_specs=(VMEM, VMEM),
        compiler_params=PARAMS,
        cost_estimate=pl.CostEstimate(
            flops=2 * count * KPAD * 512, bytes_accessed=6_000_000, transcendentals=count * 640
        ),
    )(ids, halves, patches, total, rest, bias, cell, keep)


def final_kernel(
    ids_ref,
    half_ref,
    patches_ref,
    total_ref,
    own0,
    own_rest,
    other0,
    other_rest,
    bias_ref,
    cell_ref,
    keep_ref,
    hid0_ref,
    cell0_ref,
    frame_ref,
    keep2_ref,
    proj_ref,
    hid_out,
    cell_out,
    flux_out,
    wide,
    patches,
):
    choices = [chooser(half_ref[i], (128, HID), 1) for i in range(2)]
    hid, cell = first_half(
        1, half_ref[1], ids_ref, patches_ref, total_ref, other_rest, bias_ref, cell_ref, keep_ref
    )
    cells = (cell0_ref[32:544, :], cell[32:544])
    natural = lax.dot_general(
        hid0_ref[...], choices[0], NN, preferred_element_type=F32
    ) + lax.dot_general(hid, choices[1], NN, preferred_element_type=F32)

    wide[:, 8:40, :] = natural[:576].reshape(18, 32, HID)
    for row in range(18):
        wide[row, 7:8, :] = natural[576 + row : 577 + row]
        wide[row, 40:41, :] = natural[600 + row : 601 + row]
    for b in range(3):
        moved_rows = wide[:, 7 + b : 39 + b, :].astype(BF16)
        for a in range(3):
            put(patches, slice(0, 512), (3 * a + b) * HID, moved_rows[a : a + 16].reshape(512, HID))
    put(patches, slice(0, 512), 9 * HID, frame_ref[...])

    hid, cell = None, None
    for i, (first_ref, rest_ref) in enumerate(((own0, own_rest), (other0, other_rest))):
        sums = []
        for pair in range(2):
            value = product(patches[ids_ref[0]], first_ref, pair)
            for slot in (1, 2, 3):
                value = value + product(patches[ids_ref[slot]], rest_ref, pair, slot - 1)
            sums.append(value)
        new_hid, new_cell = updated(sums, bias_ref[i], cells[i], keep_ref[32:544, :])
        one = lax.dot_general(new_hid, choices[i], NN, preferred_element_type=F32)
        two = moved(new_cell, choices[i])
        hid = one if hid is None else hid + one
        cell = two if cell is None else cell + two
    hid = hid.astype(BF16)
    hid_out[...] = hid
    cell_out[...] = cell
    flux = lax.dot_general(proj_ref[...], hid, NT, preferred_element_type=F32)
    for row in range(16):
        flux_out[row : row + 1, :] = flux[0:1, row * 32 : (row + 1) * 32] * keep2_ref[row : row + 1, :]


def finished(ids, halves, *arrays):
    return pl.pallas_call(
        final_kernel,
        out_shape=(
            jax.ShapeDtypeStruct((512, HID), BF16),
            jax.ShapeDtypeStruct((512, HID), F32),
            jax.ShapeDtypeStruct((16, 32), F32),
        ),
        in_specs=[SMEM] * 2 + [VMEM] * len(arrays),
        out_specs=(VMEM, VMEM, VMEM),
        scratch_shapes=[pltpu.VMEM((18, 48, HID), F32), pltpu.VMEM((4, 512, CHUNK), BF16)],
        compiler_params=PARAMS,
        cost_estimate=pl.CostEstimate(
            flops=2 * 824 * KPAD * 1024, bytes_accessed=14_000_000, transcendentals=1136 * 1280
        ),
    )(ids, halves, *arrays)


def compute(ids, halves, own0, pieces, swapped, prep, land_mask, bias2, proj):
    rows, cols = land_mask.shape
    patches1, frame2, cell1, keep1 = prep
    other0 = swapped(0, own0)
    total = partial(ids, patches1, own0, other0)
    pieces, total = lax.optimization_barrier((pieces, total))
    own_rest = jnp.concatenate(pieces, axis=0)
    other_rest = swapped(1, own_rest)
    hid0, cell0 = own_half(ids, halves, patches1, total, own_rest, bias2, cell1, keep1)
    hidden, cell, flux = finished(
        ids, halves, patches1, total, own0, own_rest, other0, other_rest, bias2, cell1, keep1,
        hid0, cell0, frame2, land_mask.astype(F32), proj,
    )
    return hidden.reshape(rows, cols, HID), cell.reshape(rows, cols, HID), flux


def bias_of(bias, c):
    by_half = jnp.transpose(bias.reshape(4, 4, 4, 2, 8), (3, 0, 2, 1, 4)).reshape(2, 4, 128)
    return jnp.where(c == 0, by_half, by_half[::-1])


def aux_of(frames, land_mask):
    rows, cols = land_mask.shape
    both = jnp.transpose(frames, (1, 2, 0, 3)).reshape(rows, cols, -1)
    aux = jnp.concatenate([both, land_mask.astype(BF16)[..., None]], axis=-1)
    return jnp.pad(aux, ((0, 0), (0, 0), (0, AUX - aux.shape[2])))


def body(frames, hidden_init, cell_init, conv_weight, bias, land_mask, projection):
    cx = frames.shape[3]
    x, c = lax.axis_index("x"), lax.axis_index("c")
    packed = pack_weights(conv_weight)
    unit = lax.dynamic_slice(packed, (c * 8, x * (KPAD // 4)), (8, KPAD // 4))
    by_z = spread(unit, "z").reshape(128, KPAD // 4)

    state = (hidden_init, cell_init, aux_of(frames, land_mask))
    last, first = ends_of(*state)
    low = shifted(last, ("x", "c"), 1)
    high = shifted(first, ("x", "c"), -1)
    halves = jnp.stack([c, 1 - c]).astype(jnp.int32)
    ids = jnp.stack([x, (x + 2) % 4, (x + 1) % 4, (x + 3) % 4]).astype(jnp.int32)
    proj = jnp.broadcast_to(projection[None], (16, HID))
    bias2 = bias_of(bias, c)
    by_z, low, high, halves, ids, proj, bias2 = lax.optimization_barrier(
        (by_z, low, high, halves, ids, proj, bias2)
    )

    by_y = spread(by_z, "y")
    last, first = sides_of(*state, low, high)
    left = shifted(last, ("z", "y"), 1)
    right = shifted(first, ("z", "y"), -1)

    low_half, high_half = by_y[:2], by_y[2:]
    up_low = turned(low_half, "x", 1)
    down_high = turned(high_half, "x", -1)
    up_high = turned(high_half, "x", 1)
    down_low = turned(low_half, "x", -1)
    far_low = turned(up_low, "x", 1)
    far_high = turned(down_high, "x", -1)
    pieces = [far_low, far_high, down_low, down_high, up_low, up_high]
    prep = prepared(cx, *state, low, high, left, right)
    swapped = lambda slot, piece: turned(piece, "c", 1)
    return compute(ids, halves, by_y, pieces, swapped, prep, land_mask, bias2, proj)


def solution(mesh):
    split = Mesh(mesh.devices.reshape(16, 4, 4, 2), ("z", "y", "x", "c"))
    sx, sy = ("z", "y"), ("x", "c")
    in_specs = (
        P(None, sy, sx, None),
        P(sy, sx, None),
        P(sy, sx, None),
        P(None, None, sx),
        P(),
        P(sy, sx),
        P(),
    )
    out_specs = (P(sy, sx, None), P(sy, sx, None), P(sy, sx))
    return jax.shard_map(body, mesh=split, in_specs=in_specs, out_specs=out_specs, check_vma=False)
```

```python
import functools

import jax
import jax.numpy as jnp
from jax import lax
from jax.experimental import pallas as pl
from jax.experimental.pallas import tpu as pltpu
from jax.sharding import Mesh, PartitionSpec as P

KPAD = 2560
CHUNK = KPAD // 4
HID = 256
AUX = 128
PACK = 2 * HID + AUX
F32 = jnp.float32
BF16 = jnp.bfloat16
NT = (((1,), (1,)), ((), ()))
NN = (((1,), (0,)), ((), ()))
VMEM = pl.BlockSpec(memory_space=pltpu.VMEM)
SMEM = pl.BlockSpec(memory_space=pltpu.SMEM)
PARAMS = pltpu.CompilerParams(vmem_limit_bytes=16 * 1024 * 1024)


def pack_weights(conv_weight):
    taps, cin, cols = conv_weight.shape
    cx = cin - HID
    flipped = jnp.transpose(conv_weight, (2, 0, 1))
    hidden = flipped[:, :, cx:].reshape(cols, taps * HID)
    frame = flipped[:, :, :cx].reshape(cols, taps * cx)
    packed = jnp.concatenate([hidden, frame], axis=1)
    return jnp.pad(packed, ((0, 0), (0, KPAD - packed.shape[1])))


def spread(block, axes):
    count = lax.axis_size(axes)
    copies = jnp.broadcast_to(block[None], (count,) + block.shape)
    return lax.all_to_all(copies, axes, 0, 0)


def turned(block, axis, step):
    count = lax.axis_size(axis)
    return lax.ppermute(block, axis, [(i, (i + step) % count) for i in range(count)])


def shifted(block, axes, step):
    count = lax.axis_size(axes)
    pairs = [(i, i + step) for i in range(count) if 0 <= i + step < count]
    return lax.ppermute(block, axes, pairs)


def ends_kernel(hidden_ref, cell_ref, aux_ref, last_out, first_out):
    for out, start in ((last_out, 14), (first_out, 0)):
        for j in range(2):
            rows = slice(j * 32, (j + 1) * 32)
            out[rows, :HID] = hidden_ref[start + j]
            out[rows, HID : 2 * HID] = cell_ref[start + j].astype(BF16)
            out[rows, 2 * HID :] = aux_ref[start + j]


def ends_of(hidden, cell, aux):
    return pl.pallas_call(
        ends_kernel,
        out_shape=(jax.ShapeDtypeStruct((64, PACK), BF16),) * 2,
        in_specs=[VMEM] * 3,
        out_specs=(VMEM, VMEM),
        compiler_params=PARAMS,
        cost_estimate=pl.CostEstimate(flops=0, bytes_accessed=1_000_000, transcendentals=0),
    )(hidden, cell, aux)


def sides_kernel(hidden_ref, cell_ref, aux_ref, low_ref, high_ref, last_out, first_out, last, first):
    for out, scratch, start, at in ((last_out, last, 16, 14), (first_out, first, 0, 0)):
        cols = slice(start, start + 16)
        for r in range(20):
            into = slice(2 * r, 2 * r + 2)
            if r < 2 or r >= 18:
                ref, j = (low_ref, r) if r < 2 else (high_ref, r - 18)
                block = ref[j * 32 + start : j * 32 + start + 16, :].astype(F32)
                scratch[into, :] = block[at : at + 2]
            else:
                scratch[into, :HID] = hidden_ref[r - 2, cols, :].astype(F32)[at : at + 2]
                scratch[into, HID : 2 * HID] = cell_ref[r - 2, cols, :][at : at + 2]
                scratch[into, 2 * HID :] = aux_ref[r - 2, cols, :].astype(F32)[at : at + 2]
        scratch[40:, :] = jnp.zeros((8, PACK), F32)
        out[...] = scratch[...].astype(BF16)


def sides_of(hidden, cell, aux, low, high):
    return pl.pallas_call(
        sides_kernel,
        out_shape=(jax.ShapeDtypeStruct((48, PACK), BF16),) * 2,
        in_specs=[VMEM] * 5,
        out_specs=(VMEM, VMEM),
        scratch_shapes=[pltpu.VMEM((48, PACK), F32)] * 2,
        compiler_params=PARAMS,
        cost_estimate=pl.CostEstimate(flops=0, bytes_accessed=1_000_000, transcendentals=0),
    )(hidden, cell, aux, low, high)


def placer(tap, first, cx):
    source = lax.broadcasted_iota(jnp.int32, (AUX, AUX), 0)
    target = lax.broadcasted_iota(jnp.int32, (AUX, AUX), 1)
    hit = (target - source == tap * cx - first) & (source >= first) & (source < first + cx)
    return jnp.where(hit, 1.0, 0.0).astype(BF16)


def put(ref, rows, lane, value):
    for i in range(value.shape[1] // 128):
        group = lane // 128 + i
        at = group % 5 * 128
        ref[group // 5, rows, at : at + 128] = value[:, i * 128 : (i + 1) * 128]


def prep_kernel(
    cx,
    hidden_ref,
    cell_ref,
    aux_ref,
    low_ref,
    high_ref,
    left_ref,
    right_ref,
    patches_out,
    frame_out,
    cell_out,
    keep_out,
    wide,
):
    wide[2:18, 8:40, :HID] = hidden_ref[...].astype(F32)
    wide[2:18, 8:40, HID:] = aux_ref[...].astype(F32)
    for ref, row in ((low_ref, 0), (high_ref, 18)):
        both = ref[...].astype(F32).reshape(2, 32, PACK)
        wide[row : row + 2, 8:40, :HID] = both[:, :, :HID]
        wide[row : row + 2, 8:40, HID:] = both[:, :, 2 * HID :]
    cell_out[:32, :] = low_ref[32:, HID : 2 * HID].astype(F32)
    cell_out[32:544, :] = cell_ref[...].reshape(512, HID)
    cell_out[544:576, :] = high_ref[:32, HID : 2 * HID].astype(F32)
    cell_out[576:, :] = jnp.zeros((48, HID), F32)
    for ref, col, near, base in ((left_ref, 6, 1, 575), (right_ref, 40, 0, 599)):
        rows = ref[...].astype(F32)
        for r in range(20):
            pair = rows[2 * r : 2 * r + 2]
            wide[r, col : col + 2, :HID] = pair[:, :HID]
            wide[r, col : col + 2, HID:] = pair[:, 2 * HID :]
            if 1 <= r < 19:
                cell_out[base + r : base + r + 1, :] = pair[near : near + 1, HID : 2 * HID]

    def border(b, a):
        pad = jnp.zeros((6, HID + AUX), F32)
        left = wide[a : a + 18, 6 + b, :]
        right = wide[a : a + 18, 39 + b, :]
        return jnp.concatenate([left, pad, right, pad], axis=0).astype(BF16)

    first = jnp.zeros((624, AUX), F32)
    second = jnp.zeros((512, AUX), F32)
    for b in range(3):
        cols = wide[:, 7 + b : 39 + b, :].astype(BF16)
        for a in range(3):
            t = 3 * a + b
            core = cols[a : a + 18].reshape(576, HID + AUX)
            edge = border(b, a)
            put(patches_out, slice(0, 576), t * HID, core[:, :HID])
            put(patches_out, slice(576, 624), t * HID, edge[:, :HID])
            aux = jnp.concatenate([core[:, HID:], edge[:, HID:]], axis=0)
            first = first + lax.dot_general(aux, placer(t, 0, cx), NN, preferred_element_type=F32)
            second = second + lax.dot_general(
                aux[32:544], placer(t, cx, cx), NN, preferred_element_type=F32
            )
            if t == 4:
                source = lax.broadcasted_iota(jnp.int32, (AUX, AUX), 0)
                copy = jnp.where(source == 2 * cx, 1.0, 0.0).astype(BF16)
                keep_out[...] = lax.dot_general(aux, copy, NN, preferred_element_type=F32)
    put(patches_out, slice(0, 624), 9 * HID, first.astype(BF16))
    put(patches_out, slice(0, 624), 9 * HID + AUX, jnp.zeros((624, AUX), BF16))
    frame_out[:, :AUX] = second.astype(BF16)
    frame_out[:, AUX:] = jnp.zeros((512, AUX), BF16)


def prepared(cx, hidden, cell, aux, low, high, left, right):
    return pl.pallas_call(
        functools.partial(prep_kernel, cx),
        out_shape=(
            jax.ShapeDtypeStruct((4, 624, CHUNK), BF16),
            jax.ShapeDtypeStruct((512, HID), BF16),
            jax.ShapeDtypeStruct((624, HID), F32),
            jax.ShapeDtypeStruct((624, 128), F32),
        ),
        in_specs=[VMEM] * 7,
        out_specs=(VMEM,) * 4,
        scratch_shapes=[pltpu.VMEM((20, 48, HID + AUX), F32)],
        compiler_params=PARAMS,
        cost_estimate=pl.CostEstimate(flops=0, bytes_accessed=100_000, transcendentals=0),
    )(hidden, cell, aux, low, high, left, right)


def chooser(half, shape, channel_axis):
    place = lax.broadcasted_iota(jnp.int32, shape, 1 - channel_axis)
    natural = lax.broadcasted_iota(jnp.int32, shape, channel_axis)
    y = lax.shift_right_logical(place, 5)
    zz = lax.shift_right_logical(place, 3) & 3
    wanted = zz * 64 + y * 16 + half * 8 + (place & 7)
    return jnp.where(natural == wanted, 1.0, 0.0).astype(BF16)


def parts_of(value):
    high = value.astype(BF16)
    rest = value - high.astype(F32)
    middle = rest.astype(BF16)
    return high, middle, (rest - middle.astype(F32)).astype(BF16)


def moved(value, choice):
    dots = [lax.dot_general(p, choice, NN, preferred_element_type=F32) for p in parts_of(value)]
    return dots[0] + (dots[1] + dots[2])


def product(patches, weight_ref, pair, chunk=0):
    rhs = jnp.concatenate(
        [
            weight_ref[chunk * 4 + y, q * 32 : (q + 1) * 32, :]
            for q in (2 * pair, 2 * pair + 1)
            for y in range(4)
        ],
        axis=0,
    )
    return lax.dot_general(patches, rhs, NT, preferred_element_type=F32)


def sigmoid(value):
    return 0.5 * jnp.tanh(0.5 * value) + 0.5


def updated(sums, bias, cell, keep):
    in_gate = sigmoid(sums[0][:, :128] + bias[0][None])
    decay_factor = sigmoid(sums[0][:, 128:] + bias[1][None])
    candidate = jnp.tanh(sums[1][:, :128] + bias[2][None])
    out_gate = sigmoid(sums[1][:, 128:] + bias[3][None])
    cell = decay_factor * cell + in_gate * candidate
    return (keep * out_gate * jnp.tanh(cell)).astype(BF16), cell


def gate_sums(patches_ref, ids_ref, weight_ref):
    sums = []
    for pair in range(2):
        value = None
        for slot in range(4):
            part = product(patches_ref[ids_ref[slot]], weight_ref, pair, slot)
            value = part if value is None else value + part
        sums.append(value)
    return sums


def first_half(i, half, ids_ref, patches_ref, weight_ref, bias_ref, cell_ref, keep_ref):
    sums = gate_sums(patches_ref, ids_ref, weight_ref)
    cell = moved(cell_ref[...], chooser(half, (HID, 128), 0))
    return updated(sums, bias_ref[i], cell, keep_ref[...])


def own_kernel(ids_ref, half_ref, *refs):
    *ins, hid_out, cell_out = refs
    hid_out[...], cell_out[...] = first_half(0, half_ref[0], ids_ref, *ins)


def own_half(ids, halves, patches, weight, bias, cell, keep):
    count = patches.shape[1]
    return pl.pallas_call(
        own_kernel,
        out_shape=(
            jax.ShapeDtypeStruct((count, 128), BF16),
            jax.ShapeDtypeStruct((count, 128), F32),
        ),
        in_specs=[SMEM] * 2 + [VMEM] * 5,
        out_specs=(VMEM, VMEM),
        compiler_params=PARAMS,
        cost_estimate=pl.CostEstimate(
            flops=2 * count * KPAD * 512, bytes_accessed=6_000_000, transcendentals=count * 640
        ),
    )(ids, halves, patches, weight, bias, cell, keep)


def final_kernel(
    ids_ref,
    half_ref,
    patches_ref,
    own_ref,
    other_ref,
    bias_ref,
    cell_ref,
    keep_ref,
    hid0_ref,
    cell0_ref,
    frame_ref,
    keep2_ref,
    proj_ref,
    hid_out,
    cell_out,
    flux_out,
    wide,
    patches,
):
    choices = [chooser(half_ref[i], (128, HID), 1) for i in range(2)]
    hid, cell = first_half(
        1, half_ref[1], ids_ref, patches_ref, other_ref, bias_ref, cell_ref, keep_ref
    )
    cells = (cell0_ref[32:544, :], cell[32:544])
    natural = lax.dot_general(
        hid0_ref[...], choices[0], NN, preferred_element_type=F32
    ) + lax.dot_general(hid, choices[1], NN, preferred_element_type=F32)

    wide[:, 8:40, :] = natural[:576].reshape(18, 32, HID)
    for row in range(18):
        wide[row, 7:8, :] = natural[576 + row : 577 + row]
        wide[row, 40:41, :] = natural[600 + row : 601 + row]
    for b in range(3):
        moved_rows = wide[:, 7 + b : 39 + b, :].astype(BF16)
        for a in range(3):
            put(patches, slice(0, 512), (3 * a + b) * HID, moved_rows[a : a + 16].reshape(512, HID))
    put(patches, slice(0, 512), 9 * HID, frame_ref[...])

    hid, cell = None, None
    for i, weight_ref in enumerate((own_ref, other_ref)):
        sums = gate_sums(patches, ids_ref, weight_ref)
        new_hid, new_cell = updated(sums, bias_ref[i], cells[i], keep_ref[32:544, :])
        one = lax.dot_general(new_hid, choices[i], NN, preferred_element_type=F32)
        two = moved(new_cell, choices[i])
        hid = one if hid is None else hid + one
        cell = two if cell is None else cell + two
    hid = hid.astype(BF16)
    hid_out[...] = hid
    cell_out[...] = cell
    flux = lax.dot_general(proj_ref[...], hid, NT, preferred_element_type=F32)
    for row in range(16):
        flux_out[row : row + 1, :] = flux[0:1, row * 32 : (row + 1) * 32] * keep2_ref[row : row + 1, :]


def finished(ids, halves, *arrays):
    return pl.pallas_call(
        final_kernel,
        out_shape=(
            jax.ShapeDtypeStruct((512, HID), BF16),
            jax.ShapeDtypeStruct((512, HID), F32),
            jax.ShapeDtypeStruct((16, 32), F32),
        ),
        in_specs=[SMEM] * 2 + [VMEM] * len(arrays),
        out_specs=(VMEM, VMEM, VMEM),
        scratch_shapes=[pltpu.VMEM((18, 48, HID), F32), pltpu.VMEM((4, 512, CHUNK), BF16)],
        compiler_params=PARAMS,
        cost_estimate=pl.CostEstimate(
            flops=2 * 824 * KPAD * 1024, bytes_accessed=14_000_000, transcendentals=1136 * 1280
        ),
    )(ids, halves, *arrays)


def compute(ids, halves, own, swapped, prep, land_mask, bias2, proj):
    rows, cols = land_mask.shape
    patches1, frame2, cell1, keep1 = prep
    other = swapped(own)
    hid0, cell0 = own_half(ids, halves, patches1, own, bias2, cell1, keep1)
    hidden, cell, flux = finished(
        ids, halves, patches1, own, other, bias2, cell1, keep1,
        hid0, cell0, frame2, land_mask.astype(F32), proj,
    )
    return hidden.reshape(rows, cols, HID), cell.reshape(rows, cols, HID), flux


def bias_of(bias, c):
    by_half = jnp.transpose(bias.reshape(4, 4, 4, 2, 8), (3, 0, 2, 1, 4)).reshape(2, 4, 128)
    return jnp.where(c == 0, by_half, by_half[::-1])


def aux_of(frames, land_mask):
    rows, cols = land_mask.shape
    both = jnp.transpose(frames, (1, 2, 0, 3)).reshape(rows, cols, -1)
    aux = jnp.concatenate([both, land_mask.astype(BF16)[..., None]], axis=-1)
    return jnp.pad(aux, ((0, 0), (0, 0), (0, AUX - aux.shape[2])))


def body(frames, hidden_init, cell_init, conv_weight, bias, land_mask, projection):
    cx = frames.shape[3]
    x, c = lax.axis_index("x"), lax.axis_index("c")
    packed = pack_weights(conv_weight)
    unit = lax.dynamic_slice(packed, (c * 8, x * (KPAD // 4)), (8, KPAD // 4))
    by_z = spread(unit, "z").reshape(128, KPAD // 4)

    state = (hidden_init, cell_init, aux_of(frames, land_mask))
    last, first = ends_of(*state)
    low = shifted(last, ("x", "c"), 1)
    high = shifted(first, ("x", "c"), -1)
    last, first = sides_of(*state, low, high)
    left = shifted(last, ("z", "y"), 1)
    right = shifted(first, ("z", "y"), -1)
    halves = jnp.stack([c, 1 - c]).astype(jnp.int32)
    ids = jnp.stack([x, (x + 2) % 4, (x + 1) % 4, (x + 3) % 4]).astype(jnp.int32)
    proj = jnp.broadcast_to(projection[None], (16, HID))
    bias2 = bias_of(bias, c)
    by_z, left, right, halves, ids, proj, bias2 = lax.optimization_barrier(
        (by_z, left, right, halves, ids, proj, bias2)
    )

    by_y = spread(by_z, "y")
    up = turned(by_y, "x", 1)
    down = turned(by_y, "x", -1)
    prep = prepared(cx, *state, low, high, left, right)
    up, down, prep = lax.optimization_barrier((up, down, prep))
    far_low = turned(up[:2], "x", 1)
    far_high = turned(down[2:], "x", -1)
    own = jnp.concatenate([by_y, far_low, far_high, down, up], axis=0)
    swapped = lambda piece: turned(piece, "c", 1)
    return compute(ids, halves, own, swapped, prep, land_mask, bias2, proj)


def solution(mesh):
    split = Mesh(mesh.devices.reshape(16, 4, 4, 2), ("z", "y", "x", "c"))
    sx, sy = ("z", "y"), ("x", "c")
    in_specs = (
        P(None, sy, sx, None),
        P(sy, sx, None),
        P(sy, sx, None),
        P(None, None, sx),
        P(),
        P(sy, sx),
        P(),
    )
    out_specs = (P(sy, sx, None), P(sy, sx, None), P(sy, sx))
    return jax.shard_map(body, mesh=split, in_specs=in_specs, out_specs=out_specs, check_vma=False)
```

```python
import functools

import jax
import jax.numpy as jnp
from jax import lax
from jax.experimental import pallas as pl
from jax.experimental.pallas import tpu as pltpu
from jax.sharding import Mesh, PartitionSpec as P

KPAD = 2560
CHUNK = KPAD // 4
HID = 256
AUX = 128
PACK = 2 * HID + AUX
F32 = jnp.float32
BF16 = jnp.bfloat16
NT = (((1,), (1,)), ((), ()))
NN = (((1,), (0,)), ((), ()))
VMEM = pl.BlockSpec(memory_space=pltpu.VMEM)
SMEM = pl.BlockSpec(memory_space=pltpu.SMEM)
PARAMS = pltpu.CompilerParams(vmem_limit_bytes=16 * 1024 * 1024)


def pack_weights(conv_weight):
    taps, cin, cols = conv_weight.shape
    cx = cin - HID
    flipped = jnp.transpose(conv_weight, (2, 0, 1))
    hidden = flipped[:, :, cx:].reshape(cols, taps * HID)
    frame = flipped[:, :, :cx].reshape(cols, taps * cx)
    packed = jnp.concatenate([hidden, frame], axis=1)
    return jnp.pad(packed, ((0, 0), (0, KPAD - packed.shape[1])))


def spread(block, axes):
    count = lax.axis_size(axes)
    copies = jnp.broadcast_to(block[None], (count,) + block.shape)
    return lax.all_to_all(copies, axes, 0, 0)


def turned(block, axis, step):
    count = lax.axis_size(axis)
    return lax.ppermute(block, axis, [(i, (i + step) % count) for i in range(count)])


def shifted(block, axes, step):
    count = lax.axis_size(axes)
    pairs = [(i, i + step) for i in range(count) if 0 <= i + step < count]
    return lax.ppermute(block, axes, pairs)


def ends_kernel(hidden_ref, cell_ref, aux_ref, last_out, first_out):
    for out, start in ((last_out, 14), (first_out, 0)):
        for j in range(2):
            rows = slice(j * 32, (j + 1) * 32)
            out[rows, :HID] = hidden_ref[start + j]
            out[rows, HID : 2 * HID] = cell_ref[start + j].astype(BF16)
            out[rows, 2 * HID :] = aux_ref[start + j]


def ends_of(hidden, cell, aux):
    return pl.pallas_call(
        ends_kernel,
        out_shape=(jax.ShapeDtypeStruct((64, PACK), BF16),) * 2,
        in_specs=[VMEM] * 3,
        out_specs=(VMEM, VMEM),
        compiler_params=PARAMS,
        cost_estimate=pl.CostEstimate(flops=0, bytes_accessed=1_000_000, transcendentals=0),
    )(hidden, cell, aux)


def sides_kernel(hidden_ref, cell_ref, aux_ref, low_ref, high_ref, last_out, first_out, last, first):
    for out, scratch, start, at in ((last_out, last, 16, 14), (first_out, first, 0, 0)):
        cols = slice(start, start + 16)
        for r in range(20):
            into = slice(2 * r, 2 * r + 2)
            if r < 2 or r >= 18:
                ref, j = (low_ref, r) if r < 2 else (high_ref, r - 18)
                block = ref[j * 32 + start : j * 32 + start + 16, :].astype(F32)
                scratch[into, :] = block[at : at + 2]
            else:
                scratch[into, :HID] = hidden_ref[r - 2, cols, :].astype(F32)[at : at + 2]
                scratch[into, HID : 2 * HID] = cell_ref[r - 2, cols, :][at : at + 2]
                scratch[into, 2 * HID :] = aux_ref[r - 2, cols, :].astype(F32)[at : at + 2]
        scratch[40:, :] = jnp.zeros((8, PACK), F32)
        out[...] = scratch[...].astype(BF16)


def sides_of(hidden, cell, aux, low, high):
    return pl.pallas_call(
        sides_kernel,
        out_shape=(jax.ShapeDtypeStruct((48, PACK), BF16),) * 2,
        in_specs=[VMEM] * 5,
        out_specs=(VMEM, VMEM),
        scratch_shapes=[pltpu.VMEM((48, PACK), F32)] * 2,
        compiler_params=PARAMS,
        cost_estimate=pl.CostEstimate(flops=0, bytes_accessed=1_000_000, transcendentals=0),
    )(hidden, cell, aux, low, high)


def placer(tap, first, cx):
    source = lax.broadcasted_iota(jnp.int32, (AUX, AUX), 0)
    target = lax.broadcasted_iota(jnp.int32, (AUX, AUX), 1)
    hit = (target - source == tap * cx - first) & (source >= first) & (source < first + cx)
    return jnp.where(hit, 1.0, 0.0).astype(BF16)


def put(ref, rows, lane, value):
    for i in range(value.shape[1] // 128):
        group = lane // 128 + i
        at = group % 5 * 128
        ref[group // 5, rows, at : at + 128] = value[:, i * 128 : (i + 1) * 128]


def prep_kernel(
    cx,
    hidden_ref,
    cell_ref,
    aux_ref,
    low_ref,
    high_ref,
    left_ref,
    right_ref,
    patches_out,
    frame_out,
    cell_out,
    keep_out,
    wide,
):
    wide[2:18, 8:40, :HID] = hidden_ref[...].astype(F32)
    wide[2:18, 8:40, HID:] = aux_ref[...].astype(F32)
    for ref, row in ((low_ref, 0), (high_ref, 18)):
        both = ref[...].astype(F32).reshape(2, 32, PACK)
        wide[row : row + 2, 8:40, :HID] = both[:, :, :HID]
        wide[row : row + 2, 8:40, HID:] = both[:, :, 2 * HID :]
    cell_out[:32, :] = low_ref[32:, HID : 2 * HID].astype(F32)
    cell_out[32:544, :] = cell_ref[...].reshape(512, HID)
    cell_out[544:576, :] = high_ref[:32, HID : 2 * HID].astype(F32)
    cell_out[576:, :] = jnp.zeros((48, HID), F32)
    for ref, col, near, base in ((left_ref, 6, 1, 575), (right_ref, 40, 0, 599)):
        rows = ref[...].astype(F32)
        for r in range(20):
            pair = rows[2 * r : 2 * r + 2]
            wide[r, col : col + 2, :HID] = pair[:, :HID]
            wide[r, col : col + 2, HID:] = pair[:, 2 * HID :]
            if 1 <= r < 19:
                cell_out[base + r : base + r + 1, :] = pair[near : near + 1, HID : 2 * HID]

    def border(b, a):
        pad = jnp.zeros((6, HID + AUX), F32)
        left = wide[a : a + 18, 6 + b, :]
        right = wide[a : a + 18, 39 + b, :]
        return jnp.concatenate([left, pad, right, pad], axis=0).astype(BF16)

    first = jnp.zeros((624, AUX), F32)
    second = jnp.zeros((512, AUX), F32)
    for b in range(3):
        cols = wide[:, 7 + b : 39 + b, :].astype(BF16)
        for a in range(3):
            t = 3 * a + b
            core = cols[a : a + 18].reshape(576, HID + AUX)
            edge = border(b, a)
            put(patches_out, slice(0, 576), t * HID, core[:, :HID])
            put(patches_out, slice(576, 624), t * HID, edge[:, :HID])
            aux = jnp.concatenate([core[:, HID:], edge[:, HID:]], axis=0)
            first = first + lax.dot_general(aux, placer(t, 0, cx), NN, preferred_element_type=F32)
            second = second + lax.dot_general(
                aux[32:544], placer(t, cx, cx), NN, preferred_element_type=F32
            )
            if t == 4:
                source = lax.broadcasted_iota(jnp.int32, (AUX, AUX), 0)
                copy = jnp.where(source == 2 * cx, 1.0, 0.0).astype(BF16)
                keep_out[...] = lax.dot_general(aux, copy, NN, preferred_element_type=F32)
    put(patches_out, slice(0, 624), 9 * HID, first.astype(BF16))
    put(patches_out, slice(0, 624), 9 * HID + AUX, jnp.zeros((624, AUX), BF16))
    frame_out[:, :AUX] = second.astype(BF16)
    frame_out[:, AUX:] = jnp.zeros((512, AUX), BF16)


def prepared(cx, hidden, cell, aux, low, high, left, right):
    return pl.pallas_call(
        functools.partial(prep_kernel, cx),
        out_shape=(
            jax.ShapeDtypeStruct((4, 624, CHUNK), BF16),
            jax.ShapeDtypeStruct((512, HID), BF16),
            jax.ShapeDtypeStruct((624, HID), F32),
            jax.ShapeDtypeStruct((624, 128), F32),
        ),
        in_specs=[VMEM] * 7,
        out_specs=(VMEM,) * 4,
        scratch_shapes=[pltpu.VMEM((20, 48, HID + AUX), F32)],
        compiler_params=PARAMS,
        cost_estimate=pl.CostEstimate(flops=0, bytes_accessed=100_000, transcendentals=0),
    )(hidden, cell, aux, low, high, left, right)


def chooser(half, shape, channel_axis):
    place = lax.broadcasted_iota(jnp.int32, shape, 1 - channel_axis)
    natural = lax.broadcasted_iota(jnp.int32, shape, channel_axis)
    y = lax.shift_right_logical(place, 5)
    zz = lax.shift_right_logical(place, 3) & 3
    wanted = zz * 64 + y * 16 + half * 8 + (place & 7)
    return jnp.where(natural == wanted, 1.0, 0.0).astype(BF16)


def parts_of(value):
    high = value.astype(BF16)
    rest = value - high.astype(F32)
    middle = rest.astype(BF16)
    return high, middle, (rest - middle.astype(F32)).astype(BF16)


def moved(value, choice):
    dots = [lax.dot_general(p, choice, NN, preferred_element_type=F32) for p in parts_of(value)]
    return dots[0] + (dots[1] + dots[2])


def product(patches, weight_ref, pair, x):
    rhs = jnp.concatenate(
        [
            weight_ref[y * 4 + x, q * 32 : (q + 1) * 32, :]
            for q in (2 * pair, 2 * pair + 1)
            for y in range(4)
        ],
        axis=0,
    )
    return lax.dot_general(patches, rhs, NT, preferred_element_type=F32)


def sigmoid(value):
    return 0.5 * jnp.tanh(0.5 * value) + 0.5


def updated(sums, bias, cell, keep):
    in_gate = sigmoid(sums[0][:, :128] + bias[0][None])
    decay_factor = sigmoid(sums[0][:, 128:] + bias[1][None])
    candidate = jnp.tanh(sums[1][:, :128] + bias[2][None])
    out_gate = sigmoid(sums[1][:, 128:] + bias[3][None])
    cell = decay_factor * cell + in_gate * candidate
    return (keep * out_gate * jnp.tanh(cell)).astype(BF16), cell


def gate_sums(patches_ref, weight_ref):
    sums = []
    for pair in range(2):
        value = None
        for x in range(4):
            part = product(patches_ref[x], weight_ref, pair, x)
            value = part if value is None else value + part
        sums.append(value)
    return sums


def first_half(i, half, patches_ref, weight_ref, bias_ref, cell_ref, keep_ref):
    sums = gate_sums(patches_ref, weight_ref)
    cell = moved(cell_ref[...], chooser(half, (HID, 128), 0))
    return updated(sums, bias_ref[i], cell, keep_ref[...])


def own_kernel(half_ref, *refs):
    *ins, hid_out, cell_out = refs
    hid_out[...], cell_out[...] = first_half(0, half_ref[0], *ins)


def own_half(halves, patches, weight, bias, cell, keep):
    count = patches.shape[1]
    return pl.pallas_call(
        own_kernel,
        out_shape=(
            jax.ShapeDtypeStruct((count, 128), BF16),
            jax.ShapeDtypeStruct((count, 128), F32),
        ),
        in_specs=[SMEM] + [VMEM] * 5,
        out_specs=(VMEM, VMEM),
        compiler_params=PARAMS,
        cost_estimate=pl.CostEstimate(
            flops=2 * count * KPAD * 512, bytes_accessed=6_000_000, transcendentals=count * 640
        ),
    )(halves, patches, weight, bias, cell, keep)


def final_kernel(
    half_ref,
    patches_ref,
    own_ref,
    other_ref,
    bias_ref,
    cell_ref,
    keep_ref,
    hid0_ref,
    cell0_ref,
    frame_ref,
    keep2_ref,
    proj_ref,
    hid_out,
    cell_out,
    flux_out,
    wide,
    patches,
):
    choices = [chooser(half_ref[i], (128, HID), 1) for i in range(2)]
    hid, cell = first_half(
        1, half_ref[1], patches_ref, other_ref, bias_ref, cell_ref, keep_ref
    )
    cells = (cell0_ref[32:544, :], cell[32:544])
    natural = lax.dot_general(
        hid0_ref[...], choices[0], NN, preferred_element_type=F32
    ) + lax.dot_general(hid, choices[1], NN, preferred_element_type=F32)

    wide[:, 8:40, :] = natural[:576].reshape(18, 32, HID)
    for row in range(18):
        wide[row, 7:8, :] = natural[576 + row : 577 + row]
        wide[row, 40:41, :] = natural[600 + row : 601 + row]
    for b in range(3):
        moved_rows = wide[:, 7 + b : 39 + b, :].astype(BF16)
        for a in range(3):
            put(patches, slice(0, 512), (3 * a + b) * HID, moved_rows[a : a + 16].reshape(512, HID))
    put(patches, slice(0, 512), 9 * HID, frame_ref[...])

    hid, cell = None, None
    for i, weight_ref in enumerate((own_ref, other_ref)):
        sums = gate_sums(patches, weight_ref)
        new_hid, new_cell = updated(sums, bias_ref[i], cells[i], keep_ref[32:544, :])
        one = lax.dot_general(new_hid, choices[i], NN, preferred_element_type=F32)
        two = moved(new_cell, choices[i])
        hid = one if hid is None else hid + one
        cell = two if cell is None else cell + two
    hid = hid.astype(BF16)
    hid_out[...] = hid
    cell_out[...] = cell
    flux = lax.dot_general(proj_ref[...], hid, NT, preferred_element_type=F32)
    for row in range(16):
        flux_out[row : row + 1, :] = flux[0:1, row * 32 : (row + 1) * 32] * keep2_ref[row : row + 1, :]


def finished(halves, *arrays):
    return pl.pallas_call(
        final_kernel,
        out_shape=(
            jax.ShapeDtypeStruct((512, HID), BF16),
            jax.ShapeDtypeStruct((512, HID), F32),
            jax.ShapeDtypeStruct((16, 32), F32),
        ),
        in_specs=[SMEM] + [VMEM] * len(arrays),
        out_specs=(VMEM, VMEM, VMEM),
        scratch_shapes=[pltpu.VMEM((18, 48, HID), F32), pltpu.VMEM((4, 512, CHUNK), BF16)],
        compiler_params=PARAMS,
        cost_estimate=pl.CostEstimate(
            flops=2 * 824 * KPAD * 1024, bytes_accessed=14_000_000, transcendentals=1136 * 1280
        ),
    )(halves, *arrays)


def compute(halves, own, swapped, prep, land_mask, bias2, proj):
    rows, cols = land_mask.shape
    patches1, frame2, cell1, keep1 = prep
    other = swapped(own)
    hid0, cell0 = own_half(halves, patches1, own, bias2, cell1, keep1)
    hidden, cell, flux = finished(
        halves, patches1, own, other, bias2, cell1, keep1,
        hid0, cell0, frame2, land_mask.astype(F32), proj,
    )
    return hidden.reshape(rows, cols, HID), cell.reshape(rows, cols, HID), flux


def bias_of(bias, c):
    by_half = jnp.transpose(bias.reshape(4, 4, 4, 2, 8), (3, 0, 2, 1, 4)).reshape(2, 4, 128)
    return jnp.where(c == 0, by_half, by_half[::-1])


def aux_of(frames, land_mask):
    rows, cols = land_mask.shape
    both = jnp.transpose(frames, (1, 2, 0, 3)).reshape(rows, cols, -1)
    aux = jnp.concatenate([both, land_mask.astype(BF16)[..., None]], axis=-1)
    return jnp.pad(aux, ((0, 0), (0, 0), (0, AUX - aux.shape[2])))


def body(frames, hidden_init, cell_init, conv_weight, bias, land_mask, projection):
    cx = frames.shape[3]
    x, c = lax.axis_index("x"), lax.axis_index("c")
    packed = pack_weights(conv_weight)
    unit = lax.dynamic_slice(packed, (c * 8, x * (KPAD // 4)), (8, KPAD // 4))
    by_z = spread(unit, "z").reshape(128, KPAD // 4)

    state = (hidden_init, cell_init, aux_of(frames, land_mask))
    last, first = ends_of(*state)
    low = shifted(last, ("x", "c"), 1)
    high = shifted(first, ("x", "c"), -1)
    last, first = sides_of(*state, low, high)
    left = shifted(last, ("z", "y"), 1)
    right = shifted(first, ("z", "y"), -1)
    halves = jnp.stack([c, 1 - c]).astype(jnp.int32)
    proj = jnp.broadcast_to(projection[None], (16, HID))
    bias2 = bias_of(bias, c)
    by_z, left, right, halves, proj, bias2 = lax.optimization_barrier(
        (by_z, left, right, halves, proj, bias2)
    )

    own = spread(by_z, ("y", "x"))
    prep = prepared(cx, *state, low, high, left, right)
    swapped = lambda piece: turned(piece, "c", 1)
    return compute(halves, own, swapped, prep, land_mask, bias2, proj)


def solution(mesh):
    split = Mesh(mesh.devices.reshape(16, 4, 4, 2), ("z", "y", "x", "c"))
    sx, sy = ("z", "y"), ("x", "c")
    in_specs = (
        P(None, sy, sx, None),
        P(sy, sx, None),
        P(sy, sx, None),
        P(None, None, sx),
        P(),
        P(sy, sx),
        P(),
    )
    out_specs = (P(sy, sx, None), P(sy, sx, None), P(sy, sx))
    return jax.shard_map(body, mesh=split, in_specs=in_specs, out_specs=out_specs, check_vma=False)
```

```python
import functools

import jax
import jax.numpy as jnp
from jax import lax
from jax.experimental import pallas as pl
from jax.experimental.pallas import tpu as pltpu
from jax.sharding import Mesh, PartitionSpec as P

KPAD = 2560
CHUNK = KPAD // 4
HID = 256
AUX = 128
PACK = 2 * HID + AUX
F32 = jnp.float32
BF16 = jnp.bfloat16
NT = (((1,), (1,)), ((), ()))
NN = (((1,), (0,)), ((), ()))
VMEM = pl.BlockSpec(memory_space=pltpu.VMEM)
SMEM = pl.BlockSpec(memory_space=pltpu.SMEM)
PARAMS = pltpu.CompilerParams(vmem_limit_bytes=16 * 1024 * 1024)


def pack_weights(conv_weight):
    taps, cin, cols = conv_weight.shape
    cx = cin - HID
    flipped = jnp.transpose(conv_weight, (2, 0, 1))
    hidden = flipped[:, :, cx:].reshape(cols, taps * HID)
    frame = flipped[:, :, :cx].reshape(cols, taps * cx)
    packed = jnp.concatenate([hidden, frame], axis=1)
    return jnp.pad(packed, ((0, 0), (0, KPAD - packed.shape[1])))


def spread(block, axes):
    count = lax.axis_size(axes)
    copies = jnp.broadcast_to(block[None], (count,) + block.shape)
    return lax.all_to_all(copies, axes, 0, 0)


def turned(block, axis, step):
    count = lax.axis_size(axis)
    return lax.ppermute(block, axis, [(i, (i + step) % count) for i in range(count)])


def shifted(block, axes, step):
    count = lax.axis_size(axes)
    pairs = [(i, i + step) for i in range(count) if 0 <= i + step < count]
    return lax.ppermute(block, axes, pairs)


def ends_kernel(hidden_ref, cell_ref, aux_ref, last_out, first_out):
    for out, start in ((last_out, 14), (first_out, 0)):
        for j in range(2):
            rows = slice(j * 32, (j + 1) * 32)
            out[rows, :HID] = hidden_ref[start + j]
            out[rows, HID : 2 * HID] = cell_ref[start + j].astype(BF16)
            out[rows, 2 * HID :] = aux_ref[start + j]


def ends_of(hidden, cell, aux):
    return pl.pallas_call(
        ends_kernel,
        out_shape=(jax.ShapeDtypeStruct((64, PACK), BF16),) * 2,
        in_specs=[VMEM] * 3,
        out_specs=(VMEM, VMEM),
        compiler_params=PARAMS,
        cost_estimate=pl.CostEstimate(flops=0, bytes_accessed=1_000_000, transcendentals=0),
    )(hidden, cell, aux)


def sides_kernel(hidden_ref, cell_ref, aux_ref, low_ref, high_ref, last_out, first_out, last, first):
    for out, scratch, start, at in ((last_out, last, 16, 14), (first_out, first, 0, 0)):
        cols = slice(start, start + 16)
        for r in range(20):
            into = slice(2 * r, 2 * r + 2)
            if r < 2 or r >= 18:
                ref, j = (low_ref, r) if r < 2 else (high_ref, r - 18)
                block = ref[j * 32 + start : j * 32 + start + 16, :].astype(F32)
                scratch[into, :] = block[at : at + 2]
            else:
                scratch[into, :HID] = hidden_ref[r - 2, cols, :].astype(F32)[at : at + 2]
                scratch[into, HID : 2 * HID] = cell_ref[r - 2, cols, :][at : at + 2]
                scratch[into, 2 * HID :] = aux_ref[r - 2, cols, :].astype(F32)[at : at + 2]
        scratch[40:, :] = jnp.zeros((8, PACK), F32)
        out[...] = scratch[...].astype(BF16)


def sides_of(hidden, cell, aux, low, high):
    return pl.pallas_call(
        sides_kernel,
        out_shape=(jax.ShapeDtypeStruct((48, PACK), BF16),) * 2,
        in_specs=[VMEM] * 5,
        out_specs=(VMEM, VMEM),
        scratch_shapes=[pltpu.VMEM((48, PACK), F32)] * 2,
        compiler_params=PARAMS,
        cost_estimate=pl.CostEstimate(flops=0, bytes_accessed=1_000_000, transcendentals=0),
    )(hidden, cell, aux, low, high)


def placer(tap, first, cx):
    source = lax.broadcasted_iota(jnp.int32, (AUX, AUX), 0)
    target = lax.broadcasted_iota(jnp.int32, (AUX, AUX), 1)
    hit = (target - source == tap * cx - first) & (source >= first) & (source < first + cx)
    return jnp.where(hit, 1.0, 0.0).astype(BF16)


def put(ref, rows, lane, value):
    for i in range(value.shape[1] // 128):
        group = lane // 128 + i
        at = group % 5 * 128
        ref[group // 5, rows, at : at + 128] = value[:, i * 128 : (i + 1) * 128]


def prep_kernel(
    cx,
    hidden_ref,
    cell_ref,
    aux_ref,
    low_ref,
    high_ref,
    left_ref,
    right_ref,
    patches_out,
    frame_out,
    cell_out,
    keep_out,
    wide,
):
    wide[2:18, 8:40, :HID] = hidden_ref[...].astype(F32)
    wide[2:18, 8:40, HID:] = aux_ref[...].astype(F32)
    for ref, row in ((low_ref, 0), (high_ref, 18)):
        both = ref[...].astype(F32).reshape(2, 32, PACK)
        wide[row : row + 2, 8:40, :HID] = both[:, :, :HID]
        wide[row : row + 2, 8:40, HID:] = both[:, :, 2 * HID :]
    cell_out[:32, :] = low_ref[32:, HID : 2 * HID].astype(F32)
    cell_out[32:544, :] = cell_ref[...].reshape(512, HID)
    cell_out[544:576, :] = high_ref[:32, HID : 2 * HID].astype(F32)
    cell_out[576:, :] = jnp.zeros((48, HID), F32)
    for ref, col, near, base in ((left_ref, 6, 1, 575), (right_ref, 40, 0, 599)):
        rows = ref[...].astype(F32)
        for r in range(20):
            pair = rows[2 * r : 2 * r + 2]
            wide[r, col : col + 2, :HID] = pair[:, :HID]
            wide[r, col : col + 2, HID:] = pair[:, 2 * HID :]
            if 1 <= r < 19:
                cell_out[base + r : base + r + 1, :] = pair[near : near + 1, HID : 2 * HID]

    def border(b, a):
        pad = jnp.zeros((6, HID + AUX), F32)
        left = wide[a : a + 18, 6 + b, :]
        right = wide[a : a + 18, 39 + b, :]
        return jnp.concatenate([left, pad, right, pad], axis=0).astype(BF16)

    first = jnp.zeros((624, AUX), F32)
    second = jnp.zeros((512, AUX), F32)
    for b in range(3):
        cols = wide[:, 7 + b : 39 + b, :].astype(BF16)
        for a in range(3):
            t = 3 * a + b
            core = cols[a : a + 18].reshape(576, HID + AUX)
            edge = border(b, a)
            put(patches_out, slice(0, 576), t * HID, core[:, :HID])
            put(patches_out, slice(576, 624), t * HID, edge[:, :HID])
            aux = jnp.concatenate([core[:, HID:], edge[:, HID:]], axis=0)
            first = first + lax.dot_general(aux, placer(t, 0, cx), NN, preferred_element_type=F32)
            second = second + lax.dot_general(
                aux[32:544], placer(t, cx, cx), NN, preferred_element_type=F32
            )
            if t == 4:
                source = lax.broadcasted_iota(jnp.int32, (AUX, AUX), 0)
                copy = jnp.where(source == 2 * cx, 1.0, 0.0).astype(BF16)
                keep_out[...] = lax.dot_general(aux, copy, NN, preferred_element_type=F32)
    put(patches_out, slice(0, 624), 9 * HID, first.astype(BF16))
    put(patches_out, slice(0, 624), 9 * HID + AUX, jnp.zeros((624, AUX), BF16))
    frame_out[:, :AUX] = second.astype(BF16)
    frame_out[:, AUX:] = jnp.zeros((512, AUX), BF16)


def prepared(cx, hidden, cell, aux, low, high, left, right):
    return pl.pallas_call(
        functools.partial(prep_kernel, cx),
        out_shape=(
            jax.ShapeDtypeStruct((4, 624, CHUNK), BF16),
            jax.ShapeDtypeStruct((512, HID), BF16),
            jax.ShapeDtypeStruct((624, HID), F32),
            jax.ShapeDtypeStruct((624, 128), F32),
        ),
        in_specs=[VMEM] * 7,
        out_specs=(VMEM,) * 4,
        scratch_shapes=[pltpu.VMEM((20, 48, HID + AUX), F32)],
        compiler_params=PARAMS,
        cost_estimate=pl.CostEstimate(flops=0, bytes_accessed=100_000, transcendentals=0),
    )(hidden, cell, aux, low, high, left, right)


def chooser(half, shape, channel_axis):
    place = lax.broadcasted_iota(jnp.int32, shape, 1 - channel_axis)
    natural = lax.broadcasted_iota(jnp.int32, shape, channel_axis)
    y = lax.shift_right_logical(place, 5)
    zz = lax.shift_right_logical(place, 3) & 3
    wanted = zz * 64 + y * 16 + half * 8 + (place & 7)
    return jnp.where(natural == wanted, 1.0, 0.0).astype(BF16)


def parts_of(value):
    high = value.astype(BF16)
    rest = value - high.astype(F32)
    middle = rest.astype(BF16)
    return high, middle, (rest - middle.astype(F32)).astype(BF16)


def moved(value, choice):
    dots = [lax.dot_general(p, choice, NN, preferred_element_type=F32) for p in parts_of(value)]
    return dots[0] + (dots[1] + dots[2])


def product(patches, weight_ref, pair, x):
    rhs = jnp.concatenate(
        [
            weight_ref[y * 4 + x, q * 32 : (q + 1) * 32, :]
            for q in (2 * pair, 2 * pair + 1)
            for y in range(4)
        ],
        axis=0,
    )
    return lax.dot_general(patches, rhs, NT, preferred_element_type=F32)


def sigmoid(value):
    return 0.5 * jnp.tanh(0.5 * value) + 0.5


def updated(sums, bias, cell, keep):
    in_gate = sigmoid(sums[0][:, :128] + bias[0][None])
    decay_factor = sigmoid(sums[0][:, 128:] + bias[1][None])
    candidate = jnp.tanh(sums[1][:, :128] + bias[2][None])
    out_gate = sigmoid(sums[1][:, 128:] + bias[3][None])
    cell = decay_factor * cell + in_gate * candidate
    return (keep * out_gate * jnp.tanh(cell)).astype(BF16), cell


def gate_sums(patches_ref, weight_ref):
    sums = []
    for pair in range(2):
        value = None
        for x in range(4):
            part = product(patches_ref[x], weight_ref, pair, x)
            value = part if value is None else value + part
        sums.append(value)
    return sums


def first_half(i, half, patches_ref, weight_ref, bias_ref, cell_ref, keep_ref):
    sums = gate_sums(patches_ref, weight_ref)
    cell = moved(cell_ref[...], chooser(half, (HID, 128), 0))
    return updated(sums, bias_ref[i], cell, keep_ref[...])


def own_kernel(half_ref, *refs):
    *ins, hid_out, cell_out = refs
    hid_out[...], cell_out[...] = first_half(0, half_ref[0], *ins)


def own_half(halves, patches, weight, bias, cell, keep):
    count = patches.shape[1]
    return pl.pallas_call(
        own_kernel,
        out_shape=(
            jax.ShapeDtypeStruct((count, 128), BF16),
            jax.ShapeDtypeStruct((count, 128), F32),
        ),
        in_specs=[SMEM] + [VMEM] * 5,
        out_specs=(VMEM, VMEM),
        compiler_params=PARAMS,
        cost_estimate=pl.CostEstimate(
            flops=2 * count * KPAD * 512, bytes_accessed=6_000_000, transcendentals=count * 640
        ),
    )(halves, patches, weight, bias, cell, keep)


def final_kernel(
    half_ref,
    patches_ref,
    own_ref,
    other_ref,
    bias_ref,
    cell_ref,
    keep_ref,
    hid0_ref,
    cell0_ref,
    frame_ref,
    keep2_ref,
    proj_ref,
    hid_out,
    cell_out,
    flux_out,
    wide,
    patches,
):
    choices = [chooser(half_ref[i], (128, HID), 1) for i in range(2)]
    hid, cell = first_half(
        1, half_ref[1], patches_ref, other_ref, bias_ref, cell_ref, keep_ref
    )
    cells = (cell0_ref[32:544, :], cell[32:544])
    natural = lax.dot_general(
        hid0_ref[...], choices[0], NN, preferred_element_type=F32
    ) + lax.dot_general(hid, choices[1], NN, preferred_element_type=F32)

    wide[:, 8:40, :] = natural[:576].reshape(18, 32, HID)
    for row in range(18):
        wide[row, 7:8, :] = natural[576 + row : 577 + row]
        wide[row, 40:41, :] = natural[600 + row : 601 + row]
    for b in range(3):
        moved_rows = wide[:, 7 + b : 39 + b, :].astype(BF16)
        for a in range(3):
            put(patches, slice(0, 512), (3 * a + b) * HID, moved_rows[a : a + 16].reshape(512, HID))
    put(patches, slice(0, 512), 9 * HID, frame_ref[...])

    hid, cell = None, None
    for i, weight_ref in enumerate((own_ref, other_ref)):
        sums = gate_sums(patches, weight_ref)
        new_hid, new_cell = updated(sums, bias_ref[i], cells[i], keep_ref[32:544, :])
        one = lax.dot_general(new_hid, choices[i], NN, preferred_element_type=F32)
        two = moved(new_cell, choices[i])
        hid = one if hid is None else hid + one
        cell = two if cell is None else cell + two
    hid = hid.astype(BF16)
    hid_out[...] = hid
    cell_out[...] = cell
    flux = lax.dot_general(proj_ref[...], hid, NT, preferred_element_type=F32)
    for row in range(16):
        flux_out[row : row + 1, :] = flux[0:1, row * 32 : (row + 1) * 32] * keep2_ref[row : row + 1, :]


def finished(halves, *arrays):
    return pl.pallas_call(
        final_kernel,
        out_shape=(
            jax.ShapeDtypeStruct((512, HID), BF16),
            jax.ShapeDtypeStruct((512, HID), F32),
            jax.ShapeDtypeStruct((16, 32), F32),
        ),
        in_specs=[SMEM] + [VMEM] * len(arrays),
        out_specs=(VMEM, VMEM, VMEM),
        scratch_shapes=[pltpu.VMEM((18, 48, HID), F32), pltpu.VMEM((4, 512, CHUNK), BF16)],
        compiler_params=PARAMS,
        cost_estimate=pl.CostEstimate(
            flops=2 * 824 * KPAD * 1024, bytes_accessed=14_000_000, transcendentals=1136 * 1280
        ),
    )(halves, *arrays)


def compute(halves, own, swapped, prep, land_mask, bias2, proj):
    rows, cols = land_mask.shape
    patches1, frame2, cell1, keep1 = prep
    other = swapped(own)
    hid0, cell0 = own_half(halves, patches1, own, bias2, cell1, keep1)
    hidden, cell, flux = finished(
        halves, patches1, own, other, bias2, cell1, keep1,
        hid0, cell0, frame2, land_mask.astype(F32), proj,
    )
    return hidden.reshape(rows, cols, HID), cell.reshape(rows, cols, HID), flux


def bias_of(bias, c):
    by_half = jnp.transpose(bias.reshape(4, 4, 4, 2, 8), (3, 0, 2, 1, 4)).reshape(2, 4, 128)
    return jnp.where(c == 0, by_half, by_half[::-1])


def aux_of(frames, land_mask):
    rows, cols = land_mask.shape
    both = jnp.transpose(frames, (1, 2, 0, 3)).reshape(rows, cols, -1)
    aux = jnp.concatenate([both, land_mask.astype(BF16)[..., None]], axis=-1)
    return jnp.pad(aux, ((0, 0), (0, 0), (0, AUX - aux.shape[2])))


def body(frames, hidden_init, cell_init, conv_weight, bias, land_mask, projection):
    cx = frames.shape[3]
    x, c = lax.axis_index("x"), lax.axis_index("c")
    packed = pack_weights(conv_weight)
    unit = lax.dynamic_slice(packed, (c * 8, x * (KPAD // 4)), (8, KPAD // 4))
    by_z = spread(unit, "z").reshape(128, KPAD // 4)

    state = (hidden_init, cell_init, aux_of(frames, land_mask))
    last, first = ends_of(*state)
    low = shifted(last, ("x", "c"), 1)
    high = shifted(first, ("x", "c"), -1)
    last, first = sides_of(*state, low, high)
    halves = jnp.stack([c, 1 - c]).astype(jnp.int32)
    proj = jnp.broadcast_to(projection[None], (16, HID))
    bias2 = bias_of(bias, c)
    by_z, last, first, halves, proj, bias2 = lax.optimization_barrier(
        (by_z, last, first, halves, proj, bias2)
    )

    own = spread(by_z, ("y", "x"))
    own, last, first = lax.optimization_barrier((own, last, first))
    left = shifted(last, ("z", "y"), 1)
    right = shifted(first, ("z", "y"), -1)
    prep = prepared(cx, *state, low, high, left, right)
    swapped = lambda piece: turned(piece, "c", 1)
    return compute(halves, own, swapped, prep, land_mask, bias2, proj)


def solution(mesh):
    split = Mesh(mesh.devices.reshape(16, 4, 4, 2), ("z", "y", "x", "c"))
    sx, sy = ("z", "y"), ("x", "c")
    in_specs = (
        P(None, sy, sx, None),
        P(sy, sx, None),
        P(sy, sx, None),
        P(None, None, sx),
        P(),
        P(sy, sx),
        P(),
    )
    out_specs = (P(sy, sx, None), P(sy, sx, None), P(sy, sx))
    return jax.shard_map(body, mesh=split, in_specs=in_specs, out_specs=out_specs, check_vma=False)
```

```python
import functools

import jax
import jax.numpy as jnp
from jax import lax
from jax.experimental import pallas as pl
from jax.experimental.pallas import tpu as pltpu
from jax.sharding import Mesh, PartitionSpec as P

KPAD = 2560
CHUNK = KPAD // 4
HID = 256
AUX = 128
PACK = 2 * HID + AUX
F32 = jnp.float32
BF16 = jnp.bfloat16
NT = (((1,), (1,)), ((), ()))
NN = (((1,), (0,)), ((), ()))
VMEM = pl.BlockSpec(memory_space=pltpu.VMEM)
SMEM = pl.BlockSpec(memory_space=pltpu.SMEM)
PARAMS = pltpu.CompilerParams(vmem_limit_bytes=16 * 1024 * 1024)


def pack_weights(conv_weight):
    taps, cin, cols = conv_weight.shape
    cx = cin - HID
    flipped = jnp.transpose(conv_weight, (2, 0, 1))
    hidden = flipped[:, :, cx:].reshape(cols, taps * HID)
    frame = flipped[:, :, :cx].reshape(cols, taps * cx)
    packed = jnp.concatenate([hidden, frame], axis=1)
    return jnp.pad(packed, ((0, 0), (0, KPAD - packed.shape[1])))


def spread(block, axes):
    count = lax.axis_size(axes)
    copies = jnp.broadcast_to(block[None], (count,) + block.shape)
    return lax.all_to_all(copies, axes, 0, 0)


def turned(block, axis, step):
    count = lax.axis_size(axis)
    return lax.ppermute(block, axis, [(i, (i + step) % count) for i in range(count)])


def shifted(block, axes, step):
    count = lax.axis_size(axes)
    pairs = [(i, i + step) for i in range(count) if 0 <= i + step < count]
    return lax.ppermute(block, axes, pairs)


def ends_of(hidden, cell, frames, land_mask):
    pick = lambda array, axis: jnp.concatenate(
        [lax.slice_in_dim(array, 14, 16, axis=axis), lax.slice_in_dim(array, 0, 2, axis=axis)], axis
    )
    aux = aux_of(pick(frames, 1), pick(land_mask, 0))
    packed = jnp.concatenate([pick(hidden, 0), pick(cell, 0).astype(BF16), aux], axis=-1)
    packed = packed.reshape(128, PACK)
    return packed[:64], packed[64:]


def sides_kernel(hidden_ref, cell_ref, aux_ref, low_ref, high_ref, last_out, first_out, last, first):
    for out, scratch, start, at in ((last_out, last, 16, 14), (first_out, first, 0, 0)):
        cols = slice(start, start + 16)
        for r in range(20):
            into = slice(2 * r, 2 * r + 2)
            if r < 2 or r >= 18:
                ref, j = (low_ref, r) if r < 2 else (high_ref, r - 18)
                block = ref[j * 32 + start : j * 32 + start + 16, :].astype(F32)
                scratch[into, :] = block[at : at + 2]
            else:
                scratch[into, :HID] = hidden_ref[r - 2, cols, :].astype(F32)[at : at + 2]
                scratch[into, HID : 2 * HID] = cell_ref[r - 2, cols, :][at : at + 2]
                scratch[into, 2 * HID :] = aux_ref[r - 2, cols, :].astype(F32)[at : at + 2]
        scratch[40:, :] = jnp.zeros((8, PACK), F32)
        out[...] = scratch[...].astype(BF16)


def sides_of(hidden, cell, aux, low, high):
    return pl.pallas_call(
        sides_kernel,
        out_shape=(jax.ShapeDtypeStruct((48, PACK), BF16),) * 2,
        in_specs=[VMEM] * 5,
        out_specs=(VMEM, VMEM),
        scratch_shapes=[pltpu.VMEM((48, PACK), F32)] * 2,
        compiler_params=PARAMS,
        cost_estimate=pl.CostEstimate(flops=0, bytes_accessed=1_000_000, transcendentals=0),
    )(hidden, cell, aux, low, high)


def placer(tap, first, cx):
    source = lax.broadcasted_iota(jnp.int32, (AUX, AUX), 0)
    target = lax.broadcasted_iota(jnp.int32, (AUX, AUX), 1)
    hit = (target - source == tap * cx - first) & (source >= first) & (source < first + cx)
    return jnp.where(hit, 1.0, 0.0).astype(BF16)


def put(ref, rows, lane, value):
    for i in range(value.shape[1] // 128):
        group = lane // 128 + i
        at = group % 5 * 128
        ref[group // 5, rows, at : at + 128] = value[:, i * 128 : (i + 1) * 128]


def prep_kernel(
    cx,
    hidden_ref,
    cell_ref,
    aux_ref,
    low_ref,
    high_ref,
    left_ref,
    right_ref,
    patches_out,
    frame_out,
    cell_out,
    keep_out,
    wide,
):
    wide[2:18, 8:40, :HID] = hidden_ref[...].astype(F32)
    wide[2:18, 8:40, HID:] = aux_ref[...].astype(F32)
    for ref, row in ((low_ref, 0), (high_ref, 18)):
        both = ref[...].astype(F32).reshape(2, 32, PACK)
        wide[row : row + 2, 8:40, :HID] = both[:, :, :HID]
        wide[row : row + 2, 8:40, HID:] = both[:, :, 2 * HID :]
    cell_out[:32, :] = low_ref[32:, HID : 2 * HID].astype(F32)
    cell_out[32:544, :] = cell_ref[...].reshape(512, HID)
    cell_out[544:576, :] = high_ref[:32, HID : 2 * HID].astype(F32)
    cell_out[576:, :] = jnp.zeros((48, HID), F32)
    for ref, col, near, base in ((left_ref, 6, 1, 575), (right_ref, 40, 0, 599)):
        rows = ref[...].astype(F32)
        for r in range(20):
            pair = rows[2 * r : 2 * r + 2]
            wide[r, col : col + 2, :HID] = pair[:, :HID]
            wide[r, col : col + 2, HID:] = pair[:, 2 * HID :]
            if 1 <= r < 19:
                cell_out[base + r : base + r + 1, :] = pair[near : near + 1, HID : 2 * HID]

    def border(b, a):
        pad = jnp.zeros((6, HID + AUX), F32)
        left = wide[a : a + 18, 6 + b, :]
        right = wide[a : a + 18, 39 + b, :]
        return jnp.concatenate([left, pad, right, pad], axis=0).astype(BF16)

    first = jnp.zeros((624, AUX), F32)
    second = jnp.zeros((512, AUX), F32)
    for b in range(3):
        cols = wide[:, 7 + b : 39 + b, :].astype(BF16)
        for a in range(3):
            t = 3 * a + b
            core = cols[a : a + 18].reshape(576, HID + AUX)
            edge = border(b, a)
            put(patches_out, slice(0, 576), t * HID, core[:, :HID])
            put(patches_out, slice(576, 624), t * HID, edge[:, :HID])
            aux = jnp.concatenate([core[:, HID:], edge[:, HID:]], axis=0)
            first = first + lax.dot_general(aux, placer(t, 0, cx), NN, preferred_element_type=F32)
            second = second + lax.dot_general(
                aux[32:544], placer(t, cx, cx), NN, preferred_element_type=F32
            )
            if t == 4:
                source = lax.broadcasted_iota(jnp.int32, (AUX, AUX), 0)
                copy = jnp.where(source == 2 * cx, 1.0, 0.0).astype(BF16)
                keep_out[...] = lax.dot_general(aux, copy, NN, preferred_element_type=F32)
    put(patches_out, slice(0, 624), 9 * HID, first.astype(BF16))
    put(patches_out, slice(0, 624), 9 * HID + AUX, jnp.zeros((624, AUX), BF16))
    frame_out[:, :AUX] = second.astype(BF16)
    frame_out[:, AUX:] = jnp.zeros((512, AUX), BF16)


def prepared(cx, hidden, cell, aux, low, high, left, right):
    return pl.pallas_call(
        functools.partial(prep_kernel, cx),
        out_shape=(
            jax.ShapeDtypeStruct((4, 624, CHUNK), BF16),
            jax.ShapeDtypeStruct((512, HID), BF16),
            jax.ShapeDtypeStruct((624, HID), F32),
            jax.ShapeDtypeStruct((624, 128), F32),
        ),
        in_specs=[VMEM] * 7,
        out_specs=(VMEM,) * 4,
        scratch_shapes=[pltpu.VMEM((20, 48, HID + AUX), F32)],
        compiler_params=PARAMS,
        cost_estimate=pl.CostEstimate(flops=0, bytes_accessed=100_000, transcendentals=0),
    )(hidden, cell, aux, low, high, left, right)


def chooser(half, shape, channel_axis):
    place = lax.broadcasted_iota(jnp.int32, shape, 1 - channel_axis)
    natural = lax.broadcasted_iota(jnp.int32, shape, channel_axis)
    y = lax.shift_right_logical(place, 5)
    zz = lax.shift_right_logical(place, 3) & 3
    wanted = zz * 64 + y * 16 + half * 8 + (place & 7)
    return jnp.where(natural == wanted, 1.0, 0.0).astype(BF16)


def parts_of(value):
    high = value.astype(BF16)
    rest = value - high.astype(F32)
    middle = rest.astype(BF16)
    return high, middle, (rest - middle.astype(F32)).astype(BF16)


def moved(value, choice):
    dots = [lax.dot_general(p, choice, NN, preferred_element_type=F32) for p in parts_of(value)]
    return dots[0] + (dots[1] + dots[2])


def product(patches, weight_ref, pair, x):
    rhs = jnp.concatenate(
        [
            weight_ref[y * 4 + x, q * 32 : (q + 1) * 32, :]
            for q in (2 * pair, 2 * pair + 1)
            for y in range(4)
        ],
        axis=0,
    )
    return lax.dot_general(patches, rhs, NT, preferred_element_type=F32)


def sigmoid(value):
    return 0.5 * jnp.tanh(0.5 * value) + 0.5


def updated(sums, bias, cell, keep):
    in_gate = sigmoid(sums[0][:, :128] + bias[0][None])
    decay_factor = sigmoid(sums[0][:, 128:] + bias[1][None])
    candidate = jnp.tanh(sums[1][:, :128] + bias[2][None])
    out_gate = sigmoid(sums[1][:, 128:] + bias[3][None])
    cell = decay_factor * cell + in_gate * candidate
    return (keep * out_gate * jnp.tanh(cell)).astype(BF16), cell


def gate_sums(patches_ref, weight_ref):
    sums = []
    for pair in range(2):
        value = None
        for x in range(4):
            part = product(patches_ref[x], weight_ref, pair, x)
            value = part if value is None else value + part
        sums.append(value)
    return sums


def first_half(i, half, patches_ref, weight_ref, bias_ref, cell_ref, keep_ref):
    sums = gate_sums(patches_ref, weight_ref)
    cell = moved(cell_ref[...], chooser(half, (HID, 128), 0))
    return updated(sums, bias_ref[i], cell, keep_ref[...])


def own_kernel(half_ref, *refs):
    *ins, hid_out, cell_out = refs
    hid_out[...], cell_out[...] = first_half(0, half_ref[0], *ins)


def own_half(halves, patches, weight, bias, cell, keep):
    count = patches.shape[1]
    return pl.pallas_call(
        own_kernel,
        out_shape=(
            jax.ShapeDtypeStruct((count, 128), BF16),
            jax.ShapeDtypeStruct((count, 128), F32),
        ),
        in_specs=[SMEM] + [VMEM] * 5,
        out_specs=(VMEM, VMEM),
        compiler_params=PARAMS,
        cost_estimate=pl.CostEstimate(
            flops=2 * count * KPAD * 512, bytes_accessed=6_000_000, transcendentals=count * 640
        ),
    )(halves, patches, weight, bias, cell, keep)


def final_kernel(
    half_ref,
    patches_ref,
    own_ref,
    other_ref,
    bias_ref,
    cell_ref,
    keep_ref,
    hid0_ref,
    cell0_ref,
    frame_ref,
    keep2_ref,
    proj_ref,
    hid_out,
    cell_out,
    flux_out,
    wide,
    patches,
):
    choices = [chooser(half_ref[i], (128, HID), 1) for i in range(2)]
    hid, cell = first_half(
        1, half_ref[1], patches_ref, other_ref, bias_ref, cell_ref, keep_ref
    )
    cells = (cell0_ref[32:544, :], cell[32:544])
    natural = lax.dot_general(
        hid0_ref[...], choices[0], NN, preferred_element_type=F32
    ) + lax.dot_general(hid, choices[1], NN, preferred_element_type=F32)

    wide[:, 8:40, :] = natural[:576].reshape(18, 32, HID)
    for row in range(18):
        wide[row, 7:8, :] = natural[576 + row : 577 + row]
        wide[row, 40:41, :] = natural[600 + row : 601 + row]
    for b in range(3):
        moved_rows = wide[:, 7 + b : 39 + b, :].astype(BF16)
        for a in range(3):
            put(patches, slice(0, 512), (3 * a + b) * HID, moved_rows[a : a + 16].reshape(512, HID))
    put(patches, slice(0, 512), 9 * HID, frame_ref[...])

    hid, cell = None, None
    for i, weight_ref in enumerate((own_ref, other_ref)):
        sums = gate_sums(patches, weight_ref)
        new_hid, new_cell = updated(sums, bias_ref[i], cells[i], keep_ref[32:544, :])
        one = lax.dot_general(new_hid, choices[i], NN, preferred_element_type=F32)
        two = moved(new_cell, choices[i])
        hid = one if hid is None else hid + one
        cell = two if cell is None else cell + two
    hid = hid.astype(BF16)
    hid_out[...] = hid
    cell_out[...] = cell
    flux = lax.dot_general(proj_ref[...], hid, NT, preferred_element_type=F32)
    for row in range(16):
        flux_out[row : row + 1, :] = flux[0:1, row * 32 : (row + 1) * 32] * keep2_ref[row : row + 1, :]


def finished(halves, *arrays):
    return pl.pallas_call(
        final_kernel,
        out_shape=(
            jax.ShapeDtypeStruct((512, HID), BF16),
            jax.ShapeDtypeStruct((512, HID), F32),
            jax.ShapeDtypeStruct((16, 32), F32),
        ),
        in_specs=[SMEM] + [VMEM] * len(arrays),
        out_specs=(VMEM, VMEM, VMEM),
        scratch_shapes=[pltpu.VMEM((18, 48, HID), F32), pltpu.VMEM((4, 512, CHUNK), BF16)],
        compiler_params=PARAMS,
        cost_estimate=pl.CostEstimate(
            flops=2 * 824 * KPAD * 1024, bytes_accessed=14_000_000, transcendentals=1136 * 1280
        ),
    )(halves, *arrays)


def compute(halves, own, swapped, prep, land_mask, bias2, proj):
    rows, cols = land_mask.shape
    patches1, frame2, cell1, keep1 = prep
    other = swapped(own)
    hid0, cell0 = own_half(halves, patches1, own, bias2, cell1, keep1)
    hidden, cell, flux = finished(
        halves, patches1, own, other, bias2, cell1, keep1,
        hid0, cell0, frame2, land_mask.astype(F32), proj,
    )
    return hidden.reshape(rows, cols, HID), cell.reshape(rows, cols, HID), flux


def bias_of(bias, c):
    by_half = jnp.transpose(bias.reshape(4, 4, 4, 2, 8), (3, 0, 2, 1, 4)).reshape(2, 4, 128)
    return jnp.where(c == 0, by_half, by_half[::-1])


def aux_of(frames, land_mask):
    rows, cols = land_mask.shape
    both = jnp.transpose(frames, (1, 2, 0, 3)).reshape(rows, cols, -1)
    aux = jnp.concatenate([both, land_mask.astype(BF16)[..., None]], axis=-1)
    return jnp.pad(aux, ((0, 0), (0, 0), (0, AUX - aux.shape[2])))


def body(frames, hidden_init, cell_init, conv_weight, bias, land_mask, projection):
    cx = frames.shape[3]
    x, c = lax.axis_index("x"), lax.axis_index("c")
    last, first = ends_of(hidden_init, cell_init, frames, land_mask)
    low = shifted(last, ("x", "c"), 1)
    high = shifted(first, ("x", "c"), -1)
    packed = pack_weights(conv_weight)
    unit = lax.dynamic_slice(packed, (c * 8, x * CHUNK), (8, CHUNK))
    unit, low, high = lax.optimization_barrier((unit, low, high))
    by_z = spread(unit, "z").reshape(128, CHUNK)

    state = (hidden_init, cell_init, aux_of(frames, land_mask))
    last, first = sides_of(*state, low, high)
    left = shifted(last, ("z", "y"), 1)
    right = shifted(first, ("z", "y"), -1)
    prep = prepared(cx, *state, low, high, left, right)
    halves = jnp.stack([c, 1 - c]).astype(jnp.int32)
    proj = jnp.broadcast_to(projection[None], (16, HID))
    bias2 = bias_of(bias, c)
    by_z, prep, halves, proj, bias2 = lax.optimization_barrier((by_z, prep, halves, proj, bias2))

    own = spread(by_z, ("y", "x"))
    swapped = lambda piece: turned(piece, "c", 1)
    return compute(halves, own, swapped, prep, land_mask, bias2, proj)


def solution(mesh):
    split = Mesh(mesh.devices.reshape(16, 4, 4, 2), ("z", "y", "x", "c"))
    sx, sy = ("z", "y"), ("x", "c")
    in_specs = (
        P(None, sy, sx, None),
        P(sy, sx, None),
        P(sy, sx, None),
        P(None, None, sx),
        P(),
        P(sy, sx),
        P(),
    )
    out_specs = (P(sy, sx, None), P(sy, sx, None), P(sy, sx))
    return jax.shard_map(body, mesh=split, in_specs=in_specs, out_specs=out_specs, check_vma=False)
```

```python
import functools

import jax
import jax.numpy as jnp
from jax import lax
from jax.experimental import pallas as pl
from jax.experimental.pallas import tpu as pltpu
from jax.sharding import Mesh, PartitionSpec as P

KPAD = 2560
CHUNK = KPAD // 4
HID = 256
AUX = 128
PACK = 2 * HID + AUX
F32 = jnp.float32
BF16 = jnp.bfloat16
NT = (((1,), (1,)), ((), ()))
NN = (((1,), (0,)), ((), ()))
VMEM = pl.BlockSpec(memory_space=pltpu.VMEM)
SMEM = pl.BlockSpec(memory_space=pltpu.SMEM)
PARAMS = pltpu.CompilerParams(vmem_limit_bytes=16 * 1024 * 1024)


def pack_weights(conv_weight):
    taps, cin, cols = conv_weight.shape
    cx = cin - HID
    flipped = jnp.transpose(conv_weight, (2, 0, 1))
    hidden = flipped[:, :, cx:].reshape(cols, taps * HID)
    frame = flipped[:, :, :cx].reshape(cols, taps * cx)
    packed = jnp.concatenate([hidden, frame], axis=1)
    return jnp.pad(packed, ((0, 0), (0, KPAD - packed.shape[1])))


def spread(block, axes):
    count = lax.axis_size(axes)
    copies = jnp.broadcast_to(block[None], (count,) + block.shape)
    return lax.all_to_all(copies, axes, 0, 0)


def turned(block, axis, step):
    count = lax.axis_size(axis)
    return lax.ppermute(block, axis, [(i, (i + step) % count) for i in range(count)])


def shifted(block, axes, step):
    count = lax.axis_size(axes)
    pairs = [(i, i + step) for i in range(count) if 0 <= i + step < count]
    return lax.ppermute(block, axes, pairs)


def ends_kernel(hidden_ref, cell_ref, aux_ref, last_out, first_out):
    for out, start in ((last_out, 14), (first_out, 0)):
        for j in range(2):
            rows = slice(j * 32, (j + 1) * 32)
            out[rows, :HID] = hidden_ref[start + j]
            out[rows, HID : 2 * HID] = cell_ref[start + j].astype(BF16)
            out[rows, 2 * HID :] = aux_ref[start + j]


def ends_of(hidden, cell, aux):
    return pl.pallas_call(
        ends_kernel,
        out_shape=(jax.ShapeDtypeStruct((64, PACK), BF16),) * 2,
        in_specs=[VMEM] * 3,
        out_specs=(VMEM, VMEM),
        compiler_params=PARAMS,
        cost_estimate=pl.CostEstimate(flops=0, bytes_accessed=1_000_000, transcendentals=0),
    )(hidden, cell, aux)


def sides_kernel(hidden_ref, cell_ref, aux_ref, low_ref, high_ref, last_out, first_out, last, first):
    for out, scratch, start, at in ((last_out, last, 16, 14), (first_out, first, 0, 0)):
        cols = slice(start, start + 16)
        for r in range(20):
            into = slice(2 * r, 2 * r + 2)
            if r < 2 or r >= 18:
                ref, j = (low_ref, r) if r < 2 else (high_ref, r - 18)
                block = ref[j * 32 + start : j * 32 + start + 16, :].astype(F32)
                scratch[into, :] = block[at : at + 2]
            else:
                scratch[into, :HID] = hidden_ref[r - 2, cols, :].astype(F32)[at : at + 2]
                scratch[into, HID : 2 * HID] = cell_ref[r - 2, cols, :][at : at + 2]
                scratch[into, 2 * HID :] = aux_ref[r - 2, cols, :].astype(F32)[at : at + 2]
        scratch[40:, :] = jnp.zeros((8, PACK), F32)
        out[...] = scratch[...].astype(BF16)


def sides_of(hidden, cell, aux, low, high):
    return pl.pallas_call(
        sides_kernel,
        out_shape=(jax.ShapeDtypeStruct((48, PACK), BF16),) * 2,
        in_specs=[VMEM] * 5,
        out_specs=(VMEM, VMEM),
        scratch_shapes=[pltpu.VMEM((48, PACK), F32)] * 2,
        compiler_params=PARAMS,
        cost_estimate=pl.CostEstimate(flops=0, bytes_accessed=1_000_000, transcendentals=0),
    )(hidden, cell, aux, low, high)


def placer(tap, first, cx):
    source = lax.broadcasted_iota(jnp.int32, (AUX, AUX), 0)
    target = lax.broadcasted_iota(jnp.int32, (AUX, AUX), 1)
    hit = (target - source == tap * cx - first) & (source >= first) & (source < first + cx)
    return jnp.where(hit, 1.0, 0.0).astype(BF16)


def prep_kernel(
    cx,
    hidden_ref,
    cell_ref,
    aux_ref,
    low_ref,
    high_ref,
    left_ref,
    right_ref,
    patches_out,
    frame_out,
    cell_out,
    keep_out,
    wide,
):
    wide[2:18, 8:40, :HID] = hidden_ref[...].astype(F32)
    wide[2:18, 8:40, HID:] = aux_ref[...].astype(F32)
    for ref, row in ((low_ref, 0), (high_ref, 18)):
        both = ref[...].astype(F32).reshape(2, 32, PACK)
        wide[row : row + 2, 8:40, :HID] = both[:, :, :HID]
        wide[row : row + 2, 8:40, HID:] = both[:, :, 2 * HID :]
    cell_out[:32, :] = low_ref[32:, HID : 2 * HID].astype(F32)
    cell_out[32:544, :] = cell_ref[...].reshape(512, HID)
    cell_out[544:576, :] = high_ref[:32, HID : 2 * HID].astype(F32)
    cell_out[576:, :] = jnp.zeros((48, HID), F32)
    for ref, col, near, base in ((left_ref, 6, 1, 575), (right_ref, 40, 0, 599)):
        rows = ref[...].astype(F32)
        for r in range(20):
            pair = rows[2 * r : 2 * r + 2]
            wide[r, col : col + 2, :HID] = pair[:, :HID]
            wide[r, col : col + 2, HID:] = pair[:, 2 * HID :]
            if 1 <= r < 19:
                cell_out[base + r : base + r + 1, :] = pair[near : near + 1, HID : 2 * HID]

    def border(b, a):
        pad = jnp.zeros((6, HID + AUX), F32)
        left = wide[a : a + 18, 6 + b, :]
        right = wide[a : a + 18, 39 + b, :]
        return jnp.concatenate([left, pad, right, pad], axis=0).astype(BF16)

    first = jnp.zeros((624, AUX), F32)
    second = jnp.zeros((512, AUX), F32)
    for b in range(3):
        cols = wide[:, 7 + b : 39 + b, :].astype(BF16)
        for a in range(3):
            t = 3 * a + b
            core = cols[a : a + 18].reshape(576, HID + AUX)
            edge = border(b, a)
            patches_out[:576, t * HID : (t + 1) * HID] = core[:, :HID]
            patches_out[576:, t * HID : (t + 1) * HID] = edge[:, :HID]
            aux = jnp.concatenate([core[:, HID:], edge[:, HID:]], axis=0)
            first = first + lax.dot_general(aux, placer(t, 0, cx), NN, preferred_element_type=F32)
            second = second + lax.dot_general(
                aux[32:544], placer(t, cx, cx), NN, preferred_element_type=F32
            )
            if t == 4:
                source = lax.broadcasted_iota(jnp.int32, (AUX, AUX), 0)
                copy = jnp.where(source == 2 * cx, 1.0, 0.0).astype(BF16)
                keep_out[...] = lax.dot_general(aux, copy, NN, preferred_element_type=F32)
    patches_out[:, 9 * HID : 9 * HID + AUX] = first.astype(BF16)
    patches_out[:, 9 * HID + AUX :] = jnp.zeros((624, AUX), BF16)
    frame_out[:, :AUX] = second.astype(BF16)
    frame_out[:, AUX:] = jnp.zeros((512, AUX), BF16)


def prepared(cx, hidden, cell, aux, low, high, left, right):
    return pl.pallas_call(
        functools.partial(prep_kernel, cx),
        out_shape=(
            jax.ShapeDtypeStruct((624, KPAD), BF16),
            jax.ShapeDtypeStruct((512, HID), BF16),
            jax.ShapeDtypeStruct((624, HID), F32),
            jax.ShapeDtypeStruct((624, 128), F32),
        ),
        in_specs=[VMEM] * 7,
        out_specs=(VMEM,) * 4,
        scratch_shapes=[pltpu.VMEM((20, 48, HID + AUX), F32)],
        compiler_params=PARAMS,
        cost_estimate=pl.CostEstimate(flops=0, bytes_accessed=100_000, transcendentals=0),
    )(hidden, cell, aux, low, high, left, right)


def chooser(half, shape, channel_axis):
    place = lax.broadcasted_iota(jnp.int32, shape, 1 - channel_axis)
    natural = lax.broadcasted_iota(jnp.int32, shape, channel_axis)
    y = lax.shift_right_logical(place, 5)
    zz = lax.shift_right_logical(place, 3) & 3
    wanted = zz * 64 + y * 16 + half * 8 + (place & 7)
    return jnp.where(natural == wanted, 1.0, 0.0).astype(BF16)


def parts_of(value):
    high = value.astype(BF16)
    rest = value - high.astype(F32)
    middle = rest.astype(BF16)
    return high, middle, (rest - middle.astype(F32)).astype(BF16)


def moved(values, choices):
    lhs = jnp.concatenate([part for value in values for part in parts_of(value)], axis=1)
    rhs = jnp.concatenate([choice for choice in choices for _ in range(3)], axis=0)
    return lax.dot_general(lhs, rhs, NN, preferred_element_type=F32)


def joined(values, choices):
    lhs, rhs = jnp.concatenate(values, axis=1), jnp.concatenate(choices, axis=0)
    return lax.dot_general(lhs, rhs, NN, preferred_element_type=F32)


def sigmoid(value):
    return 0.5 * jnp.tanh(0.5 * value) + 0.5


def updated(sums, bias, cell, keep):
    in_gate = sigmoid(sums[0][:, :128] + bias[0][None])
    decay_factor = sigmoid(sums[0][:, 128:] + bias[1][None])
    candidate = jnp.tanh(sums[1][:, :128] + bias[2][None])
    out_gate = sigmoid(sums[1][:, 128:] + bias[3][None])
    cell = decay_factor * cell + in_gate * candidate
    return (keep * out_gate * jnp.tanh(cell)).astype(BF16), cell


def gate_sums(patches, weight_ref):
    sums = []
    for pair in range(2):
        rhs = jnp.concatenate(
            [
                jnp.concatenate(
                    [
                        weight_ref[y * 4 + x, q * 32 : (q + 1) * 32, :]
                        for q in (2 * pair, 2 * pair + 1)
                        for y in range(4)
                    ],
                    axis=0,
                )
                for x in range(4)
            ],
            axis=1,
        )
        sums.append(lax.dot_general(patches, rhs, NT, preferred_element_type=F32))
    return sums


def first_half(i, half, patches_ref, weight_ref, bias_ref, cell_ref, keep_ref):
    sums = gate_sums(patches_ref[...], weight_ref)
    cell = moved([cell_ref[...]], [chooser(half, (HID, 128), 0)])
    return updated(sums, bias_ref[i], cell, keep_ref[...])


def own_kernel(half_ref, *refs):
    *ins, hid_out, cell_out = refs
    hid_out[...], cell_out[...] = first_half(0, half_ref[0], *ins)


def own_half(halves, patches, weight, bias, cell, keep):
    count = patches.shape[0]
    return pl.pallas_call(
        own_kernel,
        out_shape=(
            jax.ShapeDtypeStruct((count, 128), BF16),
            jax.ShapeDtypeStruct((count, 128), F32),
        ),
        in_specs=[SMEM] + [VMEM] * 5,
        out_specs=(VMEM, VMEM),
        compiler_params=PARAMS,
        cost_estimate=pl.CostEstimate(
            flops=2 * count * KPAD * 512, bytes_accessed=6_000_000, transcendentals=count * 640
        ),
    )(halves, patches, weight, bias, cell, keep)


def final_kernel(
    half_ref,
    patches_ref,
    own_ref,
    other_ref,
    bias_ref,
    cell_ref,
    keep_ref,
    hid0_ref,
    cell0_ref,
    frame_ref,
    keep2_ref,
    proj_ref,
    hid_out,
    cell_out,
    flux_out,
    wide,
    patches,
):
    choices = [chooser(half_ref[i], (128, HID), 1) for i in range(2)]
    hid, cell = first_half(
        1, half_ref[1], patches_ref, other_ref, bias_ref, cell_ref, keep_ref
    )
    cells = (cell0_ref[32:544, :], cell[32:544])
    natural = joined([hid0_ref[...], hid], choices)

    wide[:, 8:40, :] = natural[:576].reshape(18, 32, HID)
    for row in range(18):
        wide[row, 7:8, :] = natural[576 + row : 577 + row]
        wide[row, 40:41, :] = natural[600 + row : 601 + row]
    for b in range(3):
        moved_rows = wide[:, 7 + b : 39 + b, :].astype(BF16)
        for a in range(3):
            t = 3 * a + b
            patches[:, t * HID : (t + 1) * HID] = moved_rows[a : a + 16].reshape(512, HID)
    patches[:, 9 * HID :] = frame_ref[...]

    new_hids, new_cells = [], []
    for i, weight_ref in enumerate((own_ref, other_ref)):
        sums = gate_sums(patches[...], weight_ref)
        new_hid, new_cell = updated(sums, bias_ref[i], cells[i], keep_ref[32:544, :])
        new_hids.append(new_hid)
        new_cells.append(new_cell)
    hid = joined(new_hids, choices).astype(BF16)
    cell = moved(new_cells, choices)
    hid_out[...] = hid
    cell_out[...] = cell
    flux = lax.dot_general(proj_ref[...], hid, NT, preferred_element_type=F32)
    for row in range(16):
        flux_out[row : row + 1, :] = flux[0:1, row * 32 : (row + 1) * 32] * keep2_ref[row : row + 1, :]


def finished(halves, *arrays):
    return pl.pallas_call(
        final_kernel,
        out_shape=(
            jax.ShapeDtypeStruct((512, HID), BF16),
            jax.ShapeDtypeStruct((512, HID), F32),
            jax.ShapeDtypeStruct((16, 32), F32),
        ),
        in_specs=[SMEM] + [VMEM] * len(arrays),
        out_specs=(VMEM, VMEM, VMEM),
        scratch_shapes=[pltpu.VMEM((18, 48, HID), F32), pltpu.VMEM((512, KPAD), BF16)],
        compiler_params=PARAMS,
        cost_estimate=pl.CostEstimate(
            flops=2 * 824 * KPAD * 1024, bytes_accessed=14_000_000, transcendentals=1136 * 1280
        ),
    )(halves, *arrays)


def compute(halves, own, swapped, prep, land_mask, bias2, proj):
    rows, cols = land_mask.shape
    patches1, frame2, cell1, keep1 = prep
    other = swapped(own)
    hid0, cell0 = own_half(halves, patches1, own, bias2, cell1, keep1)
    hidden, cell, flux = finished(
        halves, patches1, own, other, bias2, cell1, keep1,
        hid0, cell0, frame2, land_mask.astype(F32), proj,
    )
    return hidden.reshape(rows, cols, HID), cell.reshape(rows, cols, HID), flux


def bias_of(bias, c):
    by_half = jnp.transpose(bias.reshape(4, 4, 4, 2, 8), (3, 0, 2, 1, 4)).reshape(2, 4, 128)
    return jnp.where(c == 0, by_half, by_half[::-1])


def aux_of(frames, land_mask):
    rows, cols = land_mask.shape
    both = jnp.transpose(frames, (1, 2, 0, 3)).reshape(rows, cols, -1)
    aux = jnp.concatenate([both, land_mask.astype(BF16)[..., None]], axis=-1)
    return jnp.pad(aux, ((0, 0), (0, 0), (0, AUX - aux.shape[2])))


def body(frames, hidden_init, cell_init, conv_weight, bias, land_mask, projection):
    cx = frames.shape[3]
    x, c = lax.axis_index("x"), lax.axis_index("c")
    packed = pack_weights(conv_weight)
    unit = lax.dynamic_slice(packed, (c * 8, x * (KPAD // 4)), (8, KPAD // 4))
    by_z = spread(unit, "z").reshape(128, KPAD // 4)

    state = (hidden_init, cell_init, aux_of(frames, land_mask))
    last, first = ends_of(*state)
    low = shifted(last, ("x", "c"), 1)
    high = shifted(first, ("x", "c"), -1)
    last, first = sides_of(*state, low, high)
    halves = jnp.stack([c, 1 - c]).astype(jnp.int32)
    proj = jnp.broadcast_to(projection[None], (16, HID))
    bias2 = bias_of(bias, c)
    by_z, last, first, halves, proj, bias2 = lax.optimization_barrier(
        (by_z, last, first, halves, proj, bias2)
    )

    own = spread(by_z, ("y", "x"))
    left = shifted(last, ("z", "y"), 1)
    right = shifted(first, ("z", "y"), -1)
    own, left, right = lax.optimization_barrier((own, left, right))
    prep = prepared(cx, *state, low, high, left, right)
    swapped = lambda piece: turned(piece, "c", 1)
    return compute(halves, own, swapped, prep, land_mask, bias2, proj)


def solution(mesh):
    split = Mesh(mesh.devices.reshape(16, 4, 4, 2), ("z", "y", "x", "c"))
    sx, sy = ("z", "y"), ("x", "c")
    in_specs = (
        P(None, sy, sx, None),
        P(sy, sx, None),
        P(sy, sx, None),
        P(None, None, sx),
        P(),
        P(sy, sx),
        P(),
    )
    out_specs = (P(sy, sx, None), P(sy, sx, None), P(sy, sx))
    return jax.shard_map(body, mesh=split, in_specs=in_specs, out_specs=out_specs, check_vma=False)
```

```python
import functools

import jax
import jax.numpy as jnp
from jax import lax
from jax.experimental import pallas as pl
from jax.experimental.pallas import tpu as pltpu
from jax.sharding import Mesh, PartitionSpec as P

KPAD = 2560
CHUNK = KPAD // 4
HID = 256
AUX = 128
PACK = 2 * HID + AUX
F32 = jnp.float32
BF16 = jnp.bfloat16
NT = (((1,), (1,)), ((), ()))
NN = (((1,), (0,)), ((), ()))
VMEM = pl.BlockSpec(memory_space=pltpu.VMEM)
SMEM = pl.BlockSpec(memory_space=pltpu.SMEM)
PARAMS = pltpu.CompilerParams(vmem_limit_bytes=16 * 1024 * 1024)


def pack_weights(conv_weight):
    taps, cin, cols = conv_weight.shape
    cx = cin - HID
    flipped = jnp.transpose(conv_weight, (2, 0, 1))
    hidden = flipped[:, :, cx:].reshape(cols, taps * HID)
    frame = flipped[:, :, :cx].reshape(cols, taps * cx)
    packed = jnp.concatenate([hidden, frame], axis=1)
    return jnp.pad(packed, ((0, 0), (0, KPAD - packed.shape[1])))


def spread(block, axes):
    count = lax.axis_size(axes)
    copies = jnp.broadcast_to(block[None], (count,) + block.shape)
    return lax.all_to_all(copies, axes, 0, 0)


def turned(block, axis, step):
    count = lax.axis_size(axis)
    return lax.ppermute(block, axis, [(i, (i + step) % count) for i in range(count)])


def shifted(block, axes, step):
    count = lax.axis_size(axes)
    pairs = [(i, i + step) for i in range(count) if 0 <= i + step < count]
    return lax.ppermute(block, axes, pairs)


def ends_kernel(hidden_ref, cell_ref, aux_ref, last_out, first_out):
    for out, start in ((last_out, 14), (first_out, 0)):
        for j in range(2):
            rows = slice(j * 32, (j + 1) * 32)
            out[rows, :HID] = hidden_ref[start + j]
            out[rows, HID : 2 * HID] = cell_ref[start + j].astype(BF16)
            out[rows, 2 * HID :] = aux_ref[start + j]


def ends_of(hidden, cell, aux):
    return pl.pallas_call(
        ends_kernel,
        out_shape=(jax.ShapeDtypeStruct((64, PACK), BF16),) * 2,
        in_specs=[VMEM] * 3,
        out_specs=(VMEM, VMEM),
        compiler_params=PARAMS,
        cost_estimate=pl.CostEstimate(flops=0, bytes_accessed=1_000_000, transcendentals=0),
    )(hidden, cell, aux)


def sides_kernel(hidden_ref, cell_ref, aux_ref, low_ref, high_ref, last_out, first_out, last, first):
    for out, scratch, start, at in ((last_out, last, 16, 14), (first_out, first, 0, 0)):
        cols = slice(start, start + 16)
        for r in range(20):
            into = slice(2 * r, 2 * r + 2)
            if r < 2 or r >= 18:
                ref, j = (low_ref, r) if r < 2 else (high_ref, r - 18)
                block = ref[j * 32 + start : j * 32 + start + 16, :].astype(F32)
                scratch[into, :] = block[at : at + 2]
            else:
                scratch[into, :HID] = hidden_ref[r - 2, cols, :].astype(F32)[at : at + 2]
                scratch[into, HID : 2 * HID] = cell_ref[r - 2, cols, :][at : at + 2]
                scratch[into, 2 * HID :] = aux_ref[r - 2, cols, :].astype(F32)[at : at + 2]
        scratch[40:, :] = jnp.zeros((8, PACK), F32)
        out[...] = scratch[...].astype(BF16)


def sides_of(hidden, cell, aux, low, high):
    return pl.pallas_call(
        sides_kernel,
        out_shape=(jax.ShapeDtypeStruct((48, PACK), BF16),) * 2,
        in_specs=[VMEM] * 5,
        out_specs=(VMEM, VMEM),
        scratch_shapes=[pltpu.VMEM((48, PACK), F32)] * 2,
        compiler_params=PARAMS,
        cost_estimate=pl.CostEstimate(flops=0, bytes_accessed=1_000_000, transcendentals=0),
    )(hidden, cell, aux, low, high)


def placer(tap, first, cx):
    source = lax.broadcasted_iota(jnp.int32, (AUX, AUX), 0)
    target = lax.broadcasted_iota(jnp.int32, (AUX, AUX), 1)
    hit = (target - source == tap * cx - first) & (source >= first) & (source < first + cx)
    return jnp.where(hit, 1.0, 0.0).astype(BF16)


def prep_kernel(
    cx,
    hidden_ref,
    cell_ref,
    aux_ref,
    low_ref,
    high_ref,
    left_ref,
    right_ref,
    patches_out,
    frame_out,
    cell_out,
    keep_out,
    wide,
):
    wide[2:18, 8:40, :HID] = hidden_ref[...].astype(F32)
    wide[2:18, 8:40, HID:] = aux_ref[...].astype(F32)
    for ref, row in ((low_ref, 0), (high_ref, 18)):
        both = ref[...].astype(F32).reshape(2, 32, PACK)
        wide[row : row + 2, 8:40, :HID] = both[:, :, :HID]
        wide[row : row + 2, 8:40, HID:] = both[:, :, 2 * HID :]
    cell_out[:32, :] = low_ref[32:, HID : 2 * HID].astype(F32)
    cell_out[32:544, :] = cell_ref[...].reshape(512, HID)
    cell_out[544:576, :] = high_ref[:32, HID : 2 * HID].astype(F32)
    cell_out[576:, :] = jnp.zeros((48, HID), F32)
    for ref, col, near, base in ((left_ref, 6, 1, 575), (right_ref, 40, 0, 599)):
        rows = ref[...].astype(F32)
        for r in range(20):
            pair = rows[2 * r : 2 * r + 2]
            wide[r, col : col + 2, :HID] = pair[:, :HID]
            wide[r, col : col + 2, HID:] = pair[:, 2 * HID :]
            if 1 <= r < 19:
                cell_out[base + r : base + r + 1, :] = pair[near : near + 1, HID : 2 * HID]

    def border(b, a):
        pad = jnp.zeros((6, HID + AUX), F32)
        left = wide[a : a + 18, 6 + b, :]
        right = wide[a : a + 18, 39 + b, :]
        return jnp.concatenate([left, pad, right, pad], axis=0).astype(BF16)

    first = jnp.zeros((624, AUX), F32)
    second = jnp.zeros((512, AUX), F32)
    for b in range(3):
        cols = wide[:, 7 + b : 39 + b, :].astype(BF16)
        for a in range(3):
            t = 3 * a + b
            core = cols[a : a + 18].reshape(576, HID + AUX)
            edge = border(b, a)
            patches_out[:576, t * HID : (t + 1) * HID] = core[:, :HID]
            patches_out[576:, t * HID : (t + 1) * HID] = edge[:, :HID]
            aux = jnp.concatenate([core[:, HID:], edge[:, HID:]], axis=0)
            first = first + lax.dot_general(aux, placer(t, 0, cx), NN, preferred_element_type=F32)
            second = second + lax.dot_general(
                aux[32:544], placer(t, cx, cx), NN, preferred_element_type=F32
            )
            if t == 4:
                source = lax.broadcasted_iota(jnp.int32, (AUX, AUX), 0)
                copy = jnp.where(source == 2 * cx, 1.0, 0.0).astype(BF16)
                keep_out[...] = lax.dot_general(aux, copy, NN, preferred_element_type=F32)
    patches_out[:, 9 * HID : 9 * HID + AUX] = first.astype(BF16)
    patches_out[:, 9 * HID + AUX :] = jnp.zeros((624, AUX), BF16)
    frame_out[:, :AUX] = second.astype(BF16)
    frame_out[:, AUX:] = jnp.zeros((512, AUX), BF16)


def prepared(cx, hidden, cell, aux, low, high, left, right):
    return pl.pallas_call(
        functools.partial(prep_kernel, cx),
        out_shape=(
            jax.ShapeDtypeStruct((624, KPAD), BF16),
            jax.ShapeDtypeStruct((512, HID), BF16),
            jax.ShapeDtypeStruct((624, HID), F32),
            jax.ShapeDtypeStruct((624, 128), F32),
        ),
        in_specs=[VMEM] * 7,
        out_specs=(VMEM,) * 4,
        scratch_shapes=[pltpu.VMEM((20, 48, HID + AUX), F32)],
        compiler_params=PARAMS,
        cost_estimate=pl.CostEstimate(flops=0, bytes_accessed=100_000, transcendentals=0),
    )(hidden, cell, aux, low, high, left, right)


def chooser(half, shape, channel_axis):
    place = lax.broadcasted_iota(jnp.int32, shape, 1 - channel_axis)
    natural = lax.broadcasted_iota(jnp.int32, shape, channel_axis)
    y = lax.shift_right_logical(place, 5)
    zz = lax.shift_right_logical(place, 3) & 3
    wanted = zz * 64 + y * 16 + half * 8 + (place & 7)
    return jnp.where(natural == wanted, 1.0, 0.0).astype(BF16)


def parts_of(value):
    high = value.astype(BF16)
    rest = value - high.astype(F32)
    middle = rest.astype(BF16)
    return high, middle, (rest - middle.astype(F32)).astype(BF16)


def moved(values, choices):
    lhs = jnp.concatenate([part for value in values for part in parts_of(value)], axis=1)
    rhs = jnp.concatenate([choice for choice in choices for _ in range(3)], axis=0)
    return lax.dot_general(lhs, rhs, NN, preferred_element_type=F32)


def joined(values, choices):
    lhs, rhs = jnp.concatenate(values, axis=1), jnp.concatenate(choices, axis=0)
    return lax.dot_general(lhs, rhs, NN, preferred_element_type=F32)


def sigmoid(value):
    return 0.5 * jnp.tanh(0.5 * value) + 0.5


def updated(sums, bias, cell, keep):
    in_gate = sigmoid(sums[0][:, :128] + bias[0][None])
    decay_factor = sigmoid(sums[0][:, 128:] + bias[1][None])
    candidate = jnp.tanh(sums[1][:, :128] + bias[2][None])
    out_gate = sigmoid(sums[1][:, 128:] + bias[3][None])
    cell = decay_factor * cell + in_gate * candidate
    return (keep * out_gate * jnp.tanh(cell)).astype(BF16), cell


def gate_sums(patches, weight_ref):
    sums = []
    for pair in range(2):
        rhs = jnp.concatenate(
            [
                jnp.concatenate(
                    [
                        weight_ref[y * 4 + x, q * 32 : (q + 1) * 32, :]
                        for q in (2 * pair, 2 * pair + 1)
                        for y in range(4)
                    ],
                    axis=0,
                )
                for x in range(4)
            ],
            axis=1,
        )
        sums.append(lax.dot_general(patches, rhs, NT, preferred_element_type=F32))
    return sums


def first_half(i, half, patches_ref, weight_ref, bias_ref, cell_ref, keep_ref):
    sums = gate_sums(patches_ref[...], weight_ref)
    cell = moved([cell_ref[...]], [chooser(half, (HID, 128), 0)])
    return updated(sums, bias_ref[i], cell, keep_ref[...])


def own_kernel(half_ref, *refs):
    *ins, hid_out, cell_out = refs
    hid_out[...], cell_out[...] = first_half(0, half_ref[0], *ins)


def own_half(halves, patches, weight, bias, cell, keep):
    count = patches.shape[0]
    return pl.pallas_call(
        own_kernel,
        out_shape=(
            jax.ShapeDtypeStruct((count, 128), BF16),
            jax.ShapeDtypeStruct((count, 128), F32),
        ),
        in_specs=[SMEM] + [VMEM] * 5,
        out_specs=(VMEM, VMEM),
        compiler_params=PARAMS,
        cost_estimate=pl.CostEstimate(
            flops=2 * count * KPAD * 512, bytes_accessed=6_000_000, transcendentals=count * 640
        ),
    )(halves, patches, weight, bias, cell, keep)


def final_kernel(
    half_ref,
    patches_ref,
    own_ref,
    other_ref,
    bias_ref,
    cell_ref,
    keep_ref,
    hid0_ref,
    cell0_ref,
    frame_ref,
    keep2_ref,
    proj_ref,
    hid_out,
    cell_out,
    flux_out,
    wide,
    patches,
):
    choices = [chooser(half_ref[i], (128, HID), 1) for i in range(2)]
    hid, cell = first_half(
        1, half_ref[1], patches_ref, other_ref, bias_ref, cell_ref, keep_ref
    )
    cells = (cell0_ref[32:544, :], cell[32:544])
    natural = joined([hid0_ref[...], hid], choices)

    wide[:, 8:40, :] = natural[:576].reshape(18, 32, HID)
    for row in range(18):
        wide[row, 7:8, :] = natural[576 + row : 577 + row]
        wide[row, 40:41, :] = natural[600 + row : 601 + row]
    for b in range(3):
        moved_rows = wide[:, 7 + b : 39 + b, :].astype(BF16)
        for a in range(3):
            t = 3 * a + b
            patches[:, t * HID : (t + 1) * HID] = moved_rows[a : a + 16].reshape(512, HID)
    patches[:, 9 * HID :] = frame_ref[...]

    new_hids, new_cells = [], []
    for i, weight_ref in enumerate((own_ref, other_ref)):
        sums = gate_sums(patches[...], weight_ref)
        new_hid, new_cell = updated(sums, bias_ref[i], cells[i], keep_ref[32:544, :])
        new_hids.append(new_hid)
        new_cells.append(new_cell)
    hid = joined(new_hids, choices).astype(BF16)
    cell = moved(new_cells, choices)
    hid_out[...] = hid
    cell_out[...] = cell
    flux = lax.dot_general(proj_ref[...], hid, NT, preferred_element_type=F32)
    for row in range(16):
        flux_out[row : row + 1, :] = flux[0:1, row * 32 : (row + 1) * 32] * keep2_ref[row : row + 1, :]


def finished(halves, *arrays):
    return pl.pallas_call(
        final_kernel,
        out_shape=(
            jax.ShapeDtypeStruct((512, HID), BF16),
            jax.ShapeDtypeStruct((512, HID), F32),
            jax.ShapeDtypeStruct((16, 32), F32),
        ),
        in_specs=[SMEM] + [VMEM] * len(arrays),
        out_specs=(VMEM, VMEM, VMEM),
        scratch_shapes=[pltpu.VMEM((18, 48, HID), F32), pltpu.VMEM((512, KPAD), BF16)],
        compiler_params=PARAMS,
        cost_estimate=pl.CostEstimate(
            flops=2 * 824 * KPAD * 1024, bytes_accessed=14_000_000, transcendentals=1136 * 1280
        ),
    )(halves, *arrays)


def compute(halves, own, swapped, prep, land_mask, bias2, proj):
    rows, cols = land_mask.shape
    patches1, frame2, cell1, keep1 = prep
    other = swapped(own)
    hid0, cell0 = own_half(halves, patches1, own, bias2, cell1, keep1)
    hidden, cell, flux = finished(
        halves, patches1, own, other, bias2, cell1, keep1,
        hid0, cell0, frame2, land_mask.astype(F32), proj,
    )
    return hidden.reshape(rows, cols, HID), cell.reshape(rows, cols, HID), flux


def bias_of(bias, c):
    by_half = jnp.transpose(bias.reshape(4, 4, 4, 2, 8), (3, 0, 2, 1, 4)).reshape(2, 4, 128)
    return jnp.where(c == 0, by_half, by_half[::-1])


def aux_of(frames, land_mask):
    rows, cols = land_mask.shape
    both = jnp.transpose(frames, (1, 2, 0, 3)).reshape(rows, cols, -1)
    aux = jnp.concatenate([both, land_mask.astype(BF16)[..., None]], axis=-1)
    return jnp.pad(aux, ((0, 0), (0, 0), (0, AUX - aux.shape[2])))


def body(frames, hidden_init, cell_init, conv_weight, bias, land_mask, projection):
    cx = frames.shape[3]
    x, c = lax.axis_index("x"), lax.axis_index("c")
    packed = pack_weights(conv_weight)
    unit = lax.dynamic_slice(packed, (c * 8, x * (KPAD // 4)), (8, KPAD // 4))
    by_z = spread(unit, "z").reshape(128, KPAD // 4)

    state = (hidden_init, cell_init, aux_of(frames, land_mask))
    last, first = ends_of(*state)
    low = shifted(last, ("x", "c"), 1)
    high = shifted(first, ("x", "c"), -1)
    last, first = sides_of(*state, low, high)
    halves = jnp.stack([c, 1 - c]).astype(jnp.int32)
    proj = jnp.broadcast_to(projection[None], (16, HID))
    bias2 = bias_of(bias, c)
    by_z, last, first, halves, proj, bias2 = lax.optimization_barrier(
        (by_z, last, first, halves, proj, bias2)
    )

    own = spread(by_z, ("y", "x"))
    own, last, first = lax.optimization_barrier((own, last, first))
    left = shifted(last, ("z", "y"), 1)
    right = shifted(first, ("z", "y"), -1)
    prep = prepared(cx, *state, low, high, left, right)
    swapped = lambda piece: turned(piece, "c", 1)
    return compute(halves, own, swapped, prep, land_mask, bias2, proj)


def solution(mesh):
    split = Mesh(mesh.devices.reshape(16, 4, 4, 2), ("z", "y", "x", "c"))
    sx, sy = ("z", "y"), ("x", "c")
    in_specs = (
        P(None, sy, sx, None),
        P(sy, sx, None),
        P(sy, sx, None),
        P(None, None, sx),
        P(),
        P(sy, sx),
        P(),
    )
    out_specs = (P(sy, sx, None), P(sy, sx, None), P(sy, sx))
    return jax.shard_map(body, mesh=split, in_specs=in_specs, out_specs=out_specs, check_vma=False)
```

```python
import functools

import jax
import jax.numpy as jnp
from jax import lax
from jax.experimental import pallas as pl
from jax.experimental.pallas import tpu as pltpu
from jax.sharding import Mesh, PartitionSpec as P

KPAD = 2560
CHUNK = KPAD // 4
HID = 256
AUX = 128
PACK = 2 * HID + AUX
F32 = jnp.float32
BF16 = jnp.bfloat16
NT = (((1,), (1,)), ((), ()))
NN = (((1,), (0,)), ((), ()))
VMEM = pl.BlockSpec(memory_space=pltpu.VMEM)
SMEM = pl.BlockSpec(memory_space=pltpu.SMEM)
PARAMS = pltpu.CompilerParams(vmem_limit_bytes=16 * 1024 * 1024)


def pack_kernel(place_ref, weight_ref, out, whole):
    cx = weight_ref.shape[2] - HID
    frame = jnp.zeros((16, AUX), F32)
    for t in range(9):
        block = weight_ref[t]
        whole[:, t * HID : (t + 1) * HID] = block.astype(F32)[:, cx:]
        frame = frame + lax.dot_general(
            block[:, :AUX], placer(t, 0, cx), NN, preferred_element_type=F32
        )
    whole[:, 9 * HID : 9 * HID + AUX] = frame
    whole[:, 9 * HID + AUX :] = jnp.zeros((16, AUX), F32)
    row = pl.multiple_of(place_ref[0] * 8, 8)
    lane = pl.multiple_of(place_ref[1] * CHUNK, 128)
    unit = whole[pl.ds(row, 8), pl.ds(lane, CHUNK)]
    out[...] = jnp.concatenate([unit] * 16, axis=0).astype(BF16)


def packed_unit(place, conv_weight):
    return pl.pallas_call(
        pack_kernel,
        out_shape=jax.ShapeDtypeStruct((128, CHUNK), BF16),
        in_specs=[SMEM, VMEM],
        out_specs=VMEM,
        scratch_shapes=[pltpu.VMEM((16, KPAD), F32)],
        compiler_params=PARAMS,
        cost_estimate=pl.CostEstimate(flops=0, bytes_accessed=300_000, transcendentals=0),
    )(place, jnp.transpose(conv_weight, (0, 2, 1)))


def spread(block, axes):
    count = lax.axis_size(axes)
    copies = jnp.broadcast_to(block[None], (count,) + block.shape)
    return lax.all_to_all(copies, axes, 0, 0)


def turned(block, axis, step):
    count = lax.axis_size(axis)
    return lax.ppermute(block, axis, [(i, (i + step) % count) for i in range(count)])


def shifted(block, axes, step):
    count = lax.axis_size(axes)
    pairs = [(i, i + step) for i in range(count) if 0 <= i + step < count]
    return lax.ppermute(block, axes, pairs)


def ends_kernel(hidden_ref, cell_ref, aux_ref, last_out, first_out):
    for out, start in ((last_out, 14), (first_out, 0)):
        for j in range(2):
            rows = slice(j * 32, (j + 1) * 32)
            out[rows, :HID] = hidden_ref[start + j]
            out[rows, HID : 2 * HID] = cell_ref[start + j].astype(BF16)
            out[rows, 2 * HID :] = aux_ref[start + j]


def ends_of(hidden, cell, aux):
    return pl.pallas_call(
        ends_kernel,
        out_shape=(jax.ShapeDtypeStruct((64, PACK), BF16),) * 2,
        in_specs=[VMEM] * 3,
        out_specs=(VMEM, VMEM),
        compiler_params=PARAMS,
        cost_estimate=pl.CostEstimate(flops=0, bytes_accessed=1_000_000, transcendentals=0),
    )(hidden, cell, aux)


def sides_kernel(hidden_ref, cell_ref, aux_ref, low_ref, high_ref, last_out, first_out, last, first):
    for out, scratch, start, at in ((last_out, last, 16, 14), (first_out, first, 0, 0)):
        cols = slice(start, start + 16)
        for r in range(20):
            into = slice(2 * r, 2 * r + 2)
            if r < 2 or r >= 18:
                ref, j = (low_ref, r) if r < 2 else (high_ref, r - 18)
                block = ref[j * 32 + start : j * 32 + start + 16, :].astype(F32)
                scratch[into, :] = block[at : at + 2]
            else:
                scratch[into, :HID] = hidden_ref[r - 2, cols, :].astype(F32)[at : at + 2]
                scratch[into, HID : 2 * HID] = cell_ref[r - 2, cols, :][at : at + 2]
                scratch[into, 2 * HID :] = aux_ref[r - 2, cols, :].astype(F32)[at : at + 2]
        scratch[40:, :] = jnp.zeros((8, PACK), F32)
        out[...] = scratch[...].astype(BF16)


def sides_of(hidden, cell, aux, low, high):
    return pl.pallas_call(
        sides_kernel,
        out_shape=(jax.ShapeDtypeStruct((48, PACK), BF16),) * 2,
        in_specs=[VMEM] * 5,
        out_specs=(VMEM, VMEM),
        scratch_shapes=[pltpu.VMEM((48, PACK), F32)] * 2,
        compiler_params=PARAMS,
        cost_estimate=pl.CostEstimate(flops=0, bytes_accessed=1_000_000, transcendentals=0),
    )(hidden, cell, aux, low, high)


def placer(tap, first, cx):
    source = lax.broadcasted_iota(jnp.int32, (AUX, AUX), 0)
    target = lax.broadcasted_iota(jnp.int32, (AUX, AUX), 1)
    hit = (target - source == tap * cx - first) & (source >= first) & (source < first + cx)
    return jnp.where(hit, 1.0, 0.0).astype(BF16)


def prep_kernel(
    cx,
    hidden_ref,
    cell_ref,
    aux_ref,
    low_ref,
    high_ref,
    left_ref,
    right_ref,
    patches_out,
    frame_out,
    cell_out,
    keep_out,
    wide,
):
    wide[2:18, 8:40, :HID] = hidden_ref[...].astype(F32)
    wide[2:18, 8:40, HID:] = aux_ref[...].astype(F32)
    for ref, row in ((low_ref, 0), (high_ref, 18)):
        both = ref[...].astype(F32).reshape(2, 32, PACK)
        wide[row : row + 2, 8:40, :HID] = both[:, :, :HID]
        wide[row : row + 2, 8:40, HID:] = both[:, :, 2 * HID :]
    cell_out[:32, :] = low_ref[32:, HID : 2 * HID].astype(F32)
    cell_out[32:544, :] = cell_ref[...].reshape(512, HID)
    cell_out[544:576, :] = high_ref[:32, HID : 2 * HID].astype(F32)
    cell_out[576:, :] = jnp.zeros((48, HID), F32)
    for ref, col, near, base in ((left_ref, 6, 1, 575), (right_ref, 40, 0, 599)):
        rows = ref[...].astype(F32)
        for r in range(20):
            pair = rows[2 * r : 2 * r + 2]
            wide[r, col : col + 2, :HID] = pair[:, :HID]
            wide[r, col : col + 2, HID:] = pair[:, 2 * HID :]
            if 1 <= r < 19:
                cell_out[base + r : base + r + 1, :] = pair[near : near + 1, HID : 2 * HID]

    def border(b, a):
        pad = jnp.zeros((6, HID + AUX), F32)
        left = wide[a : a + 18, 6 + b, :]
        right = wide[a : a + 18, 39 + b, :]
        return jnp.concatenate([left, pad, right, pad], axis=0).astype(BF16)

    first = jnp.zeros((624, AUX), F32)
    second = jnp.zeros((512, AUX), F32)
    for b in range(3):
        cols = wide[:, 7 + b : 39 + b, :].astype(BF16)
        for a in range(3):
            t = 3 * a + b
            core = cols[a : a + 18].reshape(576, HID + AUX)
            edge = border(b, a)
            patches_out[:576, t * HID : (t + 1) * HID] = core[:, :HID]
            patches_out[576:, t * HID : (t + 1) * HID] = edge[:, :HID]
            aux = jnp.concatenate([core[:, HID:], edge[:, HID:]], axis=0)
            first = first + lax.dot_general(aux, placer(t, 0, cx), NN, preferred_element_type=F32)
            second = second + lax.dot_general(
                aux[32:544], placer(t, cx, cx), NN, preferred_element_type=F32
            )
            if t == 4:
                source = lax.broadcasted_iota(jnp.int32, (AUX, AUX), 0)
                copy = jnp.where(source == 2 * cx, 1.0, 0.0).astype(BF16)
                keep_out[...] = lax.dot_general(aux, copy, NN, preferred_element_type=F32)
    patches_out[:, 9 * HID : 9 * HID + AUX] = first.astype(BF16)
    patches_out[:, 9 * HID + AUX :] = jnp.zeros((624, AUX), BF16)
    frame_out[:, :AUX] = second.astype(BF16)
    frame_out[:, AUX:] = jnp.zeros((512, AUX), BF16)


def prepared(cx, hidden, cell, aux, low, high, left, right):
    return pl.pallas_call(
        functools.partial(prep_kernel, cx),
        out_shape=(
            jax.ShapeDtypeStruct((624, KPAD), BF16),
            jax.ShapeDtypeStruct((512, HID), BF16),
            jax.ShapeDtypeStruct((624, HID), F32),
            jax.ShapeDtypeStruct((624, 128), F32),
        ),
        in_specs=[VMEM] * 7,
        out_specs=(VMEM,) * 4,
        scratch_shapes=[pltpu.VMEM((20, 48, HID + AUX), F32)],
        compiler_params=PARAMS,
        cost_estimate=pl.CostEstimate(flops=0, bytes_accessed=100_000, transcendentals=0),
    )(hidden, cell, aux, low, high, left, right)


def chooser(half, shape, channel_axis):
    place = lax.broadcasted_iota(jnp.int32, shape, 1 - channel_axis)
    natural = lax.broadcasted_iota(jnp.int32, shape, channel_axis)
    y = lax.shift_right_logical(place, 5)
    zz = lax.shift_right_logical(place, 3) & 3
    wanted = zz * 64 + y * 16 + half * 8 + (place & 7)
    return jnp.where(natural == wanted, 1.0, 0.0).astype(BF16)


def parts_of(value):
    high = value.astype(BF16)
    rest = value - high.astype(F32)
    middle = rest.astype(BF16)
    return high, middle, (rest - middle.astype(F32)).astype(BF16)


def moved(values, choices):
    lhs = jnp.concatenate([part for value in values for part in parts_of(value)], axis=1)
    rhs = jnp.concatenate([choice for choice in choices for _ in range(3)], axis=0)
    return lax.dot_general(lhs, rhs, NN, preferred_element_type=F32)


def joined(values, choices):
    lhs, rhs = jnp.concatenate(values, axis=1), jnp.concatenate(choices, axis=0)
    return lax.dot_general(lhs, rhs, NN, preferred_element_type=F32)


def sigmoid(value):
    return 0.5 * jnp.tanh(0.5 * value) + 0.5


def updated(sums, bias, cell, keep):
    in_gate = sigmoid(sums[0][:, :128] + bias[0][None])
    decay_factor = sigmoid(sums[0][:, 128:] + bias[1][None])
    candidate = jnp.tanh(sums[1][:, :128] + bias[2][None])
    out_gate = sigmoid(sums[1][:, 128:] + bias[3][None])
    cell = decay_factor * cell + in_gate * candidate
    return (keep * out_gate * jnp.tanh(cell)).astype(BF16), cell


def gate_sums(patches, weight_ref):
    sums = []
    for pair in range(2):
        rhs = jnp.concatenate(
            [
                jnp.concatenate(
                    [
                        weight_ref[y * 4 + x, q * 32 : (q + 1) * 32, :]
                        for q in (2 * pair, 2 * pair + 1)
                        for y in range(4)
                    ],
                    axis=0,
                )
                for x in range(4)
            ],
            axis=1,
        )
        sums.append(lax.dot_general(patches, rhs, NT, preferred_element_type=F32))
    return sums


def first_half(i, half, patches_ref, weight_ref, bias_ref, cell_ref, keep_ref):
    sums = gate_sums(patches_ref[...], weight_ref)
    cell = moved([cell_ref[...]], [chooser(half, (HID, 128), 0)])
    return updated(sums, bias_ref[i], cell, keep_ref[...])


def own_kernel(half_ref, *refs):
    *ins, hid_out, cell_out = refs
    hid_out[...], cell_out[...] = first_half(0, half_ref[0], *ins)


def own_half(halves, patches, weight, bias, cell, keep):
    count = patches.shape[0]
    return pl.pallas_call(
        own_kernel,
        out_shape=(
            jax.ShapeDtypeStruct((count, 128), BF16),
            jax.ShapeDtypeStruct((count, 128), F32),
        ),
        in_specs=[SMEM] + [VMEM] * 5,
        out_specs=(VMEM, VMEM),
        compiler_params=PARAMS,
        cost_estimate=pl.CostEstimate(
            flops=2 * count * KPAD * 512, bytes_accessed=6_000_000, transcendentals=count * 640
        ),
    )(halves, patches, weight, bias, cell, keep)


def final_kernel(
    half_ref,
    patches_ref,
    own_ref,
    other_ref,
    bias_ref,
    cell_ref,
    keep_ref,
    hid0_ref,
    cell0_ref,
    frame_ref,
    keep2_ref,
    proj_ref,
    hid_out,
    cell_out,
    flux_out,
    wide,
    patches,
):
    choices = [chooser(half_ref[i], (128, HID), 1) for i in range(2)]
    hid, cell = first_half(
        1, half_ref[1], patches_ref, other_ref, bias_ref, cell_ref, keep_ref
    )
    cells = (cell0_ref[32:544, :], cell[32:544])
    natural = joined([hid0_ref[...], hid], choices)

    wide[:, 8:40, :] = natural[:576].reshape(18, 32, HID)
    for row in range(18):
        wide[row, 7:8, :] = natural[576 + row : 577 + row]
        wide[row, 40:41, :] = natural[600 + row : 601 + row]
    for b in range(3):
        moved_rows = wide[:, 7 + b : 39 + b, :].astype(BF16)
        for a in range(3):
            t = 3 * a + b
            patches[:, t * HID : (t + 1) * HID] = moved_rows[a : a + 16].reshape(512, HID)
    patches[:, 9 * HID :] = frame_ref[...]

    new_hids, new_cells = [], []
    for i, weight_ref in enumerate((own_ref, other_ref)):
        sums = gate_sums(patches[...], weight_ref)
        new_hid, new_cell = updated(sums, bias_ref[i], cells[i], keep_ref[32:544, :])
        new_hids.append(new_hid)
        new_cells.append(new_cell)
    hid = joined(new_hids, choices).astype(BF16)
    cell = moved(new_cells, choices)
    hid_out[...] = hid
    cell_out[...] = cell
    flux = lax.dot_general(proj_ref[...], hid, NT, preferred_element_type=F32)
    for row in range(16):
        flux_out[row : row + 1, :] = flux[0:1, row * 32 : (row + 1) * 32] * keep2_ref[row : row + 1, :]


def finished(halves, *arrays):
    return pl.pallas_call(
        final_kernel,
        out_shape=(
            jax.ShapeDtypeStruct((512, HID), BF16),
            jax.ShapeDtypeStruct((512, HID), F32),
            jax.ShapeDtypeStruct((16, 32), F32),
        ),
        in_specs=[SMEM] + [VMEM] * len(arrays),
        out_specs=(VMEM, VMEM, VMEM),
        scratch_shapes=[pltpu.VMEM((18, 48, HID), F32), pltpu.VMEM((512, KPAD), BF16)],
        compiler_params=PARAMS,
        cost_estimate=pl.CostEstimate(
            flops=2 * 824 * KPAD * 1024, bytes_accessed=14_000_000, transcendentals=1136 * 1280
        ),
    )(halves, *arrays)


def compute(halves, own, swapped, prep, land_mask, bias2, proj):
    rows, cols = land_mask.shape
    patches1, frame2, cell1, keep1 = prep
    other = swapped(own)
    hid0, cell0 = own_half(halves, patches1, own, bias2, cell1, keep1)
    hidden, cell, flux = finished(
        halves, patches1, own, other, bias2, cell1, keep1,
        hid0, cell0, frame2, land_mask.astype(F32), proj,
    )
    return hidden.reshape(rows, cols, HID), cell.reshape(rows, cols, HID), flux


def bias_of(bias, c):
    by_half = jnp.transpose(bias.reshape(4, 4, 4, 2, 8), (3, 0, 2, 1, 4)).reshape(2, 4, 128)
    return jnp.where(c == 0, by_half, by_half[::-1])


def aux_of(frames, land_mask):
    rows, cols = land_mask.shape
    both = jnp.transpose(frames, (1, 2, 0, 3)).reshape(rows, cols, -1)
    aux = jnp.concatenate([both, land_mask.astype(BF16)[..., None]], axis=-1)
    return jnp.pad(aux, ((0, 0), (0, 0), (0, AUX - aux.shape[2])))


def body(frames, hidden_init, cell_init, conv_weight, bias, land_mask, projection):
    cx = frames.shape[3]
    x, c = lax.axis_index("x"), lax.axis_index("c")
    copies = packed_unit(jnp.stack([c, x]).astype(jnp.int32), conv_weight)
    by_z = lax.all_to_all(copies.reshape(16, 8, CHUNK), "z", 0, 0).reshape(128, CHUNK)

    state = (hidden_init, cell_init, aux_of(frames, land_mask))
    last, first = ends_of(*state)
    low = shifted(last, ("x", "c"), 1)
    high = shifted(first, ("x", "c"), -1)
    last, first = sides_of(*state, low, high)
    halves = jnp.stack([c, 1 - c]).astype(jnp.int32)
    proj = jnp.broadcast_to(projection[None], (16, HID))
    bias2 = bias_of(bias, c)
    by_z, last, first, halves, proj, bias2 = lax.optimization_barrier(
        (by_z, last, first, halves, proj, bias2)
    )

    own = spread(by_z, ("y", "x"))
    own, last, first = lax.optimization_barrier((own, last, first))
    left = shifted(last, ("z", "y"), 1)
    right = shifted(first, ("z", "y"), -1)
    prep = prepared(cx, *state, low, high, left, right)
    swapped = lambda piece: turned(piece, "c", 1)
    return compute(halves, own, swapped, prep, land_mask, bias2, proj)


def solution(mesh):
    split = Mesh(mesh.devices.reshape(16, 4, 4, 2), ("z", "y", "x", "c"))
    sx, sy = ("z", "y"), ("x", "c")
    in_specs = (
        P(None, sy, sx, None),
        P(sy, sx, None),
        P(sy, sx, None),
        P(None, None, sx),
        P(),
        P(sy, sx),
        P(),
    )
    out_specs = (P(sy, sx, None), P(sy, sx, None), P(sy, sx))
    return jax.shard_map(body, mesh=split, in_specs=in_specs, out_specs=out_specs, check_vma=False)
```

```python
import functools

import jax
import jax.numpy as jnp
from jax import lax
from jax.experimental import pallas as pl
from jax.experimental.pallas import tpu as pltpu
from jax.sharding import Mesh, PartitionSpec as P

KPAD = 2560
CHUNK = KPAD // 4
HID = 256
AUX = 128
PACK = 2 * HID + AUX
F32 = jnp.float32
BF16 = jnp.bfloat16
NT = (((1,), (1,)), ((), ()))
NN = (((1,), (0,)), ((), ()))
VMEM = pl.BlockSpec(memory_space=pltpu.VMEM)
SMEM = pl.BlockSpec(memory_space=pltpu.SMEM)
PARAMS = pltpu.CompilerParams(vmem_limit_bytes=16 * 1024 * 1024)


def pack_kernel(place_ref, weight_ref, out, whole):
    cx = weight_ref.shape[2] - HID
    frame = jnp.zeros((16, AUX), F32)
    for t in range(9):
        block = weight_ref[t]
        whole[:, t * HID : (t + 1) * HID] = block.astype(F32)[:, cx:]
        frame = frame + lax.dot_general(
            block[:, :AUX], placer(t, 0, cx), NN, preferred_element_type=F32
        )
    whole[:, 9 * HID : 9 * HID + AUX] = frame
    whole[:, 9 * HID + AUX :] = jnp.zeros((16, AUX), F32)
    row = pl.multiple_of(place_ref[0] * 8, 8)
    lane = pl.multiple_of(place_ref[1] * CHUNK, 128)
    unit = whole[pl.ds(row, 8), pl.ds(lane, CHUNK)]
    out[...] = jnp.concatenate([unit] * 16, axis=0).astype(BF16)


def packed_unit(place, conv_weight):
    return pl.pallas_call(
        pack_kernel,
        out_shape=jax.ShapeDtypeStruct((128, CHUNK), BF16),
        in_specs=[SMEM, VMEM],
        out_specs=VMEM,
        scratch_shapes=[pltpu.VMEM((16, KPAD), F32)],
        compiler_params=PARAMS,
        cost_estimate=pl.CostEstimate(flops=0, bytes_accessed=300_000, transcendentals=0),
    )(place, jnp.transpose(conv_weight, (0, 2, 1)))


def spread(block, axes):
    count = lax.axis_size(axes)
    copies = jnp.broadcast_to(block[None], (count,) + block.shape)
    return lax.all_to_all(copies, axes, 0, 0)


def turned(block, axis, step):
    count = lax.axis_size(axis)
    return lax.ppermute(block, axis, [(i, (i + step) % count) for i in range(count)])


def shifted(block, axes, step):
    count = lax.axis_size(axes)
    pairs = [(i, i + step) for i in range(count) if 0 <= i + step < count]
    return lax.ppermute(block, axes, pairs)


def ends_kernel(hidden_ref, cell_ref, aux_ref, last_out, first_out):
    for out, start in ((last_out, 14), (first_out, 0)):
        for j in range(2):
            rows = slice(j * 32, (j + 1) * 32)
            out[rows, :HID] = hidden_ref[start + j]
            out[rows, HID : 2 * HID] = cell_ref[start + j].astype(BF16)
            out[rows, 2 * HID :] = aux_ref[start + j]


def ends_of(hidden, cell, aux):
    return pl.pallas_call(
        ends_kernel,
        out_shape=(jax.ShapeDtypeStruct((64, PACK), BF16),) * 2,
        in_specs=[VMEM] * 3,
        out_specs=(VMEM, VMEM),
        compiler_params=PARAMS,
        cost_estimate=pl.CostEstimate(flops=0, bytes_accessed=1_000_000, transcendentals=0),
    )(hidden, cell, aux)


def sides_kernel(hidden_ref, cell_ref, aux_ref, low_ref, high_ref, last_out, first_out, last, first):
    for out, scratch, start, at in ((last_out, last, 16, 14), (first_out, first, 0, 0)):
        cols = slice(start, start + 16)
        for r in range(20):
            into = slice(2 * r, 2 * r + 2)
            if r < 2 or r >= 18:
                ref, j = (low_ref, r) if r < 2 else (high_ref, r - 18)
                block = ref[j * 32 + start : j * 32 + start + 16, :].astype(F32)
                scratch[into, :] = block[at : at + 2]
            else:
                scratch[into, :HID] = hidden_ref[r - 2, cols, :].astype(F32)[at : at + 2]
                scratch[into, HID : 2 * HID] = cell_ref[r - 2, cols, :][at : at + 2]
                scratch[into, 2 * HID :] = aux_ref[r - 2, cols, :].astype(F32)[at : at + 2]
        scratch[40:, :] = jnp.zeros((8, PACK), F32)
        out[...] = scratch[...].astype(BF16)


def sides_of(hidden, cell, aux, low, high):
    return pl.pallas_call(
        sides_kernel,
        out_shape=(jax.ShapeDtypeStruct((48, PACK), BF16),) * 2,
        in_specs=[VMEM] * 5,
        out_specs=(VMEM, VMEM),
        scratch_shapes=[pltpu.VMEM((48, PACK), F32)] * 2,
        compiler_params=PARAMS,
        cost_estimate=pl.CostEstimate(flops=0, bytes_accessed=1_000_000, transcendentals=0),
    )(hidden, cell, aux, low, high)


def placer(tap, first, cx):
    source = lax.broadcasted_iota(jnp.int32, (AUX, AUX), 0)
    target = lax.broadcasted_iota(jnp.int32, (AUX, AUX), 1)
    hit = (target - source == tap * cx - first) & (source >= first) & (source < first + cx)
    return jnp.where(hit, 1.0, 0.0).astype(BF16)


def prep_kernel(
    cx,
    hidden_ref,
    cell_ref,
    aux_ref,
    low_ref,
    high_ref,
    left_ref,
    right_ref,
    patches_out,
    frame_out,
    cell_out,
    keep_out,
    wide,
):
    wide[2:18, 8:40, :HID] = hidden_ref[...].astype(F32)
    wide[2:18, 8:40, HID:] = aux_ref[...].astype(F32)
    for ref, row in ((low_ref, 0), (high_ref, 18)):
        both = ref[...].astype(F32).reshape(2, 32, PACK)
        wide[row : row + 2, 8:40, :HID] = both[:, :, :HID]
        wide[row : row + 2, 8:40, HID:] = both[:, :, 2 * HID :]
    cell_out[:32, :] = low_ref[32:, HID : 2 * HID].astype(F32)
    cell_out[32:544, :] = cell_ref[...].reshape(512, HID)
    cell_out[544:576, :] = high_ref[:32, HID : 2 * HID].astype(F32)
    cell_out[576:, :] = jnp.zeros((48, HID), F32)
    for ref, col, near, base in ((left_ref, 6, 1, 575), (right_ref, 40, 0, 599)):
        rows = ref[...].astype(F32)
        for r in range(20):
            pair = rows[2 * r : 2 * r + 2]
            wide[r, col : col + 2, :HID] = pair[:, :HID]
            wide[r, col : col + 2, HID:] = pair[:, 2 * HID :]
            if 1 <= r < 19:
                cell_out[base + r : base + r + 1, :] = pair[near : near + 1, HID : 2 * HID]

    def border(b, a):
        pad = jnp.zeros((6, HID + AUX), F32)
        left = wide[a : a + 18, 6 + b, :]
        right = wide[a : a + 18, 39 + b, :]
        return jnp.concatenate([left, pad, right, pad], axis=0).astype(BF16)

    first = jnp.zeros((624, AUX), F32)
    second = jnp.zeros((512, AUX), F32)
    for b in range(3):
        cols = wide[:, 7 + b : 39 + b, :].astype(BF16)
        for a in range(3):
            t = 3 * a + b
            core = cols[a : a + 18].reshape(576, HID + AUX)
            edge = border(b, a)
            patches_out[:576, t * HID : (t + 1) * HID] = core[:, :HID]
            patches_out[576:, t * HID : (t + 1) * HID] = edge[:, :HID]
            aux = jnp.concatenate([core[:, HID:], edge[:, HID:]], axis=0)
            first = first + lax.dot_general(aux, placer(t, 0, cx), NN, preferred_element_type=F32)
            second = second + lax.dot_general(
                aux[32:544], placer(t, cx, cx), NN, preferred_element_type=F32
            )
            if t == 4:
                source = lax.broadcasted_iota(jnp.int32, (AUX, AUX), 0)
                copy = jnp.where(source == 2 * cx, 1.0, 0.0).astype(BF16)
                keep_out[...] = lax.dot_general(aux, copy, NN, preferred_element_type=F32)
    patches_out[:, 9 * HID : 9 * HID + AUX] = first.astype(BF16)
    patches_out[:, 9 * HID + AUX :] = jnp.zeros((624, AUX), BF16)
    frame_out[:, :AUX] = second.astype(BF16)
    frame_out[:, AUX:] = jnp.zeros((512, AUX), BF16)


def prepared(cx, hidden, cell, aux, low, high, left, right):
    return pl.pallas_call(
        functools.partial(prep_kernel, cx),
        out_shape=(
            jax.ShapeDtypeStruct((624, KPAD), BF16),
            jax.ShapeDtypeStruct((512, HID), BF16),
            jax.ShapeDtypeStruct((624, HID), F32),
            jax.ShapeDtypeStruct((624, 128), F32),
        ),
        in_specs=[VMEM] * 7,
        out_specs=(VMEM,) * 4,
        scratch_shapes=[pltpu.VMEM((20, 48, HID + AUX), F32)],
        compiler_params=PARAMS,
        cost_estimate=pl.CostEstimate(flops=0, bytes_accessed=100_000, transcendentals=0),
    )(hidden, cell, aux, low, high, left, right)


def chooser(half, shape, channel_axis):
    place = lax.broadcasted_iota(jnp.int32, shape, 1 - channel_axis)
    natural = lax.broadcasted_iota(jnp.int32, shape, channel_axis)
    y = lax.shift_right_logical(place, 5)
    zz = lax.shift_right_logical(place, 3) & 3
    wanted = zz * 64 + y * 16 + half * 8 + (place & 7)
    return jnp.where(natural == wanted, 1.0, 0.0).astype(BF16)


def parts_of(value):
    high = value.astype(BF16)
    rest = value - high.astype(F32)
    middle = rest.astype(BF16)
    return high, middle, (rest - middle.astype(F32)).astype(BF16)


def moved(values, choices):
    lhs = jnp.concatenate([part for value in values for part in parts_of(value)], axis=1)
    rhs = jnp.concatenate([choice for choice in choices for _ in range(3)], axis=0)
    return lax.dot_general(lhs, rhs, NN, preferred_element_type=F32)


def joined(values, choices):
    lhs, rhs = jnp.concatenate(values, axis=1), jnp.concatenate(choices, axis=0)
    return lax.dot_general(lhs, rhs, NN, preferred_element_type=F32)


def sigmoid(value):
    return 0.5 * jnp.tanh(0.5 * value) + 0.5


def updated(sums, bias, cell, keep):
    in_gate = sigmoid(sums[0][:, :128] + bias[0][None])
    decay_factor = sigmoid(sums[0][:, 128:] + bias[1][None])
    candidate = jnp.tanh(sums[1][:, :128] + bias[2][None])
    out_gate = sigmoid(sums[1][:, 128:] + bias[3][None])
    cell = decay_factor * cell + in_gate * candidate
    return (keep * out_gate * jnp.tanh(cell)).astype(BF16), cell


def gate_sums(patches, weight_ref):
    sums = []
    for pair in range(2):
        rhs = jnp.concatenate(
            [
                jnp.concatenate(
                    [
                        weight_ref[y * 4 + x, q * 32 : (q + 1) * 32, :]
                        for q in (2 * pair, 2 * pair + 1)
                        for y in range(4)
                    ],
                    axis=0,
                )
                for x in range(4)
            ],
            axis=1,
        )
        sums.append(lax.dot_general(patches, rhs, NT, preferred_element_type=F32))
    return sums


def first_half(i, half, patches_ref, weight_ref, bias_ref, cell_ref, keep_ref):
    sums = gate_sums(patches_ref[...], weight_ref)
    cell = moved([cell_ref[...]], [chooser(half, (HID, 128), 0)])
    return updated(sums, bias_ref[i], cell, keep_ref[...])


def own_kernel(half_ref, *refs):
    *ins, hid_out, cell_out = refs
    hid_out[...], cell_out[...] = first_half(0, half_ref[0], *ins)


def own_half(halves, patches, weight, bias, cell, keep):
    count = patches.shape[0]
    return pl.pallas_call(
        own_kernel,
        out_shape=(
            jax.ShapeDtypeStruct((count, 128), BF16),
            jax.ShapeDtypeStruct((count, 128), F32),
        ),
        in_specs=[SMEM] + [VMEM] * 5,
        out_specs=(VMEM, VMEM),
        compiler_params=PARAMS,
        cost_estimate=pl.CostEstimate(
            flops=2 * count * KPAD * 512, bytes_accessed=6_000_000, transcendentals=count * 640
        ),
    )(halves, patches, weight, bias, cell, keep)


def final_kernel(
    half_ref,
    patches_ref,
    own_ref,
    other_ref,
    bias_ref,
    cell_ref,
    keep_ref,
    hid0_ref,
    cell0_ref,
    frame_ref,
    keep2_ref,
    proj_ref,
    hid_out,
    cell_out,
    flux_out,
    wide,
    patches,
):
    choices = [chooser(half_ref[i], (128, HID), 1) for i in range(2)]
    hid, cell = first_half(
        1, half_ref[1], patches_ref, other_ref, bias_ref, cell_ref, keep_ref
    )
    cells = (cell0_ref[32:544, :], cell[32:544])
    natural = joined([hid0_ref[...], hid], choices)

    wide[:, 8:40, :] = natural[:576].reshape(18, 32, HID)
    for row in range(18):
        wide[row, 7:8, :] = natural[576 + row : 577 + row]
        wide[row, 40:41, :] = natural[600 + row : 601 + row]
    for b in range(3):
        moved_rows = wide[:, 7 + b : 39 + b, :].astype(BF16)
        for a in range(3):
            t = 3 * a + b
            patches[:, t * HID : (t + 1) * HID] = moved_rows[a : a + 16].reshape(512, HID)
    patches[:, 9 * HID :] = frame_ref[...]

    new_hids, new_cells = [], []
    for i, weight_ref in enumerate((own_ref, other_ref)):
        sums = gate_sums(patches[...], weight_ref)
        new_hid, new_cell = updated(sums, bias_ref[i], cells[i], keep_ref[32:544, :])
        new_hids.append(new_hid)
        new_cells.append(new_cell)
    hid = joined(new_hids, choices).astype(BF16)
    cell = moved(new_cells, choices)
    hid_out[...] = hid
    cell_out[...] = cell
    flux = lax.dot_general(proj_ref[...], hid, NT, preferred_element_type=F32)
    for row in range(16):
        flux_out[row : row + 1, :] = flux[0:1, row * 32 : (row + 1) * 32] * keep2_ref[row : row + 1, :]


def finished(halves, *arrays):
    return pl.pallas_call(
        final_kernel,
        out_shape=(
            jax.ShapeDtypeStruct((512, HID), BF16),
            jax.ShapeDtypeStruct((512, HID), F32),
            jax.ShapeDtypeStruct((16, 32), F32),
        ),
        in_specs=[SMEM] + [VMEM] * len(arrays),
        out_specs=(VMEM, VMEM, VMEM),
        scratch_shapes=[pltpu.VMEM((18, 48, HID), F32), pltpu.VMEM((512, KPAD), BF16)],
        compiler_params=PARAMS,
        cost_estimate=pl.CostEstimate(
            flops=2 * 824 * KPAD * 1024, bytes_accessed=14_000_000, transcendentals=1136 * 1280
        ),
    )(halves, *arrays)


def compute(halves, own, swapped, prep, land_mask, bias2, proj):
    rows, cols = land_mask.shape
    patches1, frame2, cell1, keep1 = prep
    other = swapped(own)
    hid0, cell0 = own_half(halves, patches1, own, bias2, cell1, keep1)
    hidden, cell, flux = finished(
        halves, patches1, own, other, bias2, cell1, keep1,
        hid0, cell0, frame2, land_mask.astype(F32), proj,
    )
    return hidden.reshape(rows, cols, HID), cell.reshape(rows, cols, HID), flux


def bias_of(bias, c):
    by_half = jnp.transpose(bias.reshape(4, 4, 4, 2, 8), (3, 0, 2, 1, 4)).reshape(2, 4, 128)
    return jnp.where(c == 0, by_half, by_half[::-1])


def aux_of(frames, land_mask):
    rows, cols = land_mask.shape
    both = jnp.transpose(frames, (1, 2, 0, 3)).reshape(rows, cols, -1)
    aux = jnp.concatenate([both, land_mask.astype(BF16)[..., None]], axis=-1)
    return jnp.pad(aux, ((0, 0), (0, 0), (0, AUX - aux.shape[2])))


def body(frames, hidden_init, cell_init, conv_weight, bias, land_mask, projection):
    cx = frames.shape[3]
    x, c = lax.axis_index("x"), lax.axis_index("c")
    copies = packed_unit(jnp.stack([c, x]).astype(jnp.int32), conv_weight)
    by_z = lax.all_to_all(copies.reshape(16, 8, CHUNK), "z", 0, 0).reshape(128, CHUNK)

    state = (hidden_init, cell_init, aux_of(frames, land_mask))
    last, first = ends_of(*state)
    low = shifted(last, ("x", "c"), 1)
    high = shifted(first, ("x", "c"), -1)
    last, first = sides_of(*state, low, high)
    halves = jnp.stack([c, 1 - c]).astype(jnp.int32)
    proj = jnp.broadcast_to(projection[None], (16, HID))
    bias2 = bias_of(bias, c)
    by_z, last, first, halves, proj, bias2 = lax.optimization_barrier(
        (by_z, last, first, halves, proj, bias2)
    )

    own = spread(by_z, ("y", "x"))
    own, last, first = lax.optimization_barrier((own, last, first))
    left = shifted(last, ("z", "y"), 1)
    right = shifted(first, ("z", "y"), -1)
    own, left, right = lax.optimization_barrier((own, left, right))
    prep = prepared(cx, *state, low, high, left, right)
    swapped = lambda piece: turned(piece, "c", 1)
    return compute(halves, own, swapped, prep, land_mask, bias2, proj)


def solution(mesh):
    split = Mesh(mesh.devices.reshape(16, 4, 4, 2), ("z", "y", "x", "c"))
    sx, sy = ("z", "y"), ("x", "c")
    in_specs = (
        P(None, sy, sx, None),
        P(sy, sx, None),
        P(sy, sx, None),
        P(None, None, sx),
        P(),
        P(sy, sx),
        P(),
    )
    out_specs = (P(sy, sx, None), P(sy, sx, None), P(sy, sx))
    return jax.shard_map(body, mesh=split, in_specs=in_specs, out_specs=out_specs, check_vma=False)
```

```python
import functools

import jax
import jax.numpy as jnp
from jax import lax
from jax.experimental import pallas as pl
from jax.experimental.pallas import tpu as pltpu
from jax.sharding import Mesh, PartitionSpec as P

KPAD = 2560
CHUNK = KPAD // 4
HID = 256
AUX = 128
PACK = 2 * HID + AUX
F32 = jnp.float32
BF16 = jnp.bfloat16
NT = (((1,), (1,)), ((), ()))
NN = (((1,), (0,)), ((), ()))
VMEM = pl.BlockSpec(memory_space=pltpu.VMEM)
SMEM = pl.BlockSpec(memory_space=pltpu.SMEM)
PARAMS = pltpu.CompilerParams(vmem_limit_bytes=16 * 1024 * 1024)


def pack_kernel(place_ref, weight_ref, out, whole):
    cx = weight_ref.shape[2] - HID
    frame = jnp.zeros((16, AUX), F32)
    for t in range(9):
        block = weight_ref[t]
        whole[:, t * HID : (t + 1) * HID] = block.astype(F32)[:, cx:]
        frame = frame + lax.dot_general(
            block[:, :AUX], placer(t, 0, cx), NN, preferred_element_type=F32
        )
    whole[:, 9 * HID : 9 * HID + AUX] = frame
    whole[:, 9 * HID + AUX :] = jnp.zeros((16, AUX), F32)
    row = pl.multiple_of(place_ref[0] * 8, 8)
    lane = pl.multiple_of(place_ref[1] * CHUNK, 128)
    unit = whole[pl.ds(row, 8), pl.ds(lane, CHUNK)]
    out[...] = jnp.concatenate([unit] * 16, axis=0).astype(BF16)


def packed_unit(place, conv_weight):
    return pl.pallas_call(
        pack_kernel,
        out_shape=jax.ShapeDtypeStruct((128, CHUNK), BF16),
        in_specs=[SMEM, VMEM],
        out_specs=VMEM,
        scratch_shapes=[pltpu.VMEM((16, KPAD), F32)],
        compiler_params=PARAMS,
        cost_estimate=pl.CostEstimate(flops=0, bytes_accessed=300_000, transcendentals=0),
    )(place, jnp.transpose(conv_weight, (0, 2, 1)))


def spread(block, axes):
    count = lax.axis_size(axes)
    copies = jnp.broadcast_to(block[None], (count,) + block.shape)
    return lax.all_to_all(copies, axes, 0, 0)


def turned(block, axis, step):
    count = lax.axis_size(axis)
    return lax.ppermute(block, axis, [(i, (i + step) % count) for i in range(count)])


def shifted(block, axes, step):
    count = lax.axis_size(axes)
    pairs = [(i, i + step) for i in range(count) if 0 <= i + step < count]
    return lax.ppermute(block, axes, pairs)


def ends_kernel(hidden_ref, cell_ref, aux_ref, last_out, first_out):
    for out, start in ((last_out, 14), (first_out, 0)):
        for j in range(2):
            rows = slice(j * 32, (j + 1) * 32)
            out[rows, :HID] = hidden_ref[start + j]
            out[rows, HID : 2 * HID] = cell_ref[start + j].astype(BF16)
            out[rows, 2 * HID :] = aux_ref[start + j]


def ends_of(hidden, cell, aux):
    return pl.pallas_call(
        ends_kernel,
        out_shape=(jax.ShapeDtypeStruct((64, PACK), BF16),) * 2,
        in_specs=[VMEM] * 3,
        out_specs=(VMEM, VMEM),
        compiler_params=PARAMS,
        cost_estimate=pl.CostEstimate(flops=0, bytes_accessed=1_000_000, transcendentals=0),
    )(hidden, cell, aux)


def sides_kernel(hidden_ref, cell_ref, aux_ref, low_ref, high_ref, last_out, first_out, last, first):
    for out, scratch, start, at in ((last_out, last, 16, 14), (first_out, first, 0, 0)):
        cols = slice(start, start + 16)
        for r in range(20):
            into = slice(2 * r, 2 * r + 2)
            if r < 2 or r >= 18:
                ref, j = (low_ref, r) if r < 2 else (high_ref, r - 18)
                block = ref[j * 32 + start : j * 32 + start + 16, :].astype(F32)
                scratch[into, :] = block[at : at + 2]
            else:
                scratch[into, :HID] = hidden_ref[r - 2, cols, :].astype(F32)[at : at + 2]
                scratch[into, HID : 2 * HID] = cell_ref[r - 2, cols, :][at : at + 2]
                scratch[into, 2 * HID :] = aux_ref[r - 2, cols, :].astype(F32)[at : at + 2]
        scratch[40:, :] = jnp.zeros((8, PACK), F32)
        out[...] = scratch[...].astype(BF16)


def sides_of(hidden, cell, aux, low, high):
    return pl.pallas_call(
        sides_kernel,
        out_shape=(jax.ShapeDtypeStruct((48, PACK), BF16),) * 2,
        in_specs=[VMEM] * 5,
        out_specs=(VMEM, VMEM),
        scratch_shapes=[pltpu.VMEM((48, PACK), F32)] * 2,
        compiler_params=PARAMS,
        cost_estimate=pl.CostEstimate(flops=0, bytes_accessed=1_000_000, transcendentals=0),
    )(hidden, cell, aux, low, high)


def placer(tap, first, cx):
    source = lax.broadcasted_iota(jnp.int32, (AUX, AUX), 0)
    target = lax.broadcasted_iota(jnp.int32, (AUX, AUX), 1)
    hit = (target - source == tap * cx - first) & (source >= first) & (source < first + cx)
    return jnp.where(hit, 1.0, 0.0).astype(BF16)


def prep_kernel(
    cx,
    hidden_ref,
    cell_ref,
    aux_ref,
    low_ref,
    high_ref,
    left_ref,
    right_ref,
    patches_out,
    frame_out,
    cell_out,
    keep_out,
    wide,
):
    wide[2:18, 8:40, :HID] = hidden_ref[...].astype(F32)
    wide[2:18, 8:40, HID:] = aux_ref[...].astype(F32)
    for ref, row in ((low_ref, 0), (high_ref, 18)):
        both = ref[...].astype(F32).reshape(2, 32, PACK)
        wide[row : row + 2, 8:40, :HID] = both[:, :, :HID]
        wide[row : row + 2, 8:40, HID:] = both[:, :, 2 * HID :]
    cell_out[:32, :] = low_ref[32:, HID : 2 * HID].astype(F32)
    cell_out[32:544, :] = cell_ref[...].reshape(512, HID)
    cell_out[544:576, :] = high_ref[:32, HID : 2 * HID].astype(F32)
    cell_out[576:, :] = jnp.zeros((48, HID), F32)
    for ref, col, near, base in ((left_ref, 6, 1, 575), (right_ref, 40, 0, 599)):
        rows = ref[...].astype(F32)
        for r in range(20):
            pair = rows[2 * r : 2 * r + 2]
            wide[r, col : col + 2, :HID] = pair[:, :HID]
            wide[r, col : col + 2, HID:] = pair[:, 2 * HID :]
            if 1 <= r < 19:
                cell_out[base + r : base + r + 1, :] = pair[near : near + 1, HID : 2 * HID]

    def border(b, a):
        pad = jnp.zeros((6, HID + AUX), F32)
        left = wide[a : a + 18, 6 + b, :]
        right = wide[a : a + 18, 39 + b, :]
        return jnp.concatenate([left, pad, right, pad], axis=0).astype(BF16)

    first = jnp.zeros((624, AUX), F32)
    second = jnp.zeros((512, AUX), F32)
    for b in range(3):
        cols = wide[:, 7 + b : 39 + b, :].astype(BF16)
        for a in range(3):
            t = 3 * a + b
            core = cols[a : a + 18].reshape(576, HID + AUX)
            edge = border(b, a)
            patches_out[:576, t * HID : (t + 1) * HID] = core[:, :HID]
            patches_out[576:, t * HID : (t + 1) * HID] = edge[:, :HID]
            aux = jnp.concatenate([core[:, HID:], edge[:, HID:]], axis=0)
            first = first + lax.dot_general(aux, placer(t, 0, cx), NN, preferred_element_type=F32)
            second = second + lax.dot_general(
                aux[32:544], placer(t, cx, cx), NN, preferred_element_type=F32
            )
            if t == 4:
                source = lax.broadcasted_iota(jnp.int32, (AUX, AUX), 0)
                copy = jnp.where(source == 2 * cx, 1.0, 0.0).astype(BF16)
                keep_out[...] = lax.dot_general(aux, copy, NN, preferred_element_type=F32)
    patches_out[:, 9 * HID : 9 * HID + AUX] = first.astype(BF16)
    patches_out[:, 9 * HID + AUX :] = jnp.zeros((624, AUX), BF16)
    frame_out[:, :AUX] = second.astype(BF16)
    frame_out[:, AUX:] = jnp.zeros((512, AUX), BF16)


def prepared(cx, hidden, cell, aux, low, high, left, right):
    return pl.pallas_call(
        functools.partial(prep_kernel, cx),
        out_shape=(
            jax.ShapeDtypeStruct((624, KPAD), BF16),
            jax.ShapeDtypeStruct((512, HID), BF16),
            jax.ShapeDtypeStruct((624, HID), F32),
            jax.ShapeDtypeStruct((624, 128), F32),
        ),
        in_specs=[VMEM] * 7,
        out_specs=(VMEM,) * 4,
        scratch_shapes=[pltpu.VMEM((20, 48, HID + AUX), F32)],
        compiler_params=PARAMS,
        cost_estimate=pl.CostEstimate(flops=0, bytes_accessed=100_000, transcendentals=0),
    )(hidden, cell, aux, low, high, left, right)


def chooser(half, shape, channel_axis):
    place = lax.broadcasted_iota(jnp.int32, shape, 1 - channel_axis)
    natural = lax.broadcasted_iota(jnp.int32, shape, channel_axis)
    y = lax.shift_right_logical(place, 5)
    zz = lax.shift_right_logical(place, 3) & 3
    wanted = zz * 64 + y * 16 + half * 8 + (place & 7)
    return jnp.where(natural == wanted, 1.0, 0.0).astype(BF16)


def parts_of(value):
    high = value.astype(BF16)
    rest = value - high.astype(F32)
    middle = rest.astype(BF16)
    return high, middle, (rest - middle.astype(F32)).astype(BF16)


def moved(values, choices):
    lhs = jnp.concatenate([part for value in values for part in parts_of(value)], axis=1)
    rhs = jnp.concatenate([choice for choice in choices for _ in range(3)], axis=0)
    return lax.dot_general(lhs, rhs, NN, preferred_element_type=F32)


def joined(values, choices):
    lhs, rhs = jnp.concatenate(values, axis=1), jnp.concatenate(choices, axis=0)
    return lax.dot_general(lhs, rhs, NN, preferred_element_type=F32)


def sigmoid(value):
    return 0.5 * jnp.tanh(0.5 * value) + 0.5


def updated(sums, bias, cell, keep):
    in_gate = sigmoid(sums[0][:, :128] + bias[0][None])
    decay_factor = sigmoid(sums[0][:, 128:] + bias[1][None])
    candidate = jnp.tanh(sums[1][:, :128] + bias[2][None])
    out_gate = sigmoid(sums[1][:, 128:] + bias[3][None])
    cell = decay_factor * cell + in_gate * candidate
    return (keep * out_gate * jnp.tanh(cell)).astype(BF16), cell


def gate_sums(patches, weight_ref):
    sums = []
    for pair in range(2):
        rhs = jnp.concatenate(
            [
                jnp.concatenate(
                    [
                        weight_ref[y * 4 + x, q * 32 : (q + 1) * 32, :]
                        for q in (2 * pair, 2 * pair + 1)
                        for y in range(4)
                    ],
                    axis=0,
                )
                for x in range(4)
            ],
            axis=1,
        )
        sums.append(lax.dot_general(patches, rhs, NT, preferred_element_type=F32))
    return sums


def first_half(i, half, patches_ref, weight_ref, bias_ref, cell_ref, keep_ref):
    sums = gate_sums(patches_ref[...], weight_ref)
    cell = moved([cell_ref[...]], [chooser(half, (HID, 128), 0)])
    return updated(sums, bias_ref[i], cell, keep_ref[...])


def own_kernel(half_ref, *refs):
    *ins, hid_out, cell_out = refs
    hid_out[...], cell_out[...] = first_half(0, half_ref[0], *ins)


def own_half(halves, patches, weight, bias, cell, keep):
    count = patches.shape[0]
    return pl.pallas_call(
        own_kernel,
        out_shape=(
            jax.ShapeDtypeStruct((count, 128), BF16),
            jax.ShapeDtypeStruct((count, 128), F32),
        ),
        in_specs=[SMEM] + [VMEM] * 5,
        out_specs=(VMEM, VMEM),
        compiler_params=PARAMS,
        cost_estimate=pl.CostEstimate(
            flops=2 * count * KPAD * 512, bytes_accessed=6_000_000, transcendentals=count * 640
        ),
    )(halves, patches, weight, bias, cell, keep)


def final_kernel(
    half_ref,
    patches_ref,
    own_ref,
    other_ref,
    bias_ref,
    cell_ref,
    keep_ref,
    hid0_ref,
    cell0_ref,
    frame_ref,
    keep2_ref,
    proj_ref,
    hid_out,
    cell_out,
    flux_out,
    wide,
    patches,
):
    choices = [chooser(half_ref[i], (128, HID), 1) for i in range(2)]
    hid, cell = first_half(
        1, half_ref[1], patches_ref, other_ref, bias_ref, cell_ref, keep_ref
    )
    cells = (cell0_ref[32:544, :], cell[32:544])
    natural = joined([hid0_ref[...], hid], choices)

    wide[:, 8:40, :] = natural[:576].reshape(18, 32, HID)
    for row in range(18):
        wide[row, 7:8, :] = natural[576 + row : 577 + row]
        wide[row, 40:41, :] = natural[600 + row : 601 + row]
    for b in range(3):
        moved_rows = wide[:, 7 + b : 39 + b, :].astype(BF16)
        for a in range(3):
            t = 3 * a + b
            patches[:, t * HID : (t + 1) * HID] = moved_rows[a : a + 16].reshape(512, HID)
    patches[:, 9 * HID :] = frame_ref[...]

    new_hids, new_cells = [], []
    for i, weight_ref in enumerate((own_ref, other_ref)):
        sums = gate_sums(patches[...], weight_ref)
        new_hid, new_cell = updated(sums, bias_ref[i], cells[i], keep_ref[32:544, :])
        new_hids.append(new_hid)
        new_cells.append(new_cell)
    hid = joined(new_hids, choices).astype(BF16)
    cell = moved(new_cells, choices)
    hid_out[...] = hid
    cell_out[...] = cell
    flux = lax.dot_general(proj_ref[...], hid, NT, preferred_element_type=F32)
    for row in range(16):
        flux_out[row : row + 1, :] = flux[0:1, row * 32 : (row + 1) * 32] * keep2_ref[row : row + 1, :]


def finished(halves, *arrays):
    return pl.pallas_call(
        final_kernel,
        out_shape=(
            jax.ShapeDtypeStruct((512, HID), BF16),
            jax.ShapeDtypeStruct((512, HID), F32),
            jax.ShapeDtypeStruct((16, 32), F32),
        ),
        in_specs=[SMEM] + [VMEM] * len(arrays),
        out_specs=(VMEM, VMEM, VMEM),
        scratch_shapes=[pltpu.VMEM((18, 48, HID), F32), pltpu.VMEM((512, KPAD), BF16)],
        compiler_params=PARAMS,
        cost_estimate=pl.CostEstimate(
            flops=2 * 824 * KPAD * 1024, bytes_accessed=14_000_000, transcendentals=1136 * 1280
        ),
    )(halves, *arrays)


def compute(halves, own, swapped, prep, land_mask, bias2, proj):
    rows, cols = land_mask.shape
    patches1, frame2, cell1, keep1 = prep
    other = swapped(own)
    hid0, cell0 = own_half(halves, patches1, own, bias2, cell1, keep1)
    hidden, cell, flux = finished(
        halves, patches1, own, other, bias2, cell1, keep1,
        hid0, cell0, frame2, land_mask.astype(F32), proj,
    )
    return hidden.reshape(rows, cols, HID), cell.reshape(rows, cols, HID), flux


def bias_of(bias, c):
    by_half = jnp.transpose(bias.reshape(4, 4, 4, 2, 8), (3, 0, 2, 1, 4)).reshape(2, 4, 128)
    return jnp.where(c == 0, by_half, by_half[::-1])


def aux_of(frames, land_mask):
    rows, cols = land_mask.shape
    both = jnp.transpose(frames, (1, 2, 0, 3)).reshape(rows, cols, -1)
    aux = jnp.concatenate([both, land_mask.astype(BF16)[..., None]], axis=-1)
    return jnp.pad(aux, ((0, 0), (0, 0), (0, AUX - aux.shape[2])))


def body(frames, hidden_init, cell_init, conv_weight, bias, land_mask, projection):
    cx = frames.shape[3]
    x, c = lax.axis_index("x"), lax.axis_index("c")
    copies = packed_unit(jnp.stack([c, x]).astype(jnp.int32), conv_weight)
    by_z = lax.all_to_all(copies.reshape(16, 8, CHUNK), "z", 0, 0).reshape(128, CHUNK)

    state = (hidden_init, cell_init, aux_of(frames, land_mask))
    last, first = ends_of(*state)
    low = shifted(last, ("x", "c"), 1)
    high = shifted(first, ("x", "c"), -1)
    last, first = sides_of(*state, low, high)
    left = shifted(last, ("z", "y"), 1)
    right = shifted(first, ("z", "y"), -1)
    halves = jnp.stack([c, 1 - c]).astype(jnp.int32)
    proj = jnp.broadcast_to(projection[None], (16, HID))
    bias2 = bias_of(bias, c)
    by_z, left, right, halves, proj, bias2 = lax.optimization_barrier(
        (by_z, left, right, halves, proj, bias2)
    )

    own = spread(by_z, ("y", "x"))
    prep = prepared(cx, *state, low, high, left, right)
    swapped = lambda piece: turned(piece, "c", 1)
    return compute(halves, own, swapped, prep, land_mask, bias2, proj)


def solution(mesh):
    split = Mesh(mesh.devices.reshape(16, 4, 4, 2), ("z", "y", "x", "c"))
    sx, sy = ("z", "y"), ("x", "c")
    in_specs = (
        P(None, sy, sx, None),
        P(sy, sx, None),
        P(sy, sx, None),
        P(None, None, sx),
        P(),
        P(sy, sx),
        P(),
    )
    out_specs = (P(sy, sx, None), P(sy, sx, None), P(sy, sx))
    return jax.shard_map(body, mesh=split, in_specs=in_specs, out_specs=out_specs, check_vma=False)
```
